128 devices in a mesh: dp: 2 (over core), ctx: 16 (over y, x), head: 4 (over z).
Axes of the slice: x: 4, y: 4, z: 4, core: 2. Of those that a mesh axis runs over, the one named last changes fastest.
Arguments:
- xbc_raw: bfloat16 [2, 8192, 10240], P('dp', ('ctx', 'head')), may hold values from -6 to 6
- gate_raw: bfloat16 [2, 8192, 8192], P('dp', ('ctx', 'head')), may hold values from -6 to 6
- dt_raw: bfloat16 [2, 8192, 128], P('dp', ('ctx', 'head')), may hold values from -3 to 63
- segment_ids: int32 [2, 8192], P('dp', ('ctx', 'head')), may hold values from 0 to 3, never falling along the last dimension, each value on 1 to 4096 neighbouring positions
- conv_weight: float32 [5, 10240], P(None, 'head'), may hold values from -3 to 3
- norm_gain: float32 [8192], P('head'), may hold values from 0.5 to 1.5
- head_params: float32 [3, 128], P(None, 'head'), may hold values from -11 to 1.5
- out_cotangent: bfloat16 [2, 8192, 8192], P('dp', ('ctx', 'head')), may hold values from -6 to 6
Outputs:
- grad_xbc: bfloat16 [2, 8192, 10240], P('dp', ('ctx', 'head'))
- grad_gate: bfloat16 [2, 8192, 8192], P('dp', ('ctx', 'head'))
- grad_dt: bfloat16 [2, 8192, 128], P('dp', ('ctx', 'head'))
- grad_conv: float32 [5, 10240], P(None, 'head')
- grad_gain: float32 [8192], P('head')
- grad_heads: float32 [3, 128], P(None, 'head')
The draws below stay inside these ranges and needn't reach their ends.
Inputs may be any that keep to these rules, and one draw needn't show every extreme that they name: `segment_ids`: segment ids never fall along a sequence; every document holds at most 4096 positions and one holds exactly that many.
All inputs are finite; a program needn't handle non-finite values.
Results may differ from the reference program's by a relative error of at most 0.025.
The reference program's roundings to bfloat16 on the way count: a program that leaves them out, or rounds other values in their place, can miss the bound.
Values may be sent and summed in bfloat16 or wider, within the bound.
A program may use at most 256 MiB of HBM per device.

```python
import math
import jax
import jax.numpy as jnp
import numpy as np
from jax import lax

OWNED_MIXERS = 128
HEAD_DIM = 64
STATE = 128
GROUPS = 8
CONV_W = 4
SHARD_SPAN = 128
DOCS = 4
HP = 8192
CH = 10240
STREAM_COUNT = 2
STREAM_SPAN = 8192


def draw_dt_raw(key, part):
    key = jax.random.fold_in(key, 23)
    jitter_seed, baseline_seed, spike_seed, magnitude_seed = jax.random.split(key, 4)
    article_spans = STREAM_SPAN // SHARD_SPAN
    shape_full = (STREAM_COUNT, article_spans, SHARD_SPAN, OWNED_MIXERS)
    jitter_term = jnp.clip(0.5 * jax.random.normal(jitter_seed, shape_full, jnp.float32), -2.0, 2.0)
    baseline_shift = jax.random.uniform(baseline_seed, (STREAM_COUNT, article_spans, 1, OWNED_MIXERS), jnp.float32, -1.0, 1.0)
    spike_location = jax.random.bernoulli(spike_seed, 4.0 / STREAM_SPAN, (STREAM_COUNT, article_spans, SHARD_SPAN, 1)).astype(jnp.float32)
    spike_magnitude = jax.random.uniform(magnitude_seed, (STREAM_COUNT, article_spans, SHARD_SPAN, 1), jnp.float32, 20.0, 60.0)
    return (jitter_term + baseline_shift + spike_location * spike_magnitude).reshape(STREAM_COUNT, STREAM_SPAN, OWNED_MIXERS).astype(jnp.bfloat16)


def draw_head_params(key, part):
    key = jax.random.fold_in(key, 11)
    rate_key, bias_key, skip_key = jax.random.split(key, 3)
    log_rate = jax.random.uniform(rate_key, (OWNED_MIXERS,), jnp.float32, math.log(2e-05), math.log(0.03))
    dt_shift = jax.random.uniform(bias_key, (OWNED_MIXERS,), jnp.float32, -0.5, 0.5)
    skip_gain = jax.random.uniform(skip_key, (OWNED_MIXERS,), jnp.float32, 0.5, 1.5)
    return jnp.stack([log_rate, dt_shift, skip_gain]).astype(jnp.float32)


def block_scale(own_key, dims, shards, low, largest):
    def one(position, parts):
        draws = jax.random.uniform(jax.random.fold_in(jax.random.fold_in(own_key, 6), position), (parts,), jnp.float32, low / len(shards), largest / len(shards))
        return jnp.repeat(jnp.exp(draws), dims[position] // parts).reshape((-1,) + (1,) * (len(dims) - position - 1))

    level = one(*shards[0])
    for cut in shards[1:]:
        level = level * one(*cut)
    return level


def profile(amount, total, most, lean):
    weights = [(1 << 20) // math.isqrt(standing ** lean) + 1 for standing in range(2, amount + 1)]
    surplus, holding = total - most - (amount - 1), [1] * (amount - 1)
    while surplus > 0:
        free = [i for i in range(amount - 1) if holding[i] < most]
        whole, left = sum([weights[i] for i in free]), surplus
        for i in free:
            addition = min(most - holding[i], max(1, left * weights[i] // whole), surplus)
            holding[i] = holding[i] + addition
            surplus = surplus - addition
    return np.array([most] + holding)


def ragged(own_key, amount, total, most, skew):
    if amount == 2:
        one = jax.random.randint(own_key, (), max(1, total - most), min(most, total - 1) + 1)
        return jnp.stack([one, total - one])
    lengths = jnp.asarray(profile(amount, total, most, skew), jnp.int32)
    twos = (amount - 1) // 2
    donor, taker = lengths[1:1 + 2 * twos:2], lengths[2:2 + 2 * twos:2]
    slack = jnp.minimum(donor - 1, most - taker)
    passed = jax.random.randint(jax.random.fold_in(own_key, 1), (twos,), 0, 1 << 20) % (slack + 1)
    lengths = lengths.at[1:1 + 2 * twos:2].set(donor - passed).at[2:2 + 2 * twos:2].set(taker + passed)
    return lengths[jax.random.permutation(jax.random.fold_in(own_key, 2), amount)]


def bell_draw(own_key, shape, deviation, limit, cuts=(), held_as=jnp.bfloat16):
    level = block_scale(own_key, shape, cuts, -0.22, 0.18) if cuts else 1.0
    drawn = jax.random.normal(own_key, shape, jnp.float32) * deviation * level
    return jnp.minimum(jnp.maximum(drawn, -limit), limit).astype(held_as)


def setup_inputs(seed: int = 0) -> dict:
    key_of = jax.random.split(jax.random.key(seed), 9)
    xbc_raw = bell_draw(key_of[0], (STREAM_COUNT, STREAM_SPAN, CH), 1.0, 6.0, ((0, 2), (1, 64)))
    gate_raw = bell_draw(key_of[1], (STREAM_COUNT, STREAM_SPAN, HP), 1.0, 6.0, ((0, 2), (1, 64)))
    dt_raw = draw_dt_raw(jax.random.fold_in(key_of[8], 71), 0)
    segment_ids = jax.vmap(lambda own: jnp.searchsorted(jnp.cumsum(ragged(own, DOCS, STREAM_SPAN, STREAM_SPAN // 2, 0)), jnp.arange(STREAM_SPAN), side="right"))(jax.random.split(key_of[3], STREAM_COUNT)).reshape((STREAM_COUNT, STREAM_SPAN)).astype(jnp.int32)
    conv_weight = bell_draw(key_of[4], (CONV_W + 1, CH), CONV_W ** -0.5, 3.0, ((1, 4),), jnp.float32)
    norm_gain = jnp.clip(1.0 + 0.1 * jax.random.normal(key_of[5], (HP,), jnp.float32), 0.5, 1.5)
    head_params = draw_head_params(jax.random.fold_in(key_of[8], 71), 0)
    out_cotangent = bell_draw(key_of[7], (STREAM_COUNT, STREAM_SPAN, HP), 1.0, 6.0, ((0, 2), (1, 64)))
    return {"xbc_raw": xbc_raw, "gate_raw": gate_raw, "dt_raw": dt_raw, "segment_ids": segment_ids, "conv_weight": conv_weight, "norm_gain": norm_gain, "head_params": head_params, "out_cotangent": out_cotangent}


highest = lax.Precision.HIGHEST

def conv_block(extended, conv_taps, segment_ext, conv_width):
    row_count = extended.shape[0] - conv_width + 1
    segment_now = segment_ext[conv_width - 1:]
    summed = jnp.broadcast_to(conv_taps[conv_width], (row_count, conv_taps.shape[1]))
    for tap_index in range(conv_width):
        window = extended[tap_index:tap_index + row_count]
        same_doc = (segment_ext[tap_index:tap_index + row_count] == segment_now).astype(extended.dtype)
        summed = summed + conv_taps[tap_index] * window * same_doc[:, None]
    return summed

def split_channels(act_values, group_count):
    row_count = act_values.shape[0]
    grouped = act_values.reshape(row_count, group_count, -1)
    x_width = grouped.shape[2] - 2 * STATE
    per_group = x_width // HEAD_DIM
    x_part = grouped[:, :, :x_width].reshape(row_count, group_count, per_group, HEAD_DIM)
    b_part = grouped[:, :, x_width:x_width + STATE]
    c_part = grouped[:, :, x_width + STATE:]
    return (x_part, b_part, c_part)

def span_step(state_now, inputs):
    x_part, b_part, c_part, step_size, log_decay, seg_span, seg_prev = inputs
    span_len = seg_span.shape[0]
    running = jnp.cumsum(log_decay, axis=0)
    positions = jnp.arange(span_len)
    inside = (seg_span[:, None] == seg_span[None, :]) & (positions[:, None] >= positions[None, :])
    run_moved = jnp.transpose(running, (1, 2, 0))
    gap_values = run_moved[:, :, :, None] - run_moved[:, :, None, :]
    decay_mat = jnp.where(inside, jnp.exp(jnp.where(inside, gap_values, 0.0)), 0.0)
    scores = jnp.einsum('tgn,sgn->gts', c_part, b_part, precision=highest)
    step_moved = jnp.transpose(step_size, (1, 2, 0))
    weights = decay_mat * scores[:, None] * step_moved[:, :, None, :]
    y_part = jnp.einsum('gjts,sgjp->tgjp', weights, x_part, precision=highest)
    linked = (seg_span == seg_prev).astype(running.dtype)
    alive_mask = jnp.exp(running) * linked[:, None, None]
    y_part = y_part + alive_mask[..., None] * jnp.einsum('tgn,gjnp->tgjp', c_part, state_now, precision=highest)
    same_last = (seg_span == seg_span[-1]).astype(running.dtype)
    tail_weight = jnp.exp(running[-1][None] - running) * same_last[:, None, None] * step_size
    keep_all = jnp.exp(running[-1]) * linked[-1]
    new_state = keep_all[..., None, None] * state_now + jnp.einsum('sgn,sgj,sgjp->gjnp', b_part, tail_weight, x_part, precision=highest)
    return (new_state, y_part)

def scanned_spans(x_part, b_part, c_part, step_size, log_decay, seg_values, seg_before):
    row_count = x_part.shape[0]
    span_len = min(128, row_count)
    span_count = row_count // span_len
    prev_all = jnp.concatenate([jnp.reshape(seg_before, (1,)).astype(jnp.int32), seg_values[:-1].astype(jnp.int32)])
    span_prev = prev_all.reshape(span_count, span_len)[:, 0]

    def split_up(values_in):
        return values_in.reshape((span_count, span_len) + values_in.shape[1:])
    start_state = jnp.zeros((x_part.shape[1], x_part.shape[2], STATE, HEAD_DIM), x_part.dtype)
    final_state, outputs = lax.scan(jax.checkpoint(span_step), start_state, (split_up(x_part), split_up(b_part), split_up(c_part), split_up(step_size), split_up(log_decay), split_up(seg_values.astype(jnp.int32)), span_prev))
    return (outputs.reshape(x_part.shape), final_state)

def gate_norm(ssm_values, gate_values, gain_values, group_count):
    gated = ssm_values.astype(jnp.float32) * jax.nn.silu(gate_values.astype(jnp.float32))
    row_count = gated.shape[0]
    grouped = gated.reshape(row_count, group_count, -1)
    mean_sq = lax.optimization_barrier(jnp.mean(grouped * grouped, axis=-1, keepdims=True))
    return (grouped * lax.rsqrt(mean_sq + 1e-05)).reshape(row_count, -1) * gain_values

def reference(xbc_raw, gate_raw, dt_raw, segment_ids, conv_weight, norm_gain, head_params, out_cotangent):
    conv_width = conv_weight.shape[0] - 1
    per_group = OWNED_MIXERS // GROUPS

    def forward(xbc_in, gate_in, dt_in, conv_in, gain_in, heads_in, segment_in):
        row_count = xbc_in.shape[0]
        extended = jnp.concatenate([jnp.zeros((conv_width - 1, xbc_in.shape[1]), jnp.float32), xbc_in.astype(jnp.float32)])
        segment_ext = jnp.concatenate([jnp.full((conv_width - 1,), -1, jnp.int32), segment_in.astype(jnp.int32)])
        activated = jax.nn.silu(conv_block(extended, conv_in, segment_ext, conv_width))
        activated = lax.optimization_barrier(activated.astype(jnp.bfloat16)).astype(jnp.float32)
        x_part, b_part, c_part = split_channels(activated, GROUPS)
        step_size = jax.nn.softplus(dt_in.astype(jnp.float32) + heads_in[1])
        log_decay = -step_size * jnp.exp(heads_in[0])
        shape_three = (row_count, GROUPS, per_group)
        ssm_values, final_state = scanned_spans(x_part, b_part, c_part, step_size.reshape(shape_three), log_decay.reshape(shape_three), segment_in, jnp.full((), -1, jnp.int32))
        ssm_values = ssm_values + heads_in[2].reshape(GROUPS, per_group)[None, :, :, None] * x_part
        rounded = lax.optimization_barrier(ssm_values.reshape(row_count, -1).astype(jnp.bfloat16))
        return gate_norm(rounded, gate_in, gain_in, GROUPS)

    def one_sequence(packed):
        xbc_in, gate_in, dt_in, segment_in, cot_in = packed

        def closed_form(xbc_arg, gate_arg, dt_arg, conv_arg, gain_arg, heads_arg):
            return forward(xbc_arg, gate_arg, dt_arg, conv_arg, gain_arg, heads_arg, segment_in)
        outputs, pullback = jax.vjp(closed_form, xbc_in, gate_in, dt_in, conv_weight, norm_gain, head_params)
        return pullback(cot_in.astype(jnp.float32))
    grads = lax.map(one_sequence, (xbc_raw, gate_raw, dt_raw, segment_ids, out_cotangent))
    grad_xbc, grad_gate, grad_dt, grad_conv, grad_gain, grad_heads = grads
    return (grad_xbc, grad_gate, grad_dt, lax.optimization_barrier(jnp.sum(grad_conv, axis=0)), lax.optimization_barrier(jnp.sum(grad_gain, axis=0)), lax.optimization_barrier(jnp.sum(grad_heads, axis=0)))
```

```python
import jax
import jax.numpy as jnp
from jax import lax
from jax.experimental import pallas as pl
from jax.experimental.pallas import tpu as pltpu
from jax.sharding import PartitionSpec as P

HEADS = 128
GROUPS = 8
T = 128
GW = 1280
XW = 1024
CH = 10240
HP = 8192
LOG2E = 1.4426950408889634
EPS = 1e-05
NEG = -1e30

f32 = jnp.float32
bf16 = jnp.bfloat16
NN = ((1,), (0,))
NT = ((1,), (1,))
TN = ((0,), (0,))


def mm(a, b, dims=NN, precision=None):
    return lax.dot_general(a, b, (dims, ((), ())), preferred_element_type=f32, precision=precision)


def iota(shape, dim):
    return lax.broadcasted_iota(jnp.int32, shape, dim)


def sigmoid(v):
    return 0.5 * jnp.tanh(0.5 * v) + 0.5


def split(v):
    hi = v.astype(bf16)
    return hi, (v - hi.astype(f32)).astype(bf16)


def selector(g):
    return (iota((HEADS, XW), 0) == 16 * g + iota((HEADS, XW), 1) // 64).astype(f32).astype(bf16)


def twice(sel):
    return jnp.concatenate([sel, sel], axis=0)


def head_sums(v, sel):
    hi, lo = split(v)
    return mm(hi, sel, NT) + mm(lo, sel, NT)


def load_ext(ext, xbc_ref, halo_ref):
    ext[8:136, :] = xbc_ref[...].astype(f32)
    ext[5:8, :] = halo_ref[...].astype(f32)


def windows(ext, prep_ref, lanes):
    return [
        ext[5:133, lanes] * prep_ref[6],
        ext[6:134, lanes] * prep_ref[7],
        ext[7:135, lanes] * prep_ref[8],
        ext[8:136, lanes],
    ]


def conv(taps, wc_ref, lanes):
    pre = wc_ref[0, 4:5, lanes] + wc_ref[0, 3:4, lanes] * taps[3]
    for k in range(3):
        pre = pre + wc_ref[0, k : k + 1, lanes] * taps[k]
    return pre


def params(hp_ref, row):
    return jnp.concatenate([hp_ref[q, 5:6, 32 * row : 32 * row + 32] for q in range(4)], axis=1)


def make_prep(hseg_ref, hp_ref, dt_ref, seg_ref, prep_ref, pb_ref, segs):
    rate = jnp.exp(params(hp_ref, 0))
    dtb = dt_ref[...].astype(f32) + params(hp_ref, 1)
    step = jnp.maximum(dtb, 0.0) + jnp.log1p(jnp.exp(-jnp.abs(dtb)))
    decay = -step * rate
    rows, cols = iota((T, T), 0), iota((T, T), 1)
    low = (rows >= cols).astype(f32)
    run = mm(low, decay, NN, lax.Precision.HIGHEST) * LOG2E
    less = run - jnp.log(step) * LOG2E
    seg_row = jnp.broadcast_to(seg_ref[...].astype(f32) + 1.0, (T, T))
    seg_col = seg_row.T
    segs[8:136, :] = seg_col
    segs[5:8, :] = hseg_ref[...].astype(f32)
    prep_ref[0] = run
    prep_ref[1] = less
    prep_ref[2] = run.T
    prep_ref[3] = less.T
    same = seg_col == seg_row
    prep_ref[4] = jnp.where(same & (rows >= cols), 0.0, NEG)
    prep_ref[5] = jnp.where(same & (rows <= cols), 0.0, NEG)
    for k in range(3):
        prep_ref[6 + k] = (segs[5 + k : 133 + k, :] == seg_col).astype(f32)
    prep_ref[9] = step
    prep_ref[10] = decay
    linked = (seg_col == segs[7:8, :]).astype(f32)
    alpha = jnp.exp2(run) * linked
    omega = jnp.exp2(run[T - 1 :] - run) * (seg_col == seg_col[T - 1 :]).astype(f32) * step
    keep = alpha[T - 1 :]
    prep_ref[11] = sigmoid(dtb)
    for i, v in enumerate((alpha, omega)):
        hi, lo = split(v)
        pb_ref[i, :, :T] = hi
        pb_ref[i, :, T:] = lo
    both = jnp.where(rows == 0, params(hp_ref, 2), keep)
    hi, lo = split(both)
    pb_ref[2, :, :T] = hi
    pb_ref[2, :, T:] = lo


def k1(
    xbc_ref, halo_ref, hseg_ref, wc_ref, hp_ref, dt_ref, seg_ref,
    act_ref, pay_ref, prep_ref, pb_ref, ext, segs,
):
    g = pl.program_id(0)

    @pl.when(g == 0)
    def _():
        make_prep(hseg_ref, hp_ref, dt_ref, seg_ref, prep_ref, pb_ref, segs)

    load_ext(ext, xbc_ref, halo_ref)
    for c in range(GW // 128):
        lanes = slice(128 * c, 128 * c + 128)
        pre = conv(windows(ext, prep_ref, lanes), wc_ref, lanes)
        act_ref[:, lanes] = (pre * sigmoid(pre)).astype(bf16)
    sel = selector(g)
    omega = mm(pb_ref[1], twice(sel))
    weighted = (omega * act_ref[:, :XW].astype(f32)).astype(bf16)
    state = mm(act_ref[:, XW : XW + 128], weighted, TN).astype(bf16)
    khi = mm(pb_ref[2, :16, :T], sel)
    klo = mm(pb_ref[2, :16, T:], sel)
    tail = jnp.where(iota((16, XW), 0) == 0, khi[1:2], klo[1:2]).astype(bf16)
    for i in range(8):
        lanes = slice(128 * i, 128 * i + 128)
        pay_ref[i, :128, :] = state[:, lanes]
        pay_ref[i, 128:, :] = tail[:, lanes]


def parts_of(act_ref):
    return act_ref.at[:, :XW], act_ref.at[:, XW : XW + 128], act_ref.at[:, XW + 128 :]


def halves(v):
    left = iota(v.shape, 1) < 64
    zero = jnp.zeros_like(v)
    return jnp.concatenate([jnp.where(left, v, zero), jnp.where(left, zero, v)], axis=0)


def k2a(act_ref, prep_ref, y_ref):
    g = pl.program_id(0)
    x_ref, b_ref, c_ref = parts_of(act_ref)
    scores = mm(c_ref[...], b_ref[...], NT)
    run = pltpu.roll(prep_ref[0], (128 - 16 * g) % 128, 1)
    less = prep_ref[3, pl.ds(pl.multiple_of(16 * g, 16), 16), :]
    bias = prep_ref[4]
    for pair in range(8):
        mats = []
        for j in (2 * pair, 2 * pair + 1):
            el = jnp.exp2(run[:, j : j + 1] - less[j : j + 1, :] + bias)
            mats.append((el * scores).astype(bf16))
        lanes = slice(128 * pair, 128 * pair + 128)
        y_ref[:, lanes] = mm(jnp.concatenate(mats, axis=1), halves(x_ref[:, lanes]))


def scan_up(got_ref, start_ref):
    def one(j, state):
        start_ref[j] = state.astype(bf16)
        tail = got_ref[j, 128:, :].astype(f32)
        keep = tail[0:1] + tail[1:2]
        return keep * state + got_ref[j, :128, :].astype(f32)

    lax.fori_loop(0, 64, one, jnp.zeros((128, 128), f32))


def scan_down(tails_ref, got_ref, end_ref):
    def one(i, grad):
        j = 63 - i
        end_ref[j] = grad.astype(bf16)
        tail = tails_ref[j].astype(f32)
        keep = tail[0:1] + tail[1:2]
        return keep * grad + got_ref[j].astype(f32)

    lax.fori_loop(0, 64, one, jnp.zeros((128, 128), f32))


def wide(slots_ref):
    return jnp.concatenate([slots_ref[i] for i in range(8)], axis=1)


def k2b(
    act_ref, yi_ref, start_ref, gate_ref, cot_ref, gain_ref, pb_ref,
    dy_ref, dgate_ref, pay_ref, dcc_ref, rsum_ref, dgain_ref, dskip_ref,
    alpha_s, cs_s, ady_s, qhi_s, qlo_s,
):
    g = pl.program_id(0)
    x_ref, _, c_ref = parts_of(act_ref)

    @pl.when(g == 0)
    def _():
        rsum_ref[...] = jnp.zeros_like(rsum_ref)
        dskip_ref[...] = jnp.zeros_like(dskip_ref)

    sel = selector(g)
    both = twice(sel)
    start = wide(start_ref)
    cs_s[...] = mm(c_ref[...], start)
    alpha_s[...] = mm(pb_ref[0], both)
    skip = mm(pb_ref[2, :16, :], both)[0:1]
    gain = gain_ref[0, 5:6, :]
    dgain = jnp.zeros((16, XW), f32)
    dskip = jnp.zeros((16, XW), f32)
    for r in range(8):
        rows = slice(16 * r, 16 * r + 16)
        alpha = alpha_s[rows, :]
        yssm = yi_ref[rows, :] + alpha * cs_s[rows, :]
        x = x_ref[rows, :].astype(f32)
        ssm = (yssm + skip * x).astype(bf16).astype(f32)
        gate = gate_ref[rows, :].astype(f32)
        sg = sigmoid(gate)
        sl = gate * sg
        gated = ssm * sl
        rr = lax.rsqrt(jnp.sum(gated * gated, axis=1, keepdims=True) * (1.0 / XW) + EPS)
        norm = gated * rr
        cot = cot_ref[rows, :].astype(f32)
        dgain = dgain + cot * norm
        dn = cot * gain
        m2 = jnp.sum(dn * norm, axis=1, keepdims=True) * (1.0 / XW)
        dgated = rr * (dn - norm * m2)
        dy = (dgated * sl).astype(bf16)
        dy_ref[rows, :] = dy
        dgate_ref[rows, :] = (dgated * ssm * (sg + sl * (1.0 - sg))).astype(bf16)
        dyf = dy.astype(f32)
        ady_s[rows, :] = (alpha * dyf).astype(bf16)
        hi, lo = split(dyf * yssm)
        qhi_s[rows, :] = hi
        qlo_s[rows, :] = lo
        dskip = dskip + dyf * x
    ady = ady_s[...]
    dstart = mm(c_ref[...], ady, TN).astype(bf16)
    for i in range(8):
        pay_ref[i] = dstart[:, 128 * i : 128 * i + 128]
    dcc_ref[0] = mm(ady, start, NT)
    rsum_ref[...] += mm(qhi_s[...], sel, NT) + mm(qlo_s[...], sel, NT)
    dskip_ref[...] += head_sums(dskip, sel)
    dgain_ref[0] = jnp.sum(dgain, axis=0, keepdims=True)


def k3a(act_ref, dy_ref, prep_ref, dcc_ref, dx_ref, db_ref, dc_ref):
    g = pl.program_id(0)
    x_ref, b_ref, c_ref = parts_of(act_ref)
    scores = mm(b_ref[...], c_ref[...], NT)
    less = pltpu.roll(prep_ref[1], (128 - 16 * g) % 128, 1)
    run = prep_ref[2, pl.ds(pl.multiple_of(16 * g, 16), 16), :]
    bias = prep_ref[5]
    dscores = jnp.zeros((T, T), f32)
    for pair in range(8):
        lanes = slice(128 * pair, 128 * pair + 128)
        dy2 = halves(dy_ref[:, lanes])
        dmat = mm(x_ref[:, lanes], dy2, NT)
        mats = []
        for i in range(2):
            j = 2 * pair + i
            el = jnp.exp2(run[j : j + 1, :] - less[:, j : j + 1] + bias)
            mats.append((el * scores).astype(bf16))
            dscores = dscores + el * dmat[:, 128 * i : 128 * i + 128]
        dx_ref[:, lanes] = mm(jnp.concatenate(mats, axis=1), dy2)
    ds = dscores.astype(bf16)
    db_ref[0] = mm(ds, c_ref[...])
    dc_ref[0] = dcc_ref[0] + mm(ds, b_ref[...], TN)


def k3b(
    xbc_ref, halo_ref, wc_ref, hp_ref, act_ref, dy_ref, dxi_ref, dbi_ref, dci_ref,
    start_ref, pay_ref, end_ref, prep_ref, pb_ref, rsum_ref, dskip_ref,
    dxbc_ref, tail_ref, rim_ref, dconv_ref, ddt_ref, dhead_ref,
    ext, dact, csum, ksum,
):
    g = pl.program_id(0)

    @pl.when(g == 0)
    def _():
        csum[...] = jnp.zeros_like(csum)
        ksum[...] = jnp.zeros_like(ksum)

    sel = selector(g)
    both = twice(sel)
    b = act_ref[:, XW : XW + 128]
    end = wide(end_ref)
    rows16 = mm(pb_ref[2, :16, :], both)
    skip, keep = rows16[0:1], rows16[1:2]
    omega = mm(pb_ref[1], both)
    x = act_ref[:, :XW].astype(f32)
    dxs = dxi_ref[...] + omega * mm(b, end)
    csum[...] += head_sums(x * dxs, sel)
    dact[:, :XW] = (dxs + skip * dy_ref[...].astype(f32)).astype(bf16)
    dact[:, XW : XW + 128] = (dbi_ref[0] + mm((omega * x).astype(bf16), end, NT)).astype(bf16)
    dact[:, XW + 128 :] = dci_ref[0].astype(bf16)
    final = keep * wide(start_ref).astype(f32) + wide(pay_ref).astype(f32)
    part = jnp.sum((final * end.astype(f32)).reshape(16, 8, XW), axis=0)
    ksum[...] += head_sums(part, sel)

    load_ext(ext, xbc_ref, halo_ref)
    rows = iota((T, 128), 0)
    for c in range(GW // 128):
        lanes = slice(128 * c, 128 * c + 128)
        taps = windows(ext, prep_ref, lanes)
        pre = conv(taps, wc_ref, lanes)
        sg = sigmoid(pre)
        dpre = dact[:, lanes].astype(f32) * (sg + pre * sg * (1.0 - sg))
        for k in range(4):
            dconv_ref[0, k : k + 1, lanes] = jnp.sum(dpre * taps[k], axis=0, keepdims=True)
        dconv_ref[0, 4:5, lanes] = jnp.sum(dpre, axis=0, keepdims=True)
        total = wc_ref[0, 3:4, lanes] * dpre
        rim = jnp.zeros((8, 128), f32)
        for k in range(3):
            far = 3 - k
            moved = pltpu.roll(wc_ref[0, k : k + 1, lanes] * dpre * prep_ref[6 + k], T - far, 0)
            inside = rows < T - far
            total = total + jnp.where(inside, moved, 0.0)
            rim = rim + jnp.where(inside, 0.0, moved)[T - 8 :]
        dxbc_ref[:, lanes] = total.astype(bf16)
        tail_ref[:, lanes] = total[T - 8 :]
        rim_ref[:, lanes] = rim

    @pl.when(g == GROUPS - 1)
    def _():
        high = (iota((T, T), 0) <= iota((T, T), 1)).astype(f32)
        step, decay = prep_ref[9], prep_ref[10]
        col = csum[...]
        dlog = mm(high, rsum_ref[...] - col, NN, lax.Precision.HIGHEST)
        dlog = dlog + jnp.sum(ksum[...], axis=0, keepdims=True)
        dstep = col / step - dlog * jnp.exp(params(hp_ref, 0))
        ddt = dstep * prep_ref[11]
        ddt_ref[...] = ddt.astype(bf16)
        dhead_ref[0:1, :] = jnp.sum(dlog * decay, axis=0, keepdims=True)
        dhead_ref[1:2, :] = jnp.sum(ddt, axis=0, keepdims=True)
        dhead_ref[2:3, :] = jnp.sum(dskip_ref[...], axis=0, keepdims=True)
        dhead_ref[3:8, :] = jnp.zeros((5, HEADS), f32)


def S(shape, dtype):
    return jax.ShapeDtypeStruct(shape, dtype)


def fixed(shape):
    return pl.BlockSpec(shape, lambda g: (0,) * len(shape))


def lane_block(rows, width):
    return pl.BlockSpec((rows, width), lambda g: (0, g))


def slot_block(*shape):
    return pl.BlockSpec(shape, lambda g: (g,) + (0,) * (len(shape) - 1))


WC_SPEC = pl.BlockSpec((1, 6, GW), lambda g: (g // 2, 0, g % 2))
GAIN_SPEC = pl.BlockSpec((1, 6, XW), lambda g: (g // 2, 0, g % 2))
HP_SPEC = pl.BlockSpec((4, 6, 128), lambda g: (0, 0, 16))


def call(kernel, name, ins, in_specs, outs, out_specs, scratch=(), cost=0, grid=(GROUPS,)):
    return pl.pallas_call(
        kernel,
        grid=grid,
        in_specs=in_specs,
        out_specs=out_specs,
        out_shape=outs,
        scratch_shapes=scratch,
        compiler_params=pltpu.CompilerParams(vmem_limit_bytes=48 << 20),
        cost_estimate=pl.CostEstimate(flops=cost, bytes_accessed=8 << 20, transcendentals=0),
        name=name,
    )(*ins)


def body(
    xbc_raw, gate_raw, dt_raw, segment_ids, conv_weight, norm_gain, head_params, out_cotangent
):
    xbc, gate, dt, cot = xbc_raw[0], gate_raw[0], dt_raw[0], out_cotangent[0]
    along = ("ctx", "head")
    count = lax.axis_size("ctx") * lax.axis_size("head")
    up = [(i, i + 1) for i in range(count - 1)]
    down = [(i + 1, i) for i in range(count - 1)]

    own_w = jnp.concatenate(
        [
            conv_weight,
            jnp.concatenate(
                [norm_gain[None], head_params.reshape(1, 96), jnp.zeros((1, 416), f32)], axis=1
            ),
        ],
        axis=0,
    )
    w_all = lax.all_to_all(
        jnp.broadcast_to(own_w[None], (4, 6, 2560)), "head", split_axis=0, concat_axis=0, tiled=True
    )
    last_ids = jnp.broadcast_to((segment_ids[0, T - 3 :] + 1).astype(bf16)[:, None], (3, 128))
    halo = lax.ppermute(jnp.concatenate([xbc[T - 3 :], last_ids], axis=1), along, up)

    act, pay, prep, pb = call(
        k1,
        "conv_states",
        (xbc, halo, halo, w_all, w_all, dt, segment_ids),
        [
            lane_block(T, GW),
            lane_block(3, GW),
            pl.BlockSpec((3, 128), lambda g: (0, CH // 128)),
            WC_SPEC,
            HP_SPEC,
            fixed((T, HEADS)),
            fixed((1, T)),
        ],
        (S((T, CH), bf16), S((64, 144, 128), bf16), S((12, T, T), f32), S((3, T, 2 * T), bf16)),
        (lane_block(T, GW), slot_block(8, 144, 128), fixed((12, T, T)), fixed((3, T, 2 * T))),
        (pltpu.VMEM((136, GW), f32), pltpu.VMEM((136, 128), f32)),
    )
    got = lax.all_to_all(pay, along, split_axis=0, concat_axis=0, tiled=True)

    yi = call(
        k2a,
        "inner_forward",
        (act, prep),
        [lane_block(T, GW), fixed((12, T, T))],
        S((T, HP), f32),
        lane_block(T, XW),
        cost=4 << 30,
    )
    starts = call(
        scan_up,
        "scan_up",
        (got,),
        [fixed((64, 144, 128))],
        S((64, 128, 128), bf16),
        fixed((64, 128, 128)),
        grid=(1,),
    )
    start = lax.all_to_all(starts, along, split_axis=0, concat_axis=0, tiled=True)

    dy, dgate, pay2, dcc, rsum, dgain, dskip = call(
        k2b,
        "gate_norm",
        (act, yi, start, gate, cot, w_all, pb),
        [
            lane_block(T, GW),
            lane_block(T, XW),
            slot_block(8, 128, 128),
            lane_block(T, XW),
            lane_block(T, XW),
            GAIN_SPEC,
            fixed((3, T, 2 * T)),
        ],
        (
            S((T, HP), bf16),
            S((T, HP), bf16),
            S((64, 128, 128), bf16),
            S((8, T, 128), f32),
            S((T, HEADS), f32),
            S((8, 1, XW), f32),
            S((16, HEADS), f32),
        ),
        (
            lane_block(T, XW),
            lane_block(T, XW),
            slot_block(8, 128, 128),
            slot_block(1, T, 128),
            fixed((T, HEADS)),
            slot_block(1, 1, XW),
            fixed((16, HEADS)),
        ),
        (
            pltpu.VMEM((T, XW), f32),
            pltpu.VMEM((T, XW), f32),
            pltpu.VMEM((T, XW), bf16),
            pltpu.VMEM((T, XW), bf16),
            pltpu.VMEM((T, XW), bf16),
        ),
    )
    got2 = lax.all_to_all(pay2, along, split_axis=0, concat_axis=0, tiled=True)
    dxi, dbi, dci = call(
        k3a,
        "inner_backward",
        (act, dy, prep, dcc),
        [lane_block(T, GW), lane_block(T, XW), fixed((12, T, T)), slot_block(1, T, 128)],
        (S((T, HP), f32), S((8, T, 128), f32), S((8, T, 128), f32)),
        (lane_block(T, XW), slot_block(1, T, 128), slot_block(1, T, 128)),
        cost=4 << 30,
    )
    ends = call(
        scan_down,
        "scan_down",
        (got, got2),
        [pl.BlockSpec((64, 16, 128), lambda g: (0, 8, 0)), fixed((64, 128, 128))],
        S((64, 128, 128), bf16),
        fixed((64, 128, 128)),
        grid=(1,),
    )
    end = lax.all_to_all(ends, along, split_axis=0, concat_axis=0, tiled=True)

    dxbc, tail, rim, dconv, ddt, dhead = call(
        k3b,
        "conv_backward",
        (xbc, halo, w_all, w_all, act, dy, dxi, dbi, dci, start, pay, end, prep, pb, rsum, dskip),
        [
            lane_block(T, GW),
            lane_block(3, GW),
            WC_SPEC,
            HP_SPEC,
            lane_block(T, GW),
            lane_block(T, XW),
            lane_block(T, XW),
            slot_block(1, T, 128),
            slot_block(1, T, 128),
            slot_block(8, 128, 128),
            pl.BlockSpec((8, 128, 128), lambda g: (g, 0, 0)),
            slot_block(8, 128, 128),
            fixed((12, T, T)),
            fixed((3, T, 2 * T)),
            fixed((T, HEADS)),
            fixed((16, HEADS)),
        ],
        (
            S((T, CH), bf16),
            S((8, CH), f32),
            S((8, CH), f32),
            S((4, 5, 2560), f32),
            S((T, HEADS), bf16),
            S((8, HEADS), f32),
        ),
        (
            lane_block(T, GW),
            lane_block(8, GW),
            lane_block(8, GW),
            pl.BlockSpec((1, 5, GW), lambda g: (g // 2, 0, g % 2)),
            fixed((T, HEADS)),
            fixed((8, HEADS)),
        ),
        (
            pltpu.VMEM((136, GW), f32),
            pltpu.VMEM((T, GW), bf16),
            pltpu.VMEM((T, HEADS), f32),
            pltpu.VMEM((8, HEADS), f32),
        ),
    )
    rim_in = lax.ppermute(rim[5:].astype(bf16), along, down)
    last_rows = (tail[5:] + rim_in.astype(f32)).astype(bf16)
    grad_xbc = lax.dynamic_update_slice(dxbc, last_rows, (T - 3, 0))

    heads4 = dhead[:3].reshape(3, 4, 32).transpose(1, 0, 2).reshape(4, 96)
    parts = jnp.concatenate(
        [
            dconv.reshape(4, 5 * 2560),
            dgain.reshape(4, 2048),
            heads4,
            jnp.zeros((4, 16384 - 5 * 2560 - 2048 - 96), f32),
        ],
        axis=1,
    )
    pieces = parts.reshape(4, 2, 16, 512).transpose(1, 2, 0, 3).reshape(128, 4, 128)
    everyone = ("dp", "ctx", "head")
    mine = jnp.sum(
        lax.all_to_all(pieces, everyone, split_axis=0, concat_axis=0, tiled=True), axis=0
    )
    whole = lax.all_to_all(
        jnp.broadcast_to(mine[None], (32, 4, 128)),
        ("dp", "ctx"),
        split_axis=0,
        concat_axis=0,
        tiled=True,
    ).reshape(-1)
    return (
        grad_xbc[None],
        dgate[None],
        ddt[None],
        whole[: 5 * 2560].reshape(5, 2560),
        whole[5 * 2560 : 5 * 2560 + 2048],
        whole[5 * 2560 + 2048 : 5 * 2560 + 2144].reshape(3, 32),
    )


def solution(mesh):
    token = P("dp", ("ctx", "head"), None)
    return jax.shard_map(
        body,
        mesh=mesh,
        in_specs=(
            token, token, token, P("dp", ("ctx", "head")),
            P(None, "head"), P("head"), P(None, "head"), token,
        ),
        out_specs=(token, token, token, P(None, "head"), P("head"), P(None, "head")),
        check_vma=False,
    )
```

```python
import jax
import jax.numpy as jnp
from jax import lax
from jax.experimental import pallas as pl
from jax.experimental.pallas import tpu as pltpu
from jax.sharding import PartitionSpec as P

HEADS = 128
GROUPS = 8
T = 128
GW = 1280
XW = 1024
CH = 10240
HP = 8192
LOG2E = 1.4426950408889634
EPS = 1e-05
NEG = -1e30
SPAN = 120.0
TINY = 1e-30
MESH = pl.DeviceIdType.MESH
VMEM = pltpu.VMEM

f32 = jnp.float32
bf16 = jnp.bfloat16
NN = ((1,), (0,))
NT = ((1,), (1,))
TN = ((0,), (0,))


def mm(a, b, dims=NN, precision=None):
    return lax.dot_general(a, b, (dims, ((), ())), preferred_element_type=f32, precision=precision)


def iota(shape, dim):
    return lax.broadcasted_iota(jnp.int32, shape, dim)


def sigmoid(v):
    return 0.5 * jnp.tanh(0.5 * v) + 0.5


def split(v):
    hi = v.astype(bf16)
    return hi, (v - hi.astype(f32)).astype(bf16)


def selector(g):
    return (iota((HEADS, XW), 0) == 16 * g + iota((HEADS, XW), 1) // 64).astype(f32).astype(bf16)


def twice(sel):
    return jnp.concatenate([sel, sel], axis=0)


def head_sums(v, sel):
    hi, lo = split(v)
    return mm(hi, sel, NT) + mm(lo, sel, NT)


def place():
    return lax.axis_index("ctx") * 4 + lax.axis_index("head")


def at(p):
    return {"ctx": p // 4, "head": lax.rem(p, 4)}


def off(index, width):
    return pl.multiple_of(index * width, width)


def greet(me):
    barrier = pltpu.get_barrier_semaphore()

    def one(k, carry):
        pl.semaphore_signal(
            barrier, inc=1, device_id=at(lax.rem(me + k, 64)), device_id_type=MESH
        )
        return carry

    lax.fori_loop(1, 64, one, 0)
    return barrier


def await_bytes(ref, sem):
    pltpu.make_async_copy(ref, ref, sem).wait()


def send_slot(me, p, src, dst, send_sem, recv_sem):
    @pl.when(p == me)
    def _():
        pltpu.make_async_copy(src, dst, recv_sem).start()

    @pl.when(p != me)
    def _():
        pltpu.make_async_remote_copy(
            src_ref=src, dst_ref=dst, send_sem=send_sem, recv_sem=recv_sem,
            device_id=at(p), device_id_type=MESH,
        ).start()


def turn(me, i):
    return lax.rem(me // 8 + i, 8)


def load_ext(g, ext, xbc_ref, halo):
    ext[8:136, :] = xbc_ref[:, pl.ds(off(g, GW), GW)].astype(f32)
    rows = pl.multiple_of(g * 32, 32)
    for k in range(3):
        for c in range(10):
            ext[5 + k : 6 + k, 128 * c : 128 * c + 128] = halo[pl.ds(rows + 10 * k + c, 1), :]


def windows(ext, prep_ref, lanes):
    return [
        ext[5:133, lanes] * prep_ref[6],
        ext[6:134, lanes] * prep_ref[7],
        ext[7:135, lanes] * prep_ref[8],
        ext[8:136, lanes],
    ]


def taps_of(w_ref, g, c):
    lanes = pl.ds(pl.multiple_of(lax.rem(g, 2) * GW + 128 * c, 128), 128)
    return [w_ref[g // 2, k : k + 1, lanes] for k in range(5)]


def conv(wins, taps):
    pre = taps[4] + taps[3] * wins[3]
    for k in range(3):
        pre = pre + taps[k] * wins[k]
    return pre


def params(w_ref, row):
    first = 2048 + 32 * row
    return jnp.concatenate([w_ref[q, 5:6, first : first + 32] for q in range(4)], axis=1)


def make_prep(halo, w_ref, dt_ref, seg_ref, prep_ref, pb_ref, segs):
    rate = jnp.exp(params(w_ref, 0))
    dtb = dt_ref[...].astype(f32) + params(w_ref, 1)
    step = jnp.maximum(dtb, 0.0) + jnp.log1p(jnp.exp(-jnp.abs(dtb)))
    decay = -step * rate
    rows, cols = iota((T, T), 0), iota((T, T), 1)
    low = (rows >= cols).astype(f32)
    run = mm(low, decay, NN, lax.Precision.HIGHEST) * LOG2E
    less = run - jnp.log(step) * LOG2E
    seg_row = jnp.broadcast_to(seg_ref[...].astype(f32) + 1.0, (T, T))
    seg_col = seg_row.T
    segs[8:136, :] = seg_col
    segs[5:8, :] = halo[256:259, :]
    prep_ref[0] = run
    prep_ref[1] = less
    prep_ref[2] = run.T
    prep_ref[3] = less.T
    same = seg_col == seg_row
    prep_ref[4] = jnp.where(same & (rows >= cols), 0.0, NEG)
    prep_ref[5] = jnp.where(same & (rows <= cols), 0.0, NEG)
    for k in range(3):
        prep_ref[6 + k] = (segs[5 + k : 133 + k, :] == seg_col).astype(f32)
    prep_ref[9] = step
    prep_ref[10] = decay
    linked = (seg_col == segs[7:8, :]).astype(f32)
    alpha = jnp.exp2(run) * linked
    omega = jnp.exp2(run[T - 1 :] - run) * (seg_col == seg_col[T - 1 :]).astype(f32) * step
    keep = alpha[T - 1 :]
    prep_ref[11] = sigmoid(dtb)
    for i, v in enumerate((alpha, omega)):
        hi, lo = split(v)
        pb_ref[i, :, :T] = hi
        pb_ref[i, :, T:] = lo
    both = jnp.where(rows == 0, params(w_ref, 2), keep)
    hi, lo = split(both)
    pb_ref[2, :, :T] = hi
    pb_ref[2, :, T:] = lo


def conv_group(g, xbc_ref, halo, w_ref, prep_ref, pb_ref, act_ref, pay_ref, ext):
    load_ext(g, ext, xbc_ref, halo)
    base = off(g, GW)
    for c in range(GW // 128):
        pre = conv(windows(ext, prep_ref, slice(128 * c, 128 * c + 128)), taps_of(w_ref, g, c))
        act_ref[:, pl.ds(base + 128 * c, 128)] = (pre * sigmoid(pre)).astype(bf16)
    sel = selector(g)
    omega = mm(pb_ref[1], twice(sel))
    x_ref, b_ref, _ = parts_of(act_ref, g)
    weighted = (omega * x_ref[...].astype(f32)).astype(bf16)
    state = mm(b_ref[...], weighted, TN).astype(bf16)
    khi = mm(pb_ref[2, :16, :T], sel)
    klo = mm(pb_ref[2, :16, T:], sel)
    tail = jnp.where(iota((16, XW), 0) == 0, khi[1:2], klo[1:2]).astype(bf16)
    for i in range(8):
        lanes = slice(128 * i, 128 * i + 128)
        pay_ref[8 * g + i, :128, :] = state[:, lanes]
        pay_ref[8 * g + i, 128:, :] = tail[:, lanes]


def parts_of(act_ref, g):
    base = off(g, GW)
    return (
        act_ref.at[:, pl.ds(base, XW)],
        act_ref.at[:, pl.ds(base + XW, 128)],
        act_ref.at[:, pl.ds(base + XW + 128, 128)],
    )


def halves(v):
    left = iota(v.shape, 1) < 64
    zero = jnp.zeros_like(v)
    return jnp.concatenate([jnp.where(left, v, zero), jnp.where(left, zero, v)], axis=0)


def scan_up(got_ref, start_ref):
    def one(j, state):
        top = jnp.maximum(jnp.max(jnp.abs(state), axis=0, keepdims=True) * 1.01, TINY)
        scale = top.astype(bf16).astype(f32)
        start_ref[j, :128, :] = jnp.exp2(state * (SPAN / scale)).astype(bf16)
        start_ref[j, 128:, :] = jnp.broadcast_to(scale, (16, 128)).astype(bf16)
        tail = got_ref[j, 128:, :].astype(f32)
        keep = tail[0:1] + tail[1:2]
        return keep * state + got_ref[j, :128, :].astype(f32)

    lax.fori_loop(0, 64, one, jnp.zeros((128, 128), f32))


def scan_down(tails_ref, got_ref, end_ref):
    def one(i, grad):
        j = 63 - i
        end_ref[j] = grad.astype(bf16)
        tail = tails_ref[j].astype(f32)
        keep = tail[0:1] + tail[1:2]
        return keep * grad + got_ref[j].astype(f32)

    lax.fori_loop(0, 64, one, jnp.zeros((128, 128), f32))


def wide(slots_ref, g):
    return jnp.concatenate([slots_ref[8 * g + i, :128, :] for i in range(8)], axis=1)


def first_kernel(
    xbc_ref, own_ref, dt_ref, seg_ref,
    act_ref, pay_ref, prep_ref, pb_ref, w_ref, halo, start_ref, tails_ref,
    got, rim, ext, segs, near_send, w_sem, halo_sem, send_sem, recv_sem,
):
    me = place()
    h = lax.axis_index("head")
    barrier = greet(me)

    def pack(c, carry):
        last = xbc_ref[112:128, pl.ds(off(c, 128), 128)].astype(f32)
        for k in range(3):
            rim[pl.ds((c // 10) * 32 + 10 * k + lax.rem(c, 10), 1), :] = last[13 + k : 14 + k]
        return carry

    lax.fori_loop(0, 80, pack, 0)
    for i in range(8):
        rim[32 * i + 30 : 32 * i + 32, :] = jnp.zeros((2, 128), f32)
    ids = jnp.broadcast_to(seg_ref[...].astype(f32) + 1.0, (T, T)).T
    rim[256:264, :] = jnp.zeros((8, 128), f32)
    rim[256:259, :] = ids[T - 3 :]
    pl.semaphore_wait(barrier, 63)

    pltpu.make_async_copy(own_ref, w_ref.at[h], w_sem).start()
    for k in range(1, 4):
        pltpu.make_async_remote_copy(
            src_ref=own_ref, dst_ref=w_ref.at[h], send_sem=near_send, recv_sem=w_sem,
            device_id=at(me - h + lax.rem(h + k, 4)), device_id_type=MESH,
        ).start()

    @pl.when(me < 63)
    def _():
        pltpu.make_async_remote_copy(
            src_ref=rim, dst_ref=halo, send_sem=send_sem, recv_sem=halo_sem,
            device_id=at(lax.rem(me + 1, 64)), device_id_type=MESH,
        ).start()

    @pl.when(me == 0)
    def _():
        halo[...] = jnp.zeros_like(halo)

    await_bytes(w_ref, w_sem)
    await_bytes(w_ref.at[pl.ds(0, 3)], near_send)

    @pl.when(me > 0)
    def _():
        await_bytes(halo, halo_sem)

    @pl.when(me < 63)
    def _():
        await_bytes(rim, send_sem)

    make_prep(halo, w_ref, dt_ref, seg_ref, prep_ref, pb_ref, segs)

    def one(i, carry):
        g = turn(me, i)
        conv_group(g, xbc_ref, halo, w_ref, prep_ref, pb_ref, act_ref, pay_ref, ext)
        for s in range(8):
            p = 8 * g + s
            send_slot(me, p, pay_ref.at[p], got.at[me], send_sem, recv_sem)
        return carry

    lax.fori_loop(0, 8, one, 0)
    await_bytes(got, recv_sem)
    scan_up(got, start_ref)
    tails_ref[...] = got[:, 128:, :]
    await_bytes(got.at[pl.ds(0, 63)], send_sem)


def inner_forward(g, act_ref, prep_ref, y_ref):
    x_ref, b_ref, c_ref = parts_of(act_ref, g)
    scores = mm(c_ref[...], b_ref[...], NT)
    run = pltpu.roll(prep_ref[0], lax.rem(128 - 16 * g, 128), 1)
    less = prep_ref[3, pl.ds(off(g, 16), 16), :]
    bias = prep_ref[4]
    for pair in range(8):
        mats = []
        for j in (2 * pair, 2 * pair + 1):
            el = jnp.exp2(run[:, j : j + 1] - less[j : j + 1, :] + bias)
            mats.append((el * scores).astype(bf16))
        lanes = slice(128 * pair, 128 * pair + 128)
        y_ref[:, pl.ds(off(g, XW) + 128 * pair, 128)] = mm(
            jnp.concatenate(mats, axis=1), halves(x_ref[:, lanes])
        )


def decode(code_ref, g):
    codes = wide(code_ref, g).astype(f32)
    scale = jnp.concatenate([code_ref[8 * g + i, 128:, :] for i in range(8)], axis=1)
    return jnp.log2(codes) * (scale[0:1].astype(f32) * (1.0 / SPAN))


def gate_group(
    g, act_ref, yi_ref, code_ref, start_ref, gate_ref, cot_ref, w_ref, pb_ref,
    dy_ref, dgate_ref, pay_ref, dcc_ref, rsum_ref, dgain_ref, dskip_ref,
    alpha_s, cs_s, ady_s, qhi_s, qlo_s,
):
    x_ref, _, c_ref = parts_of(act_ref, g)
    base = pl.ds(off(g, XW), XW)
    yi_ref, gate_ref, cot_ref = yi_ref.at[:, base], gate_ref.at[:, base], cot_ref.at[:, base]
    dy_ref, dgate_ref = dy_ref.at[:, base], dgate_ref.at[:, base]
    sel = selector(g)
    both = twice(sel)
    start, start_lo = split(decode(code_ref, g))
    for i in range(8):
        start_ref[8 * g + i] = start[:, 128 * i : 128 * i + 128]
    cs_s[...] = mm(c_ref[...], start) + mm(c_ref[...], start_lo)
    alpha_s[...] = mm(pb_ref[0], both)
    skip = mm(pb_ref[2, :16, :], both)[0:1]
    gain = w_ref[g // 2, 5:6, pl.ds(off(lax.rem(g, 2), XW), XW)]
    dgain = jnp.zeros((16, XW), f32)
    dskip = jnp.zeros((16, XW), f32)
    for r in range(8):
        rows = slice(16 * r, 16 * r + 16)
        alpha = alpha_s[rows, :]
        yssm = yi_ref[rows, :] + alpha * cs_s[rows, :]
        x = x_ref[rows, :].astype(f32)
        ssm = (yssm + skip * x).astype(bf16).astype(f32)
        gate = gate_ref[rows, :].astype(f32)
        sg = sigmoid(gate)
        sl = gate * sg
        gated = ssm * sl
        rr = lax.rsqrt(jnp.sum(gated * gated, axis=1, keepdims=True) * (1.0 / XW) + EPS)
        norm = gated * rr
        cot = cot_ref[rows, :].astype(f32)
        dgain = dgain + cot * norm
        dn = cot * gain
        m2 = jnp.sum(dn * norm, axis=1, keepdims=True) * (1.0 / XW)
        dgated = rr * (dn - norm * m2)
        dy = (dgated * sl).astype(bf16)
        dy_ref[rows, :] = dy
        dgate_ref[rows, :] = (dgated * ssm * (sg + sl * (1.0 - sg))).astype(bf16)
        dyf = dy.astype(f32)
        ady_s[rows, :] = (alpha * dyf).astype(bf16)
        hi, lo = split(dyf * yssm)
        qhi_s[rows, :] = hi
        qlo_s[rows, :] = lo
        dskip = dskip + dyf * x
    ady = ady_s[...]
    dstart = mm(c_ref[...], ady, TN).astype(bf16)
    for i in range(8):
        pay_ref[8 * g + i] = dstart[:, 128 * i : 128 * i + 128]
    dcc_ref[g] = mm(ady, start, NT) + mm(ady, start_lo, NT)
    rsum_ref[...] += mm(qhi_s[...], sel, NT) + mm(qlo_s[...], sel, NT)
    dskip_ref[...] += head_sums(dskip, sel)
    dgain_ref[g] = jnp.sum(dgain, axis=0, keepdims=True)


def send_back(me, values, landing, send_sem, recv_sems):
    mine = me // 8

    def one(i, carry):
        group = lax.rem(mine + 8 - i, 8)
        for s in range(8):
            p = 8 * group + s
            send_slot(me, p, values.at[p], landing.at[me], send_sem, recv_sems.at[mine])
        return carry

    lax.fori_loop(0, 8, one, 0)


def second_kernel(
    act_ref, start_own, tails_ref, gate_ref, cot_ref, w_ref, prep_ref, pb_ref,
    start_ref, dy_ref, dgate_ref, dcc_ref, rsum_ref, dgain_ref, dskip_ref, end_ref,
    codes, yi_s, pay, got, alpha_s, cs_s, ady_s, qhi_s, qlo_s, back_send, back_recv, send_sem, recv_sem,
):
    me = place()
    barrier = greet(me)
    rsum_ref[...] = jnp.zeros_like(rsum_ref)
    dskip_ref[...] = jnp.zeros_like(dskip_ref)

    def forward(i, carry):
        inner_forward(i, act_ref, prep_ref, yi_s)
        return carry

    lax.fori_loop(0, 8, forward, 0)
    pl.semaphore_wait(barrier, 63)
    send_back(me, start_own, codes, back_send, back_recv)

    def one(i, carry):
        g = turn(me, i)
        await_bytes(codes.at[pl.ds(8 * g, 8)], back_recv.at[g])
        gate_group(
            g, act_ref, yi_s, codes, start_ref, gate_ref, cot_ref, w_ref, pb_ref,
            dy_ref, dgate_ref, pay, dcc_ref, rsum_ref, dgain_ref, dskip_ref,
            alpha_s, cs_s, ady_s, qhi_s, qlo_s,
        )
        for s in range(8):
            p = 8 * g + s
            send_slot(me, p, pay.at[p], got.at[me], send_sem, recv_sem)
        return carry

    lax.fori_loop(0, 8, one, 0)
    await_bytes(got, recv_sem)
    scan_down(tails_ref, got, end_ref)
    await_bytes(got.at[pl.ds(0, 63)], send_sem)
    await_bytes(codes.at[pl.ds(0, 63)], back_send)


def inner_backward(g, act_ref, dy_ref, prep_ref, dcc_ref, dx_ref, db_ref, dc_ref):
    x_ref, b_ref, c_ref = parts_of(act_ref, g)
    scores = mm(b_ref[...], c_ref[...], NT)
    less = pltpu.roll(prep_ref[1], lax.rem(128 - 16 * g, 128), 1)
    run = prep_ref[2, pl.ds(off(g, 16), 16), :]
    bias = prep_ref[5]
    dscores = jnp.zeros((T, T), f32)
    for pair in range(8):
        out_lanes = pl.ds(off(g, XW) + 128 * pair, 128)
        dy2 = halves(dy_ref[:, out_lanes])
        dmat = mm(x_ref[:, 128 * pair : 128 * pair + 128], dy2, NT)
        mats = []
        for i in range(2):
            j = 2 * pair + i
            el = jnp.exp2(run[j : j + 1, :] - less[:, j : j + 1] + bias)
            mats.append((el * scores).astype(bf16))
            dscores = dscores + el * dmat[:, 128 * i : 128 * i + 128]
        dx_ref[:, out_lanes] = mm(jnp.concatenate(mats, axis=1), dy2)
    ds = dscores.astype(bf16)
    db_ref[g] = mm(ds, c_ref[...])
    dc_ref[g] = dcc_ref[g] + mm(ds, b_ref[...], TN)


def back_group(
    g, xbc_ref, halo, w_ref, act_ref, dy_ref, dxi, dbi, dci, start_ref, pay_ref, end,
    prep_ref, pb_ref, dgain_ref, dxbc_ref, tail, rim, part, ext, dact, csum, ksum,
):
    x_ref, b_ref, _ = parts_of(act_ref, g)
    base = pl.ds(off(g, XW), XW)
    sel = selector(g)
    both = twice(sel)
    end_g = wide(end, g)
    rows16 = mm(pb_ref[2, :16, :], both)
    skip, keep = rows16[0:1], rows16[1:2]
    omega = mm(pb_ref[1], both)
    x = x_ref[...].astype(f32)
    dxs = dxi[:, base] + omega * mm(b_ref[...], end_g)
    csum[...] += head_sums(x * dxs, sel)
    dact[:, :XW] = (dxs + skip * dy_ref[:, base].astype(f32)).astype(bf16)
    dact[:, XW : XW + 128] = (dbi[g] + mm((omega * x).astype(bf16), end_g, NT)).astype(bf16)
    dact[:, XW + 128 :] = dci[g].astype(bf16)
    final = keep * wide(start_ref, g).astype(f32) + wide(pay_ref, g).astype(f32)
    ksum[...] += head_sums(jnp.sum((final * end_g.astype(f32)).reshape(16, 8, XW), axis=0), sel)

    load_ext(g, ext, xbc_ref, halo)
    rows = iota((T, 128), 0)
    for c in range(GW // 128):
        lanes = slice(128 * c, 128 * c + 128)
        wide_lanes = pl.ds(off(g, GW) + 128 * c, 128)
        wins = windows(ext, prep_ref, lanes)
        taps = taps_of(w_ref, g, c)
        pre = conv(wins, taps)
        sg = sigmoid(pre)
        dpre = dact[:, lanes].astype(f32) * (sg + pre * sg * (1.0 - sg))
        for k in range(4):
            part[g, c, k : k + 1, :] = jnp.sum(dpre * wins[k], axis=0, keepdims=True)
        part[g, c, 4:5, :] = jnp.sum(dpre, axis=0, keepdims=True)
        if c < 8:
            part[g, c, 5:6, :] = dgain_ref[g, :, lanes]
        else:
            part[g, c, 5:6, :] = jnp.zeros((1, 128), f32)
        part[g, c, 6:8, :] = jnp.zeros((2, 128), f32)
        total = taps[3] * dpre
        over = jnp.zeros((8, 128), f32)
        for k in range(3):
            far = 3 - k
            moved = pltpu.roll(taps[k] * dpre * prep_ref[6 + k], T - far, 0)
            inside = rows < T - far
            total = total + jnp.where(inside, moved, 0.0)
            over = over + jnp.where(inside, 0.0, moved)[T - 8 :]
        dxbc_ref[:, wide_lanes] = total.astype(bf16)
        tail[:, wide_lanes] = total[T - 16 :]
        for k in range(3):
            rim[pl.ds(pl.multiple_of(g * 32, 32) + 10 * k + c, 1), :] = over[5 + k : 6 + k]


def third_kernel(
    xbc_ref, halo, w_ref, act_ref, dy_ref, dcc_ref, start_ref, pay_ref, end_own,
    prep_ref, pb_ref, rsum_ref, dgain_ref, dskip_ref,
    dxbc_ref, ddt_ref, gconv_ref, ggain_ref, gheads_ref,
    dxi, dbi, dci, end, tail, rim, rim_in, part, ext, dact, csum, ksum,
    zbuf, hbuf, own, dhead, rbuf, total, fbuf,
    back_send, back_recv, rim_send, rim_sem, z_send, z_sem, h_send, h_sem,
    r_send, r_sem, f_send, f_sem,
):
    me = place()
    c, h, d = lax.axis_index("ctx"), lax.axis_index("head"), lax.axis_index("dp")
    barrier = greet(me)

    def greet_twin(k, carry):
        pl.semaphore_signal(
            barrier, inc=1, device_id={"dp": 1 - d, "ctx": k, "head": h}, device_id_type=MESH
        )
        return carry

    lax.fori_loop(0, 16, greet_twin, 0)
    csum[...] = jnp.zeros_like(csum)
    ksum[...] = jnp.zeros_like(ksum)
    rim[...] = jnp.zeros_like(rim)

    def inner(i, carry):
        inner_backward(i, act_ref, dy_ref, prep_ref, dcc_ref, dxi, dbi, dci)
        return carry

    lax.fori_loop(0, 8, inner, 0)
    pl.semaphore_wait(barrier, 63 + 16)
    send_back(me, end_own, end, back_send, back_recv)

    def one(i, carry):
        g = turn(me, i)
        await_bytes(end.at[pl.ds(8 * g, 8)], back_recv.at[g])
        back_group(
            g, xbc_ref, halo, w_ref, act_ref, dy_ref, dxi, dbi, dci, start_ref, pay_ref, end,
            prep_ref, pb_ref, dgain_ref, dxbc_ref, tail, rim, part, ext, dact, csum, ksum,
        )
        send_slot(
            me, me - h + g // 2, part.at[g], zbuf.at[h, lax.rem(g, 2)], z_send, z_sem
        )

        @pl.when(me > 0)
        def _():
            rows = pl.ds(pl.multiple_of(g * 32, 32), 32)
            pltpu.make_async_remote_copy(
                src_ref=rim.at[rows], dst_ref=rim_in.at[rows], send_sem=rim_send,
                recv_sem=rim_sem, device_id=at(lax.rem(me + 63, 64)), device_id_type=MESH,
            ).start()

        return carry

    lax.fori_loop(0, 8, one, 0)

    high = (iota((T, T), 0) <= iota((T, T), 1)).astype(f32)
    step, decay = prep_ref[9], prep_ref[10]
    col = csum[...]
    dlog = mm(high, rsum_ref[...] - col, NN, lax.Precision.HIGHEST)
    dlog = dlog + jnp.sum(ksum[...], axis=0, keepdims=True)
    dstep = col / step - dlog * jnp.exp(params(w_ref, 0))
    ddt = dstep * prep_ref[11]
    ddt_ref[...] = ddt.astype(bf16)
    dhead[0:1, :] = jnp.sum(dlog * decay, axis=0, keepdims=True)
    dhead[1:2, :] = jnp.sum(ddt, axis=0, keepdims=True)
    dhead[2:3, :] = jnp.sum(dskip_ref[...], axis=0, keepdims=True)
    dhead[3:8, :] = jnp.zeros((5, HEADS), f32)
    pltpu.make_async_copy(dhead, hbuf.at[h], h_sem).start()
    for k in range(1, 4):
        pltpu.make_async_remote_copy(
            src_ref=dhead, dst_ref=hbuf.at[h], send_sem=h_send, recv_sem=h_sem,
            device_id=at(me - h + lax.rem(h + k, 4)), device_id_type=MESH,
        ).start()

    await_bytes(zbuf, z_sem)
    for q in range(2):
        own[10 * q : 10 * q + 10] = zbuf[0, q] + zbuf[1, q] + zbuf[2, q] + zbuf[3, q]
    await_bytes(hbuf, h_sem)
    own[20] = hbuf[0] + hbuf[1] + hbuf[2] + hbuf[3]
    rank = d * 16 + c

    def to_rank(r, src, dst, send_sem, recv_sem):
        @pl.when(r == rank)
        def _():
            pltpu.make_async_copy(src, dst, recv_sem).start()

        @pl.when(r != rank)
        def _():
            pltpu.make_async_remote_copy(
                src_ref=src, dst_ref=dst, send_sem=send_sem, recv_sem=recv_sem,
                device_id={"dp": r // 16, "ctx": lax.rem(r, 16), "head": h},
                device_id_type=MESH,
            ).start()

    def spread(r, carry):
        to_rank(r, own.at[r], rbuf.at[rank], r_send, r_sem)
        return carry

    lax.fori_loop(0, 21, spread, 0)

    @pl.when(rank < 21)
    def _():
        await_bytes(rbuf, r_sem)
        total[...] = jnp.sum(rbuf[...], axis=0)

        def share(k, carry):
            to_rank(lax.rem(rank + k, 32), total, fbuf.at[rank], f_send, f_sem)
            return carry

        lax.fori_loop(0, 32, share, 0)

    @pl.when(me < 63)
    def _():
        await_bytes(rim_in, rim_sem)

        def fix(t, carry):
            lanes = pl.ds(off(t, 128), 128)
            for k in range(3):
                row = rim_in[pl.ds((t // 10) * 32 + 10 * k + lax.rem(t, 10), 1), :]
                tail[13 + k : 14 + k, lanes] += row
            dxbc_ref[112:128, lanes] = tail[:, lanes].astype(bf16)
            return carry

        lax.fori_loop(0, 80, fix, 0)

    await_bytes(fbuf, f_sem)
    for q in range(2):
        for t in range(10):
            lanes = slice(GW * q + 128 * t, GW * q + 128 * t + 128)
            gconv_ref[:, lanes] = fbuf[10 * q + t, :5, :]
            if t < 8:
                lanes = slice(XW * q + 128 * t, XW * q + 128 * t + 128)
                ggain_ref[:, lanes] = fbuf[10 * q + t, 5:6, :]
    gheads_ref[...] = pltpu.roll(fbuf[20], lax.rem(128 - 32 * h, 128), 1)[:3, :32]

    await_bytes(end.at[pl.ds(0, 63)], back_send)
    await_bytes(hbuf.at[pl.ds(0, 3)], h_send)
    await_bytes(part.at[pl.ds(0, 6)], z_send)

    @pl.when(me > 0)
    def _():
        await_bytes(rim, rim_send)

    @pl.when(rank < 21)
    def _():
        await_bytes(rbuf.at[pl.ds(0, 20)], r_send)
        await_bytes(rbuf.at[pl.ds(0, 31)], f_send)

    @pl.when(rank >= 21)
    def _():
        await_bytes(rbuf.at[pl.ds(0, 21)], r_send)


def S(shape, dtype):
    return jax.ShapeDtypeStruct(shape, dtype)


def call(kernel, name, ins, outs, scratch, cid):
    spec = pl.BlockSpec(memory_space=VMEM)
    return pl.pallas_call(
        kernel,
        in_specs=[spec] * len(ins),
        out_specs=[spec] * len(outs),
        out_shape=outs,
        scratch_shapes=scratch,
        compiler_params=pltpu.CompilerParams(
            vmem_limit_bytes=56 << 20, collective_id=cid, has_side_effects=True
        ),
        cost_estimate=pl.CostEstimate(flops=4 << 30, bytes_accessed=16 << 20, transcendentals=0),
        name=name,
    )(*ins)


def body(
    xbc_raw, gate_raw, dt_raw, segment_ids, conv_weight, norm_gain, head_params, out_cotangent
):
    xbc, gate, dt, cot = xbc_raw[0], gate_raw[0], dt_raw[0], out_cotangent[0]
    own_w = jnp.concatenate(
        [
            conv_weight,
            jnp.concatenate(
                [norm_gain[None], head_params.reshape(1, 96), jnp.zeros((1, 416), f32)], axis=1
            ),
        ],
        axis=0,
    )
    dma = pltpu.SemaphoreType.DMA
    act, pay, prep, pb, w_all, halo, starts, tails = call(
        first_kernel,
        "conv_states",
        (xbc, own_w, dt, segment_ids),
        (
            S((T, CH), bf16),
            S((64, 144, 128), bf16),
            S((12, T, T), f32),
            S((3, T, 2 * T), bf16),
            S((4, 6, 2560), f32),
            S((264, 128), f32),
            S((64, 144, 128), bf16),
            S((64, 16, 128), bf16),
        ),
        (
            VMEM((64, 144, 128), bf16),
            VMEM((264, 128), f32),
            VMEM((136, GW), f32),
            VMEM((136, 128), f32),
            dma, dma, dma, dma, dma,
        ),
        1,
    )
    start, dy, dgate, dcc, rsum, dgain, dskip, ends = call(
        second_kernel,
        "gate_norm",
        (act, starts, tails, gate, cot, w_all, prep, pb),
        (
            S((64, 128, 128), bf16),
            S((T, HP), bf16),
            S((T, HP), bf16),
            S((8, T, 128), f32),
            S((T, HEADS), f32),
            S((8, 1, XW), f32),
            S((16, HEADS), f32),
            S((64, 128, 128), bf16),
        ),
        (
            VMEM((64, 144, 128), bf16),
            VMEM((T, HP), f32),
            VMEM((64, 128, 128), bf16),
            VMEM((64, 128, 128), bf16),
            VMEM((T, XW), f32),
            VMEM((T, XW), f32),
            VMEM((T, XW), bf16),
            VMEM((T, XW), bf16),
            VMEM((T, XW), bf16),
            dma, dma((8,)), dma, dma,
        ),
        2,
    )
    dxbc, ddt, gconv, ggain, gheads = call(
        third_kernel,
        "conv_backward",
        (xbc, halo, w_all, act, dy, dcc, start, pay, ends, prep, pb, rsum, dgain, dskip),
        (
            S((T, CH), bf16),
            S((T, HEADS), bf16),
            S((5, 2560), f32),
            S((1, 2048), f32),
            S((3, 32), f32),
        ),
        (
            VMEM((T, HP), f32),
            VMEM((8, T, 128), f32),
            VMEM((8, T, 128), f32),
            VMEM((64, 128, 128), bf16),
            VMEM((16, CH), f32),
            VMEM((256, 128), f32),
            VMEM((256, 128), f32),
            VMEM((8, 10, 8, 128), f32),
            VMEM((136, GW), f32),
            VMEM((T, GW), bf16),
            VMEM((T, HEADS), f32),
            VMEM((8, HEADS), f32),
            VMEM((4, 2, 10, 8, 128), f32),
            VMEM((4, 8, 128), f32),
            VMEM((21, 8, 128), f32),
            VMEM((8, 128), f32),
            VMEM((32, 8, 128), f32),
            VMEM((8, 128), f32),
            VMEM((21, 8, 128), f32),
            dma, dma((8,)), dma, dma, dma, dma, dma, dma, dma, dma, dma, dma,
        ),
        3,
    )
    return (dxbc[None], dgate[None], ddt[None], gconv, ggain[0], gheads)


def solution(mesh):
    token = P("dp", ("ctx", "head"), None)
    return jax.shard_map(
        body,
        mesh=mesh,
        in_specs=(
            token, token, token, P("dp", ("ctx", "head")),
            P(None, "head"), P("head"), P(None, "head"), token,
        ),
        out_specs=(token, token, token, P(None, "head"), P("head"), P(None, "head")),
        check_vma=False,
    )
```

```python
import jax
import jax.numpy as jnp
from jax import lax
from jax.experimental import pallas as pl
from jax.experimental.pallas import tpu as pltpu
from jax.sharding import PartitionSpec as P

HEADS = 128
GROUPS = 8
T = 128
GW = 1280
XW = 1024
CH = 10240
HP = 8192
LOG2E = 1.4426950408889634
EPS = 1e-05
NEG = -1e30
SPAN = 120.0
TINY = 1e-30
MESH = pl.DeviceIdType.MESH
VMEM = pltpu.VMEM

f32 = jnp.float32
bf16 = jnp.bfloat16
NN = ((1,), (0,))
NT = ((1,), (1,))
TN = ((0,), (0,))


def mm(a, b, dims=NN, precision=None):
    return lax.dot_general(a, b, (dims, ((), ())), preferred_element_type=f32, precision=precision)


def iota(shape, dim):
    return lax.broadcasted_iota(jnp.int32, shape, dim)


def sigmoid(v):
    return 0.5 * jnp.tanh(0.5 * v) + 0.5


def split(v):
    hi = v.astype(bf16)
    return hi, (v - hi.astype(f32)).astype(bf16)


def selector(g):
    return (iota((HEADS, XW), 0) == 16 * g + iota((HEADS, XW), 1) // 64).astype(f32).astype(bf16)


def twice(sel):
    return jnp.concatenate([sel, sel], axis=0)


def head_sums(v, sel):
    hi, lo = split(v)
    return mm(hi, sel, NT) + mm(lo, sel, NT)


def place():
    return lax.axis_index("ctx") * 4 + lax.axis_index("head")


def at(p):
    return {"ctx": p // 4, "head": lax.rem(p, 4)}


def off(index, width):
    return pl.multiple_of(index * width, width)


def greet(me):
    barrier = pltpu.get_barrier_semaphore()

    def one(k, carry):
        pl.semaphore_signal(
            barrier, inc=1, device_id=at(lax.rem(me + k, 64)), device_id_type=MESH
        )
        return carry

    lax.fori_loop(1, 64, one, 0)
    return barrier


def await_bytes(ref, sem):
    pltpu.make_async_copy(ref, ref, sem).wait()


def send_slot(me, p, src, dst, send_sem, recv_sem):
    @pl.when(p == me)
    def _():
        pltpu.make_async_copy(src, dst, recv_sem).start()

    @pl.when(p != me)
    def _():
        pltpu.make_async_remote_copy(
            src_ref=src, dst_ref=dst, send_sem=send_sem, recv_sem=recv_sem,
            device_id=at(p), device_id_type=MESH,
        ).start()


def turn(me, i):
    return lax.rem(me // 8 + i, 8)


def load_ext(g, ext, xbc_ref, halo):
    ext[8:136, :] = xbc_ref[:, pl.ds(off(g, GW), GW)].astype(f32)
    rows = pl.multiple_of(g * 32, 32)
    for k in range(3):
        for c in range(10):
            ext[5 + k : 6 + k, 128 * c : 128 * c + 128] = halo[pl.ds(rows + 10 * k + c, 1), :]


def windows(ext, prep_ref, lanes):
    return [
        ext[5:133, lanes] * prep_ref[6],
        ext[6:134, lanes] * prep_ref[7],
        ext[7:135, lanes] * prep_ref[8],
        ext[8:136, lanes],
    ]


def taps_of(w_ref, g, c):
    lanes = pl.ds(pl.multiple_of(lax.rem(g, 2) * GW + 128 * c, 128), 128)
    return [w_ref[g // 2, k : k + 1, lanes] for k in range(5)]


def conv(wins, taps):
    pre = taps[4] + taps[3] * wins[3]
    for k in range(3):
        pre = pre + taps[k] * wins[k]
    return pre


def params(w_ref, row):
    first = 2048 + 32 * row
    return jnp.concatenate([w_ref[q, 5:6, first : first + 32] for q in range(4)], axis=1)


def make_prep(halo, w_ref, dt_ref, seg_ref, prep_ref, pb_ref, segs):
    rate = jnp.exp(params(w_ref, 0))
    dtb = dt_ref[...].astype(f32) + params(w_ref, 1)
    step = jnp.maximum(dtb, 0.0) + jnp.log1p(jnp.exp(-jnp.abs(dtb)))
    decay = -step * rate
    rows, cols = iota((T, T), 0), iota((T, T), 1)
    low = (rows >= cols).astype(f32)
    run = mm(low, decay, NN, lax.Precision.HIGHEST) * LOG2E
    less = run - jnp.log(step) * LOG2E
    seg_row = jnp.broadcast_to(seg_ref[...].astype(f32) + 1.0, (T, T))
    seg_col = seg_row.T
    segs[8:136, :] = seg_col
    segs[5:8, :] = halo[256:259, :]
    prep_ref[0] = run
    prep_ref[1] = less
    prep_ref[2] = run.T
    prep_ref[3] = less.T
    same = seg_col == seg_row
    prep_ref[4] = jnp.where(same & (rows >= cols), 0.0, NEG)
    prep_ref[5] = jnp.where(same & (rows <= cols), 0.0, NEG)
    for k in range(3):
        prep_ref[6 + k] = (segs[5 + k : 133 + k, :] == seg_col).astype(f32)
    prep_ref[9] = step
    prep_ref[10] = decay
    linked = (seg_col == segs[7:8, :]).astype(f32)
    alpha = jnp.exp2(run) * linked
    omega = jnp.exp2(run[T - 1 :] - run) * (seg_col == seg_col[T - 1 :]).astype(f32) * step
    keep = alpha[T - 1 :]
    prep_ref[11] = sigmoid(dtb)
    for i, v in enumerate((alpha, omega)):
        hi, lo = split(v)
        pb_ref[i, :, :T] = hi
        pb_ref[i, :, T:] = lo
    both = jnp.where(rows == 0, params(w_ref, 2), keep)
    hi, lo = split(both)
    pb_ref[2, :, :T] = hi
    pb_ref[2, :, T:] = lo


def conv_group(g, xbc_ref, halo, w_ref, prep_ref, pb_ref, act_ref, pay_ref, ext):
    load_ext(g, ext, xbc_ref, halo)
    base = off(g, GW)
    for c in range(GW // 128):
        pre = conv(windows(ext, prep_ref, slice(128 * c, 128 * c + 128)), taps_of(w_ref, g, c))
        act_ref[:, pl.ds(base + 128 * c, 128)] = (pre * sigmoid(pre)).astype(bf16)
    sel = selector(g)
    omega = mm(pb_ref[1], twice(sel))
    x_ref, b_ref, _ = parts_of(act_ref, g)
    weighted = (omega * x_ref[...].astype(f32)).astype(bf16)
    state = mm(b_ref[...], weighted, TN).astype(bf16)
    khi = mm(pb_ref[2, :16, :T], sel)
    klo = mm(pb_ref[2, :16, T:], sel)
    tail = jnp.where(iota((16, XW), 0) == 0, khi[1:2], klo[1:2]).astype(bf16)
    for i in range(8):
        lanes = slice(128 * i, 128 * i + 128)
        pay_ref[8 * g + i, :128, :] = state[:, lanes]
        pay_ref[8 * g + i, 128:, :] = tail[:, lanes]


def parts_of(act_ref, g):
    base = off(g, GW)
    return (
        act_ref.at[:, pl.ds(base, XW)],
        act_ref.at[:, pl.ds(base + XW, 128)],
        act_ref.at[:, pl.ds(base + XW + 128, 128)],
    )


def halves(v):
    left = iota(v.shape, 1) < 64
    zero = jnp.zeros_like(v)
    return jnp.concatenate([jnp.where(left, v, zero), jnp.where(left, zero, v)], axis=0)


def scan_up(got_ref, start_ref):
    def one(j, state):
        top = jnp.maximum(jnp.max(jnp.abs(state), axis=0, keepdims=True) * 1.01, TINY)
        scale = top.astype(bf16).astype(f32)
        start_ref[j, :128, :] = jnp.exp2(state * (SPAN / scale)).astype(bf16)
        start_ref[j, 128:, :] = jnp.broadcast_to(scale, (16, 128)).astype(bf16)
        tail = got_ref[j, 128:, :].astype(f32)
        keep = tail[0:1] + tail[1:2]
        return keep * state + got_ref[j, :128, :].astype(f32)

    lax.fori_loop(0, 64, one, jnp.zeros((128, 128), f32))


def scan_down(got_up, got_ref, end_ref):
    def one(i, grad):
        j = 63 - i
        end_ref[j] = grad.astype(bf16)
        tail = got_up[j, 128:, :].astype(f32)
        keep = tail[0:1] + tail[1:2]
        return keep * grad + got_ref[j].astype(f32)

    lax.fori_loop(0, 64, one, jnp.zeros((128, 128), f32))


def wide(slots_ref, g):
    return jnp.concatenate([slots_ref[8 * g + i, :128, :] for i in range(8)], axis=1)


def inner_forward(g, act_ref, prep_ref, y_ref):
    x_ref, b_ref, c_ref = parts_of(act_ref, g)
    scores = mm(c_ref[...], b_ref[...], NT)
    run = pltpu.roll(prep_ref[0], lax.rem(128 - 16 * g, 128), 1)
    less = prep_ref[3, pl.ds(off(g, 16), 16), :]
    bias = prep_ref[4]
    for pair in range(8):
        mats = []
        for j in (2 * pair, 2 * pair + 1):
            el = jnp.exp2(run[:, j : j + 1] - less[j : j + 1, :] + bias)
            mats.append((el * scores).astype(bf16))
        lanes = slice(128 * pair, 128 * pair + 128)
        y_ref[:, pl.ds(off(g, XW) + 128 * pair, 128)] = mm(
            jnp.concatenate(mats, axis=1), halves(x_ref[:, lanes])
        )


def decode(code_ref, g):
    codes = wide(code_ref, g).astype(f32)
    scale = jnp.concatenate([code_ref[8 * g + i, 128:, :] for i in range(8)], axis=1)
    return jnp.log2(codes) * (scale[0:1].astype(f32) * (1.0 / SPAN))


def gate_group(
    g, act_ref, yi_ref, code_ref, start_ref, gate_ref, cot_ref, w_ref, pb_ref,
    dy_ref, dgate_ref, pay_ref, dcc_ref, rsum_ref, dgain_ref, dskip_ref,
    alpha_s, cs_s, ady_s, qhi_s, qlo_s,
):
    x_ref, _, c_ref = parts_of(act_ref, g)
    base = pl.ds(off(g, XW), XW)
    yi_ref, gate_ref, cot_ref = yi_ref.at[:, base], gate_ref.at[:, base], cot_ref.at[:, base]
    dy_ref, dgate_ref = dy_ref.at[:, base], dgate_ref.at[:, base]
    sel = selector(g)
    both = twice(sel)
    start, start_lo = split(decode(code_ref, g))
    for i in range(8):
        start_ref[8 * g + i] = start[:, 128 * i : 128 * i + 128]
    cs_s[...] = mm(c_ref[...], start) + mm(c_ref[...], start_lo)
    alpha_s[...] = mm(pb_ref[0], both)
    skip = mm(pb_ref[2, :16, :], both)[0:1]
    gain = w_ref[g // 2, 5:6, pl.ds(off(lax.rem(g, 2), XW), XW)]
    dgain = jnp.zeros((16, XW), f32)
    dskip = jnp.zeros((16, XW), f32)
    for r in range(8):
        rows = slice(16 * r, 16 * r + 16)
        alpha = alpha_s[rows, :]
        yssm = yi_ref[rows, :] + alpha * cs_s[rows, :]
        x = x_ref[rows, :].astype(f32)
        ssm = (yssm + skip * x).astype(bf16).astype(f32)
        gate = gate_ref[rows, :].astype(f32)
        sg = sigmoid(gate)
        sl = gate * sg
        gated = ssm * sl
        rr = lax.rsqrt(jnp.sum(gated * gated, axis=1, keepdims=True) * (1.0 / XW) + EPS)
        norm = gated * rr
        cot = cot_ref[rows, :].astype(f32)
        dgain = dgain + cot * norm
        dn = cot * gain
        m2 = jnp.sum(dn * norm, axis=1, keepdims=True) * (1.0 / XW)
        dgated = rr * (dn - norm * m2)
        dy = (dgated * sl).astype(bf16)
        dy_ref[rows, :] = dy
        dgate_ref[rows, :] = (dgated * ssm * (sg + sl * (1.0 - sg))).astype(bf16)
        dyf = dy.astype(f32)
        ady_s[rows, :] = (alpha * dyf).astype(bf16)
        hi, lo = split(dyf * yssm)
        qhi_s[rows, :] = hi
        qlo_s[rows, :] = lo
        dskip = dskip + dyf * x
    ady = ady_s[...]
    dstart = mm(c_ref[...], ady, TN).astype(bf16)
    for i in range(8):
        pay_ref[8 * g + i] = dstart[:, 128 * i : 128 * i + 128]
    dcc_ref[g] = mm(ady, start, NT) + mm(ady, start_lo, NT)
    rsum_ref[...] += mm(qhi_s[...], sel, NT) + mm(qlo_s[...], sel, NT)
    dskip_ref[...] += head_sums(dskip, sel)
    dgain_ref[g] = jnp.sum(dgain, axis=0, keepdims=True)


def send_back(me, values, landing, send_sem, recv_sems):
    mine = me // 8

    def one(i, carry):
        group = lax.rem(mine + 8 - i, 8)
        for s in range(8):
            p = 8 * group + s
            send_slot(me, p, values.at[p], landing.at[me], send_sem, recv_sems.at[mine])
        return carry

    lax.fori_loop(0, 8, one, 0)


def inner_backward(g, act_ref, dy_ref, prep_ref, dcc_ref, dx_ref, db_ref, dc_ref):
    x_ref, b_ref, c_ref = parts_of(act_ref, g)
    scores = mm(b_ref[...], c_ref[...], NT)
    less = pltpu.roll(prep_ref[1], lax.rem(128 - 16 * g, 128), 1)
    run = prep_ref[2, pl.ds(off(g, 16), 16), :]
    bias = prep_ref[5]
    dscores = jnp.zeros((T, T), f32)
    for pair in range(8):
        out_lanes = pl.ds(off(g, XW) + 128 * pair, 128)
        dy2 = halves(dy_ref[:, out_lanes])
        dmat = mm(x_ref[:, 128 * pair : 128 * pair + 128], dy2, NT)
        mats = []
        for i in range(2):
            j = 2 * pair + i
            el = jnp.exp2(run[j : j + 1, :] - less[:, j : j + 1] + bias)
            mats.append((el * scores).astype(bf16))
            dscores = dscores + el * dmat[:, 128 * i : 128 * i + 128]
        dx_ref[:, out_lanes] = mm(jnp.concatenate(mats, axis=1), dy2)
    ds = dscores.astype(bf16)
    db_ref[g] = mm(ds, c_ref[...])
    dc_ref[g] = dcc_ref[g] + mm(ds, b_ref[...], TN)


def back_group(
    g, xbc_ref, halo, w_ref, act_ref, dy_ref, dxi, dbi, dci, start_ref, pay_ref, end,
    prep_ref, pb_ref, dgain_ref, dxbc_ref, tail, rim, part, ext, dact, csum, ksum,
):
    x_ref, b_ref, _ = parts_of(act_ref, g)
    base = pl.ds(off(g, XW), XW)
    sel = selector(g)
    both = twice(sel)
    end_g = wide(end, g)
    rows16 = mm(pb_ref[2, :16, :], both)
    skip, keep = rows16[0:1], rows16[1:2]
    omega = mm(pb_ref[1], both)
    x = x_ref[...].astype(f32)
    dxs = dxi[:, base] + omega * mm(b_ref[...], end_g)
    csum[...] += head_sums(x * dxs, sel)
    dact[:, :XW] = (dxs + skip * dy_ref[:, base].astype(f32)).astype(bf16)
    dact[:, XW : XW + 128] = (dbi[g] + mm((omega * x).astype(bf16), end_g, NT)).astype(bf16)
    dact[:, XW + 128 :] = dci[g].astype(bf16)
    final = keep * wide(start_ref, g).astype(f32) + wide(pay_ref, g).astype(f32)
    ksum[...] += head_sums(jnp.sum((final * end_g.astype(f32)).reshape(16, 8, XW), axis=0), sel)

    load_ext(g, ext, xbc_ref, halo)
    rows = iota((T, 128), 0)
    for c in range(GW // 128):
        lanes = slice(128 * c, 128 * c + 128)
        wide_lanes = pl.ds(off(g, GW) + 128 * c, 128)
        wins = windows(ext, prep_ref, lanes)
        taps = taps_of(w_ref, g, c)
        pre = conv(wins, taps)
        sg = sigmoid(pre)
        dpre = dact[:, lanes].astype(f32) * (sg + pre * sg * (1.0 - sg))
        for k in range(4):
            part[g, c, k : k + 1, :] = jnp.sum(dpre * wins[k], axis=0, keepdims=True)
        part[g, c, 4:5, :] = jnp.sum(dpre, axis=0, keepdims=True)
        if c < 8:
            part[g, c, 5:6, :] = dgain_ref[g, :, lanes]
        else:
            part[g, c, 5:6, :] = jnp.zeros((1, 128), f32)
        part[g, c, 6:8, :] = jnp.zeros((2, 128), f32)
        total = taps[3] * dpre
        over = jnp.zeros((8, 128), f32)
        for k in range(3):
            far = 3 - k
            moved = pltpu.roll(taps[k] * dpre * prep_ref[6 + k], T - far, 0)
            inside = rows < T - far
            total = total + jnp.where(inside, moved, 0.0)
            over = over + jnp.where(inside, 0.0, moved)[T - 8 :]
        dxbc_ref[:, wide_lanes] = total.astype(bf16)
        tail[:, wide_lanes] = total[T - 16 :]
        for k in range(3):
            rim[pl.ds(pl.multiple_of(g * 32, 32) + 10 * k + c, 1), :] = over[5 + k : 6 + k]


def mixer(
    xbc_ref, own_ref, dt_ref, seg_ref, gate_hbm, cot_hbm,
    dxbc_ref, dgate_hbm, ddt_ref, gconv_ref, ggain_ref, gheads_ref,
    gate_v, cot_v, dgate_v, act_ref, pay_ref, prep_ref, pb_ref, w_ref, near, halo, got,
    start_own, codes, start_ref, yi_s, dy_ref, pay2, got2, dcc_ref, dbi, rsum_ref,
    dgain_ref, dskip_ref, end_own, end, tail, rim, rim_in, part, ext, segs, dact, csum,
    ksum, zbuf, hbuf, own, dhead, rbuf, total, fbuf, alpha_s, cs_s, ady_s, qhi_s, qlo_s,
    gate_sem, cot_sem, near_send, w_sem, near_sem, halo_sem, send_sem, recv_sem, start_send,
    grad_send, grad_recv, back_send, rim_send, rim_sem, z_send, z_sem, h_send, h_sem,
    r_send, r_sem, f_send, f_sem, start_recv, back_recv,
):
    me = place()
    c, h, d = lax.axis_index("ctx"), lax.axis_index("head"), lax.axis_index("dp")
    barrier = greet(me)

    def greet_twin(k, carry):
        pl.semaphore_signal(
            barrier, inc=1, device_id={"dp": 1 - d, "ctx": k, "head": h}, device_id_type=MESH
        )
        return carry

    lax.fori_loop(0, 16, greet_twin, 0)
    gate_in = pltpu.make_async_copy(gate_hbm, gate_v, gate_sem)
    cot_in = pltpu.make_async_copy(cot_hbm, cot_v, cot_sem)
    gate_in.start()
    cot_in.start()

    def pack(t, carry):
        last = xbc_ref[112:128, pl.ds(off(t, 128), 128)].astype(f32)
        for k in range(3):
            near[pl.ds((t // 10) * 32 + 10 * k + lax.rem(t, 10), 1), :] = last[13 + k : 14 + k]
        return carry

    lax.fori_loop(0, 80, pack, 0)
    for i in range(8):
        near[32 * i + 30 : 32 * i + 32, :] = jnp.zeros((2, 128), f32)
    ids = jnp.broadcast_to(seg_ref[...].astype(f32) + 1.0, (T, T)).T
    near[256:264, :] = jnp.zeros((8, 128), f32)
    near[256:259, :] = ids[T - 3 :]
    pl.semaphore_wait(barrier, 63 + 16)

    pltpu.make_async_copy(own_ref, w_ref.at[h], w_sem).start()
    for k in range(1, 4):
        pltpu.make_async_remote_copy(
            src_ref=own_ref, dst_ref=w_ref.at[h], send_sem=near_send, recv_sem=w_sem,
            device_id=at(me - h + lax.rem(h + k, 4)), device_id_type=MESH,
        ).start()

    @pl.when(me < 63)
    def _():
        pltpu.make_async_remote_copy(
            src_ref=near, dst_ref=halo, send_sem=near_sem, recv_sem=halo_sem,
            device_id=at(lax.rem(me + 1, 64)), device_id_type=MESH,
        ).start()

    @pl.when(me == 0)
    def _():
        halo[...] = jnp.zeros_like(halo)

    await_bytes(w_ref, w_sem)
    await_bytes(w_ref.at[pl.ds(0, 3)], near_send)

    @pl.when(me > 0)
    def _():
        await_bytes(halo, halo_sem)

    @pl.when(me < 63)
    def _():
        await_bytes(near, near_sem)

    make_prep(halo, w_ref, dt_ref, seg_ref, prep_ref, pb_ref, segs)

    def conv_turn(i, carry):
        g = turn(me, i)
        conv_group(g, xbc_ref, halo, w_ref, prep_ref, pb_ref, act_ref, pay_ref, ext)
        for s in range(8):
            p = 8 * g + s
            send_slot(me, p, pay_ref.at[p], got.at[me], send_sem, recv_sem)
        return carry

    lax.fori_loop(0, 8, conv_turn, 0)

    def forward(i, carry):
        inner_forward(i, act_ref, prep_ref, yi_s)
        return carry

    lax.fori_loop(0, 8, forward, 0)
    await_bytes(got, recv_sem)
    scan_up(got, start_own)


    rsum_ref[...] = jnp.zeros_like(rsum_ref)
    dskip_ref[...] = jnp.zeros_like(dskip_ref)
    send_back(me, start_own, codes, start_send, start_recv)
    gate_in.wait()
    cot_in.wait()

    def gate_turn(i, carry):
        g = turn(me, i)
        await_bytes(codes.at[pl.ds(8 * g, 8)], start_recv.at[g])
        gate_group(
            g, act_ref, yi_s, codes, start_ref, gate_v, cot_v, w_ref, pb_ref,
            dy_ref, dgate_v, pay2, dcc_ref, rsum_ref, dgain_ref, dskip_ref,
            alpha_s, cs_s, ady_s, qhi_s, qlo_s,
        )
        for s in range(8):
            p = 8 * g + s
            send_slot(me, p, pay2.at[p], got2.at[me], grad_send, grad_recv)
        return carry

    lax.fori_loop(0, 8, gate_turn, 0)
    dgate_out = pltpu.make_async_copy(dgate_v, dgate_hbm, gate_sem)
    dgate_out.start()
    csum[...] = jnp.zeros_like(csum)
    ksum[...] = jnp.zeros_like(ksum)
    rim[...] = jnp.zeros_like(rim)

    def backward(i, carry):
        inner_backward(i, act_ref, dy_ref, prep_ref, dcc_ref, yi_s, dbi, dcc_ref)
        return carry

    lax.fori_loop(0, 8, backward, 0)
    await_bytes(got2, grad_recv)
    scan_down(got, got2, end_own)
    send_back(me, end_own, end, back_send, back_recv)

    def back_turn(i, carry):
        g = turn(me, i)
        await_bytes(end.at[pl.ds(8 * g, 8)], back_recv.at[g])
        back_group(
            g, xbc_ref, halo, w_ref, act_ref, dy_ref, yi_s, dbi, dcc_ref, start_ref, pay_ref, end,
            prep_ref, pb_ref, dgain_ref, dxbc_ref, tail, rim, part, ext, dact, csum, ksum,
        )
        send_slot(
            me, me - h + g // 2, part.at[g], zbuf.at[h, lax.rem(g, 2)], z_send, z_sem
        )

        @pl.when(me > 0)
        def _():
            rows = pl.ds(pl.multiple_of(g * 32, 32), 32)
            pltpu.make_async_remote_copy(
                src_ref=rim.at[rows], dst_ref=rim_in.at[rows], send_sem=rim_send,
                recv_sem=rim_sem, device_id=at(lax.rem(me + 63, 64)), device_id_type=MESH,
            ).start()

        return carry

    lax.fori_loop(0, 8, back_turn, 0)

    high = (iota((T, T), 0) <= iota((T, T), 1)).astype(f32)
    step, decay = prep_ref[9], prep_ref[10]
    col = csum[...]
    dlog = mm(high, rsum_ref[...] - col, NN, lax.Precision.HIGHEST)
    dlog = dlog + jnp.sum(ksum[...], axis=0, keepdims=True)
    dstep = col / step - dlog * jnp.exp(params(w_ref, 0))
    ddt = dstep * prep_ref[11]
    ddt_ref[...] = ddt.astype(bf16)
    dhead[0:1, :] = jnp.sum(dlog * decay, axis=0, keepdims=True)
    dhead[1:2, :] = jnp.sum(ddt, axis=0, keepdims=True)
    dhead[2:3, :] = jnp.sum(dskip_ref[...], axis=0, keepdims=True)
    dhead[3:8, :] = jnp.zeros((5, HEADS), f32)
    pltpu.make_async_copy(dhead, hbuf.at[h], h_sem).start()
    for k in range(1, 4):
        pltpu.make_async_remote_copy(
            src_ref=dhead, dst_ref=hbuf.at[h], send_sem=h_send, recv_sem=h_sem,
            device_id=at(me - h + lax.rem(h + k, 4)), device_id_type=MESH,
        ).start()

    await_bytes(zbuf, z_sem)
    for q in range(2):
        own[10 * q : 10 * q + 10] = zbuf[0, q] + zbuf[1, q] + zbuf[2, q] + zbuf[3, q]
    await_bytes(hbuf, h_sem)
    own[20] = hbuf[0] + hbuf[1] + hbuf[2] + hbuf[3]
    rank = d * 16 + c

    def to_rank(r, src, dst, send_sem, recv_sem):
        @pl.when(r == rank)
        def _():
            pltpu.make_async_copy(src, dst, recv_sem).start()

        @pl.when(r != rank)
        def _():
            pltpu.make_async_remote_copy(
                src_ref=src, dst_ref=dst, send_sem=send_sem, recv_sem=recv_sem,
                device_id={"dp": r // 16, "ctx": lax.rem(r, 16), "head": h},
                device_id_type=MESH,
            ).start()

    def spread(r, carry):
        to_rank(r, own.at[r], rbuf.at[rank], r_send, r_sem)
        return carry

    lax.fori_loop(0, 21, spread, 0)

    @pl.when(rank < 21)
    def _():
        await_bytes(rbuf, r_sem)
        total[...] = jnp.sum(rbuf[...], axis=0)

        def share(k, carry):
            to_rank(lax.rem(rank + k, 32), total, fbuf.at[rank], f_send, f_sem)
            return carry

        lax.fori_loop(0, 32, share, 0)

    @pl.when(me < 63)
    def _():
        await_bytes(rim_in, rim_sem)

        def fix(t, carry):
            lanes = pl.ds(off(t, 128), 128)
            for k in range(3):
                row = rim_in[pl.ds((t // 10) * 32 + 10 * k + lax.rem(t, 10), 1), :]
                tail[13 + k : 14 + k, lanes] += row
            dxbc_ref[112:128, lanes] = tail[:, lanes].astype(bf16)
            return carry

        lax.fori_loop(0, 80, fix, 0)

    await_bytes(fbuf, f_sem)
    for q in range(2):
        for t in range(10):
            lanes = slice(GW * q + 128 * t, GW * q + 128 * t + 128)
            gconv_ref[:, lanes] = fbuf[10 * q + t, :5, :]
            if t < 8:
                lanes = slice(XW * q + 128 * t, XW * q + 128 * t + 128)
                ggain_ref[:, lanes] = fbuf[10 * q + t, 5:6, :]
    gheads_ref[...] = pltpu.roll(fbuf[20], lax.rem(128 - 32 * h, 128), 1)[:3, :32]

    await_bytes(end.at[pl.ds(0, 63)], back_send)
    await_bytes(hbuf.at[pl.ds(0, 3)], h_send)
    await_bytes(part.at[pl.ds(0, 6)], z_send)

    @pl.when(me > 0)
    def _():
        await_bytes(rim, rim_send)

    @pl.when(rank < 21)
    def _():
        await_bytes(rbuf.at[pl.ds(0, 20)], r_send)
        await_bytes(rbuf.at[pl.ds(0, 31)], f_send)

    @pl.when(rank >= 21)
    def _():
        await_bytes(rbuf.at[pl.ds(0, 21)], r_send)

    await_bytes(got.at[pl.ds(0, 63)], send_sem)
    await_bytes(codes.at[pl.ds(0, 63)], start_send)
    await_bytes(got2.at[pl.ds(0, 63)], grad_send)
    dgate_out.wait()


def hand_over(*refs):
    half = len(refs) // 2
    for src, dst in zip(refs[:half], refs[half:]):
        dst[...] = src[...]


def S(shape, dtype):
    return jax.ShapeDtypeStruct(shape, dtype)


def body(
    xbc_raw, gate_raw, dt_raw, segment_ids, conv_weight, norm_gain, head_params, out_cotangent
):
    xbc, gate, dt, cot = xbc_raw[0], gate_raw[0], dt_raw[0], out_cotangent[0]
    own_w = jnp.concatenate(
        [
            conv_weight,
            jnp.concatenate(
                [norm_gain[None], head_params.reshape(1, 96), jnp.zeros((1, 416), f32)], axis=1
            ),
        ],
        axis=0,
    )
    dma = pltpu.SemaphoreType.DMA
    near = pl.BlockSpec(memory_space=VMEM)
    far = pl.BlockSpec(memory_space=pl.ANY)
    outs = (
        S((T, CH), bf16),
        S((T, HP), bf16),
        S((T, HEADS), bf16),
        S((5, 2560), f32),
        S((1, 2048), f32),
        S((3, 32), f32),
    )
    results = pl.pallas_call(
        mixer,
        in_specs=[near, near, near, near, far, far],
        out_specs=[near, far, near, near, near, near],
        out_shape=outs,
        scratch_shapes=(
            VMEM((T, HP), bf16),
            VMEM((T, HP), bf16),
            VMEM((T, HP), bf16),
            VMEM((T, CH), bf16),
            VMEM((64, 144, 128), bf16),
            VMEM((12, T, T), f32),
            VMEM((3, T, 2 * T), bf16),
            VMEM((4, 6, 2560), f32),
            VMEM((264, 128), f32),
            VMEM((264, 128), f32),
            VMEM((64, 144, 128), bf16),
            VMEM((64, 144, 128), bf16),
            VMEM((64, 144, 128), bf16),
            VMEM((64, 128, 128), bf16),
            VMEM((T, HP), f32),
            VMEM((T, HP), bf16),
            VMEM((64, 128, 128), bf16),
            VMEM((64, 128, 128), bf16),
            VMEM((8, T, 128), f32),
            VMEM((8, T, 128), f32),
            VMEM((T, HEADS), f32),
            VMEM((8, 1, XW), f32),
            VMEM((16, HEADS), f32),
            VMEM((64, 128, 128), bf16),
            VMEM((64, 128, 128), bf16),
            VMEM((16, CH), f32),
            VMEM((256, 128), f32),
            VMEM((256, 128), f32),
            VMEM((8, 10, 8, 128), f32),
            VMEM((136, GW), f32),
            VMEM((136, 128), f32),
            VMEM((T, GW), bf16),
            VMEM((T, HEADS), f32),
            VMEM((8, HEADS), f32),
            VMEM((4, 2, 10, 8, 128), f32),
            VMEM((4, 8, 128), f32),
            VMEM((21, 8, 128), f32),
            VMEM((8, 128), f32),
            VMEM((32, 8, 128), f32),
            VMEM((8, 128), f32),
            VMEM((21, 8, 128), f32),
            VMEM((T, XW), f32),
            VMEM((T, XW), f32),
            VMEM((T, XW), bf16),
            VMEM((T, XW), bf16),
            VMEM((T, XW), bf16),
            *([dma] * 22),
            dma((8,)),
            dma((8,)),
        ),
        compiler_params=pltpu.CompilerParams(
            vmem_limit_bytes=58 << 20, collective_id=1, has_side_effects=True
        ),
        cost_estimate=pl.CostEstimate(flops=4 << 30, bytes_accessed=16 << 20, transcendentals=0),
        name="mixer",
    )(xbc, own_w, dt, segment_ids, gate, cot)

    def cut(shape, dtype):
        lead = (0,) * (len(shape) - 1)
        if shape[-1] > 4096:
            return pl.BlockSpec((shape[0], shape[1] // 8), lambda g: (0, g))
        return pl.BlockSpec(shape, lambda g: lead + (0,))

    specs = [cut(o.shape, o.dtype) for o in outs]
    dxbc, dgate, ddt, gconv, ggain, gheads = pl.pallas_call(
        hand_over,
        grid=(8,),
        in_specs=specs,
        out_specs=specs,
        out_shape=outs,
        name="hand_over",
    )(*results)
    return (dxbc[None], dgate[None], ddt[None], gconv, ggain[0], gheads)


def solution(mesh):
    token = P("dp", ("ctx", "head"), None)
    return jax.shard_map(
        body,
        mesh=mesh,
        in_specs=(
            token, token, token, P("dp", ("ctx", "head")),
            P(None, "head"), P("head"), P(None, "head"), token,
        ),
        out_specs=(token, token, token, P(None, "head"), P("head"), P(None, "head")),
        check_vma=False,
    )
```

```python
import jax
import jax.numpy as jnp
from jax import lax
from jax.experimental import pallas as pl
from jax.experimental.pallas import tpu as pltpu
from jax.sharding import PartitionSpec as P

HEADS = 128
GROUPS = 8
T = 128
GW = 1280
XW = 1024
CH = 10240
HP = 8192
LOG2E = 1.4426950408889634
EPS = 1e-05
NEG = -1e30
SPAN = 120.0
TINY = 1e-30
MESH = pl.DeviceIdType.MESH
VMEM = pltpu.VMEM

f32 = jnp.float32
bf16 = jnp.bfloat16
NN = ((1,), (0,))
NT = ((1,), (1,))
TN = ((0,), (0,))


def mm(a, b, dims=NN, precision=None):
    return lax.dot_general(a, b, (dims, ((), ())), preferred_element_type=f32, precision=precision)


def iota(shape, dim):
    return lax.broadcasted_iota(jnp.int32, shape, dim)


def sigmoid(v):
    return 0.5 * jnp.tanh(0.5 * v) + 0.5


def split(v):
    hi = v.astype(bf16)
    return hi, (v - hi.astype(f32)).astype(bf16)


def selector(g):
    return (iota((HEADS, XW), 0) == 16 * g + iota((HEADS, XW), 1) // 64).astype(f32).astype(bf16)


def twice(sel):
    return jnp.concatenate([sel, sel], axis=0)


def head_sums(v, sel):
    hi, lo = split(v)
    return mm(hi, sel, NT) + mm(lo, sel, NT)


def place():
    return lax.axis_index("ctx") * 4 + lax.axis_index("head")


def at(p):
    return {"ctx": p // 4, "head": lax.rem(p, 4)}


def off(index, width):
    return pl.multiple_of(index * width, width)


def greet(me):
    barrier = pltpu.get_barrier_semaphore()

    def one(k, carry):
        pl.semaphore_signal(
            barrier, inc=1, device_id=at(lax.rem(me + k, 64)), device_id_type=MESH
        )
        return carry

    lax.fori_loop(1, 64, one, 0)
    return barrier


def await_bytes(ref, sem):
    pltpu.make_async_copy(ref, ref, sem).wait()


def send_slot(me, p, src, dst, send_sem, recv_sem):
    @pl.when(p == me)
    def _():
        pltpu.make_async_copy(src, dst, recv_sem).start()

    @pl.when(p != me)
    def _():
        pltpu.make_async_remote_copy(
            src_ref=src, dst_ref=dst, send_sem=send_sem, recv_sem=recv_sem,
            device_id=at(p), device_id_type=MESH,
        ).start()


def turn(me, i):
    return lax.rem(me // 8 + i, 8)


def load_ext(g, ext, xbc_ref, halo):
    ext[8:136, :] = xbc_ref[:, pl.ds(off(g, GW), GW)].astype(f32)
    rows = pl.multiple_of(g * 32, 32)
    for k in range(3):
        for c in range(10):
            ext[5 + k : 6 + k, 128 * c : 128 * c + 128] = halo[pl.ds(rows + 10 * k + c, 1), :]


def windows(ext, prep_ref, lanes):
    return [
        ext[5:133, lanes] * prep_ref[6],
        ext[6:134, lanes] * prep_ref[7],
        ext[7:135, lanes] * prep_ref[8],
        ext[8:136, lanes],
    ]


def taps_of(w_refs, g, c):
    lanes = pl.ds(pl.multiple_of(lax.rem(g, 2) * GW + 128 * c, 128), 128)
    return [w_refs[0][g // 2, k : k + 1, lanes] for k in range(5)]


def conv(wins, taps):
    pre = taps[4] + taps[3] * wins[3]
    for k in range(3):
        pre = pre + taps[k] * wins[k]
    return pre


def params(w_refs, row):
    return jnp.concatenate([w_refs[2][q, row : row + 1, :32] for q in range(4)], axis=1)


def make_prep(halo, w_refs, dt_ref, seg_ref, prep_ref, pb_ref, segs):
    rate = jnp.exp(params(w_refs, 0))
    dtb = dt_ref[...].astype(f32) + params(w_refs, 1)
    step = jnp.maximum(dtb, 0.0) + jnp.log1p(jnp.exp(-jnp.abs(dtb)))
    decay = -step * rate
    rows, cols = iota((T, T), 0), iota((T, T), 1)
    low = (rows >= cols).astype(f32)
    run = mm(low, decay, NN, lax.Precision.HIGHEST) * LOG2E
    less = run - jnp.log(step) * LOG2E
    seg_row = jnp.broadcast_to(seg_ref[...].astype(f32) + 1.0, (T, T))
    seg_col = seg_row.T
    segs[8:136, :] = seg_col
    segs[5:8, :] = halo[256:259, :]
    prep_ref[0] = run
    prep_ref[1] = less
    prep_ref[2] = run.T
    prep_ref[3] = less.T
    same = seg_col == seg_row
    prep_ref[4] = jnp.where(same & (rows >= cols), 0.0, NEG)
    prep_ref[5] = jnp.where(same & (rows <= cols), 0.0, NEG)
    for k in range(3):
        prep_ref[6 + k] = (segs[5 + k : 133 + k, :] == seg_col).astype(f32)
    prep_ref[9] = step
    prep_ref[10] = decay
    linked = (seg_col == segs[7:8, :]).astype(f32)
    alpha = jnp.exp2(run) * linked
    omega = jnp.exp2(run[T - 1 :] - run) * (seg_col == seg_col[T - 1 :]).astype(f32) * step
    keep = alpha[T - 1 :]
    prep_ref[11] = sigmoid(dtb)
    for i, v in enumerate((alpha, omega)):
        hi, lo = split(v)
        pb_ref[i, :, :T] = hi
        pb_ref[i, :, T:] = lo
    both = jnp.where(rows == 0, params(w_refs, 2), keep)
    hi, lo = split(both)
    pb_ref[2, :, :T] = hi
    pb_ref[2, :, T:] = lo


def conv_group(g, xbc_ref, halo, w_refs, prep_ref, pb_ref, act_ref, slope, pay_ref, keep_own, ext):
    load_ext(g, ext, xbc_ref, halo)
    base = off(g, GW)
    for c in range(GW // 128):
        pre = conv(windows(ext, prep_ref, slice(128 * c, 128 * c + 128)), taps_of(w_refs, g, c))
        sg = sigmoid(pre)
        value = pre * sg
        act_ref[:, pl.ds(base + 128 * c, 128)] = value.astype(bf16)
        slope[:, pl.ds(base + 128 * c, 128)] = sg + value * (1.0 - sg)
    sel = selector(g)
    omega = mm(pb_ref[1], twice(sel))
    x_ref, b_ref, _ = parts_of(act_ref, g)
    weighted = (omega * x_ref[...].astype(f32)).astype(bf16)
    state = mm(b_ref[...], weighted, TN).astype(bf16)
    khi = mm(pb_ref[2, :16, :T], sel)
    klo = mm(pb_ref[2, :16, T:], sel)
    keep = khi[1:2] + klo[1:2]
    for i in range(8):
        lanes = slice(128 * i, 128 * i + 128)
        pay_ref[8 * g + i] = state[:, lanes]
        keep_own[8 * g + i] = keep[:, lanes]


def parts_of(act_ref, g):
    base = off(g, GW)
    return (
        act_ref.at[:, pl.ds(base, XW)],
        act_ref.at[:, pl.ds(base + XW, 128)],
        act_ref.at[:, pl.ds(base + XW + 128, 128)],
    )


def halves(v):
    left = iota(v.shape, 1) < 64
    zero = jnp.zeros_like(v)
    return jnp.concatenate([jnp.where(left, v, zero), jnp.where(left, zero, v)], axis=0)


def scan_up(keep_in, got_ref, start_ref, scale_ref):
    def one(j, state):
        top = jnp.maximum(jnp.max(jnp.abs(state), axis=0, keepdims=True) * 1.01, TINY)
        start_ref[j] = jnp.exp2(state * (SPAN / top)).astype(bf16)
        scale_ref[j] = top
        return keep_in[j] * state + got_ref[j].astype(f32)

    lax.fori_loop(0, 64, one, jnp.zeros((128, 128), f32))


def scan_down(keep_in, got_ref, end_ref):
    def one(i, grad):
        j = 63 - i
        end_ref[j] = grad.astype(bf16)
        return keep_in[j] * grad + got_ref[j].astype(f32)

    lax.fori_loop(0, 64, one, jnp.zeros((128, 128), f32))


def wide(slots_ref, g):
    return jnp.concatenate([slots_ref[8 * g + i] for i in range(8)], axis=1)


def inner_forward(g, act_ref, prep_ref, y_ref):
    x_ref, b_ref, c_ref = parts_of(act_ref, g)
    scores = mm(c_ref[...], b_ref[...], NT)
    run = pltpu.roll(prep_ref[0], lax.rem(128 - 16 * g, 128), 1)
    less = prep_ref[3, pl.ds(off(g, 16), 16), :]
    bias = prep_ref[4]
    for pair in range(8):
        mats = []
        for j in (2 * pair, 2 * pair + 1):
            el = jnp.exp2(run[:, j : j + 1] - less[j : j + 1, :] + bias)
            mats.append((el * scores).astype(bf16))
        lanes = slice(128 * pair, 128 * pair + 128)
        y_ref[:, pl.ds(off(g, XW) + 128 * pair, 128)] = mm(
            jnp.concatenate(mats, axis=1), halves(x_ref[:, lanes])
        )


def decode(code_ref, scale_ref, g):
    codes = wide(code_ref, g).astype(f32)
    scale = jnp.concatenate([scale_ref[8 * g + i] for i in range(8)], axis=1)
    return jnp.log2(codes) * (scale * (1.0 / SPAN))


def gate_group(
    g, act_ref, yi_ref, code_ref, scale_ref, start_ref, gate_ref, cot_ref, w_refs, pb_ref,
    dy_ref, dgate_ref, pay_ref, dcc_ref, rsum_ref, dgain_ref, dskip_ref,
    alpha_s, cs_s, ady_s, ady_lo, qhi_s, qlo_s,
):
    x_ref, _, c_ref = parts_of(act_ref, g)
    base = pl.ds(off(g, XW), XW)
    yi_ref, gate_ref, cot_ref = yi_ref.at[:, base], gate_ref.at[:, base], cot_ref.at[:, base]
    dy_ref, dgate_ref = dy_ref.at[:, base], dgate_ref.at[:, base]
    sel = selector(g)
    both = twice(sel)
    start, start_lo = split(decode(code_ref, scale_ref, g))
    for i in range(8):
        start_ref[8 * g + i] = start[:, 128 * i : 128 * i + 128]
    cs_s[...] = mm(c_ref[...], start) + mm(c_ref[...], start_lo)
    alpha_s[...] = mm(pb_ref[0], both)
    skip = mm(pb_ref[2, :16, :], both)[0:1]
    gain = w_refs[1][g // 2, :, pl.ds(off(lax.rem(g, 2), XW), XW)]
    dgain = jnp.zeros((16, XW), f32)
    dskip = jnp.zeros((16, XW), f32)
    for r in range(8):
        rows = slice(16 * r, 16 * r + 16)
        alpha = alpha_s[rows, :]
        yssm = yi_ref[rows, :] + alpha * cs_s[rows, :]
        x = x_ref[rows, :].astype(f32)
        ssm = (yssm + skip * x).astype(bf16).astype(f32)
        gate = gate_ref[rows, :].astype(f32)
        sg = sigmoid(gate)
        sl = gate * sg
        gated = ssm * sl
        rr = lax.rsqrt(jnp.sum(gated * gated, axis=1, keepdims=True) * (1.0 / XW) + EPS)
        norm = gated * rr
        cot = cot_ref[rows, :].astype(f32)
        dgain = dgain + cot * norm
        dn = cot * gain
        m2 = jnp.sum(dn * norm, axis=1, keepdims=True) * (1.0 / XW)
        dgated = rr * (dn - norm * m2)
        dy = (dgated * sl).astype(bf16)
        dy_ref[rows, :] = dy
        dgate_ref[rows, :] = (dgated * ssm * (sg + sl * (1.0 - sg))).astype(bf16)
        dyf = dy.astype(f32)
        hi, lo = split(alpha * dyf)
        ady_s[rows, :] = hi
        ady_lo[rows, :] = lo
        hi, lo = split(dyf * yssm)
        qhi_s[rows, :] = hi
        qlo_s[rows, :] = lo
        dskip = dskip + dyf * x
    ady = ady_s[...]
    dstart = (mm(c_ref[...], ady, TN) + mm(c_ref[...], ady_lo[...], TN)).astype(bf16)
    for i in range(8):
        pay_ref[8 * g + i] = dstart[:, 128 * i : 128 * i + 128]
    dcc_ref[g] = mm(ady, start, NT) + mm(ady, start_lo, NT) + mm(ady_lo[...], start, NT)
    rsum_ref[...] += mm(qhi_s[...], sel, NT) + mm(qlo_s[...], sel, NT)
    dskip_ref[...] += head_sums(dskip, sel)
    dgain_ref[g] = jnp.sum(dgain, axis=0, keepdims=True)


def send_turn(me, i, pairs):
    mine = me // 8
    group = lax.rem(mine + 8 - i, 8)
    for s in range(8):
        p = 8 * group + s
        for values, landing, send_sem, recv_sems in pairs:
            send_slot(me, p, values.at[p], landing.at[me], send_sem, recv_sems.at[mine])


def send_all(me, pairs):
    def one(i, carry):
        send_turn(me, i, pairs)
        return carry

    lax.fori_loop(0, 8, one, 0)


def inner_backward(g, act_ref, dy_ref, prep_ref, dcc_ref, dx_ref, db_ref, dc_ref):
    x_ref, b_ref, c_ref = parts_of(act_ref, g)
    scores = mm(b_ref[...], c_ref[...], NT)
    less = pltpu.roll(prep_ref[1], lax.rem(128 - 16 * g, 128), 1)
    run = prep_ref[2, pl.ds(off(g, 16), 16), :]
    bias = prep_ref[5]
    dscores = jnp.zeros((T, T), f32)
    for pair in range(8):
        out_lanes = pl.ds(off(g, XW) + 128 * pair, 128)
        dy2 = halves(dy_ref[:, out_lanes])
        dmat = mm(x_ref[:, 128 * pair : 128 * pair + 128], dy2, NT)
        mats = []
        for i in range(2):
            j = 2 * pair + i
            el = jnp.exp2(run[j : j + 1, :] - less[:, j : j + 1] + bias)
            mats.append((el * scores).astype(bf16))
            dscores = dscores + el * dmat[:, 128 * i : 128 * i + 128]
        dx_ref[:, out_lanes] = mm(jnp.concatenate(mats, axis=1), dy2)
    ds = dscores.astype(bf16)
    db_ref[g] = mm(ds, c_ref[...])
    dc_ref[g] = dcc_ref[g] + mm(ds, b_ref[...], TN)


def back_group(
    g, xbc_ref, halo, w_refs, act_ref, dy_ref, dxi, dbi, dci, start_ref, pay_ref, end,
    slope, prep_ref, pb_ref, dgain_ref, dxbc_ref, tail, rim, part, ext, dact, csum, ksum,
):
    x_ref, b_ref, _ = parts_of(act_ref, g)
    base = pl.ds(off(g, XW), XW)
    sel = selector(g)
    both = twice(sel)
    end_g = wide(end, g)
    rows16 = mm(pb_ref[2, :16, :], both)
    skip, keep = rows16[0:1], rows16[1:2]
    omega = mm(pb_ref[1], both)
    x = x_ref[...].astype(f32)
    dxs = dxi[:, base] + omega * mm(b_ref[...], end_g)
    csum[...] += head_sums(x * dxs, sel)
    dact[:, :XW] = (dxs + skip * dy_ref[:, base].astype(f32)).astype(bf16)
    dact[:, XW : XW + 128] = (dbi[g] + mm((omega * x).astype(bf16), end_g, NT)).astype(bf16)
    dact[:, XW + 128 :] = dci[g].astype(bf16)
    final = keep * wide(start_ref, g).astype(f32) + wide(pay_ref, g).astype(f32)
    ksum[...] += head_sums(jnp.sum((final * end_g.astype(f32)).reshape(16, 8, XW), axis=0), sel)

    load_ext(g, ext, xbc_ref, halo)
    rows = iota((T, 128), 0)
    for c in range(GW // 128):
        lanes = slice(128 * c, 128 * c + 128)
        wide_lanes = pl.ds(off(g, GW) + 128 * c, 128)
        taps = taps_of(w_refs, g, c)
        dpre = dact[:, lanes].astype(f32) * slope[:, wide_lanes]
        part[g, c, 3:4, :] = jnp.sum(dpre * ext[8:136, lanes], axis=0, keepdims=True)
        part[g, c, 4:5, :] = jnp.sum(dpre, axis=0, keepdims=True)
        if c < 8:
            part[g, c, 5:6, :] = dgain_ref[g, :, lanes]
        else:
            part[g, c, 5:6, :] = jnp.zeros((1, 128), f32)
        part[g, c, 6:8, :] = jnp.zeros((2, 128), f32)
        total = taps[3] * dpre
        over = jnp.zeros((8, 128), f32)
        for k in range(3):
            far = 3 - k
            used = dpre * prep_ref[6 + k]
            part[g, c, k : k + 1, :] = jnp.sum(
                used * ext[5 + k : 133 + k, lanes], axis=0, keepdims=True
            )
            moved = taps[k] * pltpu.roll(used, T - far, 0)
            inside = rows < T - far
            total = total + jnp.where(inside, moved, 0.0)
            over = over + jnp.where(inside, 0.0, moved)[T - 8 :]
        dxbc_ref[:, wide_lanes] = total.astype(bf16)
        tail[:, wide_lanes] = total[T - 16 :]
        for k in range(3):
            rim[pl.ds(pl.multiple_of(g * 32, 32) + 10 * k + c, 1), :] = over[5 + k : 6 + k]


def mixer(
    xbc_ref, own_conv, own_gain, own_head, dt_ref, seg_ref, gate_hbm, cot_hbm,
    dxbc_ref, dgate_hbm, ddt_ref, gconv_ref, ggain_ref, gheads_ref,
    gate_v, cot_v, dgate_v, act_ref, pay_ref, prep_ref, pb_ref, w_conv, w_gain, w_head, near, halo, got,
    start_own, codes, start_ref, yi_s, dy_ref, pay2, got2, dcc_ref, dbi, rsum_ref,
    dgain_ref, dskip_ref, end_own, end, tail, rim, rim_in, part, ext, segs, dact, csum,
    ksum, zbuf, hbuf, own, dhead, rbuf, total, fbuf, alpha_s, cs_s, ady_s, qhi_s, qlo_s,
    slope, ady_lo, keep_own, keep_in, scale_own, scales,
    keep_send, keep_recv, scale_send, gate_sem, cot_sem, near_sem, halo_sem, send_sem, recv_sem, start_send,
    grad_send, grad_recv, back_send, rim_send, rim_sem, z_send, z_sem, h_send, h_sem,
    r_send, r_sem, f_send, f_sem, near_send, w_sem, start_recv, back_recv, scale_recv,
):
    me = place()
    c, h, d = lax.axis_index("ctx"), lax.axis_index("head"), lax.axis_index("dp")
    barrier = greet(me)

    def greet_twin(k, carry):
        pl.semaphore_signal(
            barrier, inc=1, device_id={"dp": 1 - d, "ctx": k, "head": h}, device_id_type=MESH
        )
        return carry

    lax.fori_loop(0, 16, greet_twin, 0)
    gate_in = pltpu.make_async_copy(gate_hbm, gate_v, gate_sem)
    cot_in = pltpu.make_async_copy(cot_hbm, cot_v, cot_sem)
    gate_in.start()
    cot_in.start()

    for t in range(80):
        last = xbc_ref[112:128, 128 * t : 128 * t + 128].astype(f32)
        row = (t // 10) * 32 + t % 10
        for k in range(3):
            near[row + 10 * k : row + 10 * k + 1, :] = last[13 + k : 14 + k]
    for i in range(8):
        near[32 * i + 30 : 32 * i + 32, :] = jnp.zeros((2, 128), f32)
    ids = jnp.broadcast_to(seg_ref[...].astype(f32) + 1.0, (T, T)).T
    near[256:264, :] = jnp.zeros((8, 128), f32)
    near[256:259, :] = ids[T - 3 :]
    pl.semaphore_wait(barrier, 63 + 16)

    w_refs = (w_conv, w_gain, w_head)
    for n, own_w in enumerate((own_conv, own_gain, own_head)):
        pltpu.make_async_copy(own_w, w_refs[n].at[h], w_sem.at[n]).start()
        for k in range(1, 4):
            pltpu.make_async_remote_copy(
                src_ref=own_w, dst_ref=w_refs[n].at[h], send_sem=near_send.at[n],
                recv_sem=w_sem.at[n], device_id=at(me - h + lax.rem(h + k, 4)),
                device_id_type=MESH,
            ).start()

    @pl.when(me < 63)
    def _():
        pltpu.make_async_remote_copy(
            src_ref=near, dst_ref=halo, send_sem=near_sem, recv_sem=halo_sem,
            device_id=at(lax.rem(me + 1, 64)), device_id_type=MESH,
        ).start()

    @pl.when(me == 0)
    def _():
        halo[...] = jnp.zeros_like(halo)

    for n in range(3):
        await_bytes(w_refs[n], w_sem.at[n])
        await_bytes(w_refs[n].at[pl.ds(0, 3)], near_send.at[n])

    @pl.when(me > 0)
    def _():
        await_bytes(halo, halo_sem)

    @pl.when(me < 63)
    def _():
        await_bytes(near, near_sem)

    make_prep(halo, w_refs, dt_ref, seg_ref, prep_ref, pb_ref, segs)

    def conv_turn(i, carry):
        g = turn(me, i)
        conv_group(g, xbc_ref, halo, w_refs, prep_ref, pb_ref, act_ref, slope, pay_ref, keep_own, ext)
        for s in range(8):
            p = 8 * g + s
            send_slot(me, p, keep_own.at[p], keep_in.at[me], keep_send, keep_recv)
            send_slot(me, p, pay_ref.at[p], got.at[me], send_sem, recv_sem)
        return carry

    lax.fori_loop(0, 8, conv_turn, 0)

    def forward(i, carry):
        inner_forward(i, act_ref, prep_ref, yi_s)
        return carry

    lax.fori_loop(0, 8, forward, 0)
    await_bytes(keep_in, keep_recv)
    await_bytes(got, recv_sem)
    scan_up(keep_in, got, start_own, scale_own)


    rsum_ref[...] = jnp.zeros_like(rsum_ref)
    dskip_ref[...] = jnp.zeros_like(dskip_ref)
    starts = (
        (scale_own, scales, scale_send, scale_recv),
        (start_own, codes, start_send, start_recv),
    )
    send_all(me, starts)
    gate_in.wait()
    cot_in.wait()

    def gate_turn(i, carry):
        g = turn(me, i)
        await_bytes(scales.at[pl.ds(8 * g, 8)], scale_recv.at[g])
        await_bytes(codes.at[pl.ds(8 * g, 8)], start_recv.at[g])
        gate_group(
            g, act_ref, yi_s, codes, scales, start_ref, gate_v, cot_v, w_refs, pb_ref,
            dy_ref, dgate_v, pay2, dcc_ref, rsum_ref, dgain_ref, dskip_ref,
            alpha_s, cs_s, ady_s, ady_lo, qhi_s, qlo_s,
        )
        for s in range(8):
            p = 8 * g + s
            send_slot(me, p, pay2.at[p], got2.at[me], grad_send, grad_recv)
        return carry

    lax.fori_loop(0, 8, gate_turn, 0)
    dgate_out = pltpu.make_async_copy(dgate_v, dgate_hbm, gate_sem)
    dgate_out.start()
    csum[...] = jnp.zeros_like(csum)
    ksum[...] = jnp.zeros_like(ksum)
    rim[...] = jnp.zeros_like(rim)

    def backward(i, carry):
        inner_backward(i, act_ref, dy_ref, prep_ref, dcc_ref, yi_s, dbi, dcc_ref)
        return carry

    lax.fori_loop(0, 8, backward, 0)
    await_bytes(got2, grad_recv)
    scan_down(keep_in, got2, end_own)
    ends = ((end_own, end, back_send, back_recv),)
    send_all(me, ends)

    def back_turn(i, carry):
        g = turn(me, i)
        await_bytes(end.at[pl.ds(8 * g, 8)], back_recv.at[g])
        back_group(
            g, xbc_ref, halo, w_refs, act_ref, dy_ref, yi_s, dbi, dcc_ref, start_ref, pay_ref, end,
            slope, prep_ref, pb_ref, dgain_ref, dxbc_ref, tail, rim, part, ext, dact, csum, ksum,
        )
        send_slot(
            me, me - h + g // 2, part.at[g], zbuf.at[h, lax.rem(g, 2)], z_send, z_sem
        )

        @pl.when(me > 0)
        def _():
            rows = pl.ds(pl.multiple_of(g * 32, 32), 32)
            pltpu.make_async_remote_copy(
                src_ref=rim.at[rows], dst_ref=rim_in.at[rows], send_sem=rim_send,
                recv_sem=rim_sem, device_id=at(lax.rem(me + 63, 64)), device_id_type=MESH,
            ).start()

        return carry

    lax.fori_loop(0, 8, back_turn, 0)

    high = (iota((T, T), 0) <= iota((T, T), 1)).astype(f32)
    step, decay = prep_ref[9], prep_ref[10]
    col = csum[...]
    dlog = mm(high, rsum_ref[...] - col, NN, lax.Precision.HIGHEST)
    dlog = dlog + jnp.sum(ksum[...], axis=0, keepdims=True)
    dstep = col / step - dlog * jnp.exp(params(w_refs, 0))
    ddt = dstep * prep_ref[11]
    ddt_ref[...] = ddt.astype(bf16)
    dhead[0:1, :] = jnp.sum(dlog * decay, axis=0, keepdims=True)
    dhead[1:2, :] = jnp.sum(ddt, axis=0, keepdims=True)
    dhead[2:3, :] = jnp.sum(dskip_ref[...], axis=0, keepdims=True)
    dhead[3:8, :] = jnp.zeros((5, HEADS), f32)
    pltpu.make_async_copy(dhead, hbuf.at[h], h_sem).start()
    for k in range(1, 4):
        pltpu.make_async_remote_copy(
            src_ref=dhead, dst_ref=hbuf.at[h], send_sem=h_send, recv_sem=h_sem,
            device_id=at(me - h + lax.rem(h + k, 4)), device_id_type=MESH,
        ).start()

    await_bytes(zbuf, z_sem)
    for q in range(2):
        own[10 * q : 10 * q + 10] = zbuf[0, q] + zbuf[1, q] + zbuf[2, q] + zbuf[3, q]
    await_bytes(hbuf, h_sem)
    own[20] = hbuf[0] + hbuf[1] + hbuf[2] + hbuf[3]
    rank = d * 16 + c

    def to_rank(r, src, dst, send_sem, recv_sem):
        @pl.when(r == rank)
        def _():
            pltpu.make_async_copy(src, dst, recv_sem).start()

        @pl.when(r != rank)
        def _():
            pltpu.make_async_remote_copy(
                src_ref=src, dst_ref=dst, send_sem=send_sem, recv_sem=recv_sem,
                device_id={"dp": r // 16, "ctx": lax.rem(r, 16), "head": h},
                device_id_type=MESH,
            ).start()

    def spread(r, carry):
        to_rank(r, own.at[r], rbuf.at[rank], r_send, r_sem)
        return carry

    lax.fori_loop(0, 21, spread, 0)

    @pl.when(me < 63)
    def _():
        await_bytes(rim_in, rim_sem)
        for t in range(80):
            lanes = slice(128 * t, 128 * t + 128)
            row = (t // 10) * 32 + t % 10
            for k in range(3):
                tail[13 + k : 14 + k, lanes] += rim_in[row + 10 * k : row + 10 * k + 1, :]
            dxbc_ref[112:128, lanes] = tail[:, lanes].astype(bf16)

    @pl.when(rank < 21)
    def _():
        await_bytes(rbuf, r_sem)
        total[...] = jnp.sum(rbuf[...], axis=0)

        def share(k, carry):
            to_rank(lax.rem(rank + k, 32), total, fbuf.at[rank], f_send, f_sem)
            return carry

        lax.fori_loop(0, 32, share, 0)

    await_bytes(fbuf, f_sem)
    for q in range(2):
        for t in range(10):
            lanes = slice(GW * q + 128 * t, GW * q + 128 * t + 128)
            gconv_ref[:, lanes] = fbuf[10 * q + t, :5, :]
            if t < 8:
                lanes = slice(XW * q + 128 * t, XW * q + 128 * t + 128)
                ggain_ref[:, lanes] = fbuf[10 * q + t, 5:6, :]
    gheads_ref[...] = pltpu.roll(fbuf[20], lax.rem(128 - 32 * h, 128), 1)[:3, :32]

    await_bytes(end.at[pl.ds(0, 63)], back_send)
    await_bytes(hbuf.at[pl.ds(0, 3)], h_send)
    await_bytes(part.at[pl.ds(0, 6)], z_send)

    @pl.when(me > 0)
    def _():
        await_bytes(rim, rim_send)

    @pl.when(rank < 21)
    def _():
        await_bytes(rbuf.at[pl.ds(0, 20)], r_send)
        await_bytes(rbuf.at[pl.ds(0, 31)], f_send)

    @pl.when(rank >= 21)
    def _():
        await_bytes(rbuf.at[pl.ds(0, 21)], r_send)

    await_bytes(keep_in.at[pl.ds(0, 63)], keep_send)
    await_bytes(scales.at[pl.ds(0, 63)], scale_send)
    await_bytes(got.at[pl.ds(0, 63)], send_sem)
    await_bytes(codes.at[pl.ds(0, 63)], start_send)
    await_bytes(got2.at[pl.ds(0, 63)], grad_send)
    dgate_out.wait()


def hand_over(*refs):
    half = len(refs) // 2
    for src, dst in zip(refs[:half], refs[half:]):
        dst[...] = src[...]


def S(shape, dtype):
    return jax.ShapeDtypeStruct(shape, dtype)


def body(
    xbc_raw, gate_raw, dt_raw, segment_ids, conv_weight, norm_gain, head_params, out_cotangent
):
    xbc, gate, dt, cot = xbc_raw[0], gate_raw[0], dt_raw[0], out_cotangent[0]
    own_head = jnp.pad(head_params, ((0, 5), (0, 96)))
    dma = pltpu.SemaphoreType.DMA
    near = pl.BlockSpec(memory_space=VMEM)
    far = pl.BlockSpec(memory_space=pl.ANY)
    outs = (
        S((T, CH), bf16),
        S((T, HP), bf16),
        S((T, HEADS), bf16),
        S((5, 2560), f32),
        S((1, 2048), f32),
        S((3, 32), f32),
    )
    results = pl.pallas_call(
        mixer,
        in_specs=[near, near, near, near, near, near, far, far],
        out_specs=[near, far, near, near, near, near],
        out_shape=outs,
        scratch_shapes=(
            VMEM((T, HP), bf16),
            VMEM((T, HP), bf16),
            VMEM((T, HP), bf16),
            VMEM((T, CH), bf16),
            VMEM((64, 128, 128), bf16),
            VMEM((12, T, T), f32),
            VMEM((3, T, 2 * T), bf16),
            VMEM((4, 5, 2560), f32),
            VMEM((4, 1, 2048), f32),
            VMEM((4, 8, 128), f32),
            VMEM((264, 128), f32),
            VMEM((264, 128), f32),
            VMEM((64, 128, 128), bf16),
            VMEM((64, 128, 128), bf16),
            VMEM((64, 128, 128), bf16),
            VMEM((64, 128, 128), bf16),
            VMEM((T, HP), f32),
            VMEM((T, HP), bf16),
            VMEM((64, 128, 128), bf16),
            VMEM((64, 128, 128), bf16),
            VMEM((8, T, 128), f32),
            VMEM((8, T, 128), f32),
            VMEM((T, HEADS), f32),
            VMEM((8, 1, XW), f32),
            VMEM((16, HEADS), f32),
            VMEM((64, 128, 128), bf16),
            VMEM((64, 128, 128), bf16),
            VMEM((16, CH), f32),
            VMEM((256, 128), f32),
            VMEM((256, 128), f32),
            VMEM((8, 10, 8, 128), f32),
            VMEM((136, GW), f32),
            VMEM((136, 128), f32),
            VMEM((T, GW), bf16),
            VMEM((T, HEADS), f32),
            VMEM((8, HEADS), f32),
            VMEM((4, 2, 10, 8, 128), f32),
            VMEM((4, 8, 128), f32),
            VMEM((21, 8, 128), f32),
            VMEM((8, 128), f32),
            VMEM((32, 8, 128), f32),
            VMEM((8, 128), f32),
            VMEM((21, 8, 128), f32),
            VMEM((T, XW), f32),
            VMEM((T, XW), f32),
            VMEM((T, XW), bf16),
            VMEM((T, XW), bf16),
            VMEM((T, XW), bf16),
            VMEM((T, CH), f32),
            VMEM((T, XW), bf16),
            *([VMEM((64, 1, 128), f32)] * 4),
            *([dma] * 23),
            dma((3,)),
            dma((3,)),
            dma((8,)),
            dma((8,)),
            dma((8,)),
        ),
        compiler_params=pltpu.CompilerParams(
            vmem_limit_bytes=58 << 20, collective_id=1, has_side_effects=True
        ),
        cost_estimate=pl.CostEstimate(flops=4 << 30, bytes_accessed=16 << 20, transcendentals=0),
        name="mixer",
    )(xbc, conv_weight, norm_gain[None], own_head, dt, segment_ids, gate, cot)

    def cut(shape, dtype):
        lead = (0,) * (len(shape) - 1)
        if shape[-1] > 4096:
            return pl.BlockSpec((shape[0], shape[1] // 4), lambda g: (0, g))
        return pl.BlockSpec(shape, lambda g: lead + (0,))

    specs = [cut(o.shape, o.dtype) for o in outs]
    dxbc, dgate, ddt, gconv, ggain, gheads = pl.pallas_call(
        hand_over,
        grid=(4,),
        in_specs=specs,
        out_specs=specs,
        out_shape=outs,
        name="hand_over",
    )(*results)
    return (dxbc[None], dgate[None], ddt[None], gconv, ggain[0], gheads)


def solution(mesh):
    token = P("dp", ("ctx", "head"), None)
    return jax.shard_map(
        body,
        mesh=mesh,
        in_specs=(
            token, token, token, P("dp", ("ctx", "head")),
            P(None, "head"), P("head"), P(None, "head"), token,
        ),
        out_specs=(token, token, token, P(None, "head"), P("head"), P(None, "head")),
        check_vma=False,
    )
```

```python
import jax
import jax.numpy as jnp
from jax import lax
from jax.experimental import pallas as pl
from jax.experimental.pallas import tpu as pltpu
from jax.sharding import PartitionSpec as P

HEADS = 128
GROUPS = 8
T = 128
GW = 1280
XW = 1024
CH = 10240
HP = 8192
LOG2E = 1.4426950408889634
EPS = 1e-05
NEG = -1e30
SPAN = 120.0
TINY = 1e-30
MESH = pl.DeviceIdType.MESH
VMEM = pltpu.VMEM

f32 = jnp.float32
bf16 = jnp.bfloat16
NN = ((1,), (0,))
NT = ((1,), (1,))
TN = ((0,), (0,))


def mm(a, b, dims=NN, precision=None):
    return lax.dot_general(a, b, (dims, ((), ())), preferred_element_type=f32, precision=precision)


def iota(shape, dim):
    return lax.broadcasted_iota(jnp.int32, shape, dim)


def sigmoid(v):
    return 0.5 * jnp.tanh(0.5 * v) + 0.5


def split(v):
    hi = v.astype(bf16)
    return hi, (v - hi.astype(f32)).astype(bf16)


def selector(g):
    return (iota((HEADS, XW), 0) == 16 * g + iota((HEADS, XW), 1) // 64).astype(f32).astype(bf16)


def twice(sel):
    return jnp.concatenate([sel, sel], axis=0)


def head_sums(v, sel):
    hi, lo = split(v)
    return mm(hi, sel, NT) + mm(lo, sel, NT)


def place():
    return lax.axis_index("ctx") * 4 + lax.axis_index("head")


def at(p):
    return {"ctx": p // 4, "head": lax.rem(p, 4)}


def off(index, width):
    return pl.multiple_of(index * width, width)


def greet(me):
    barrier = pltpu.get_barrier_semaphore()

    def one(k, carry):
        pl.semaphore_signal(
            barrier, inc=1, device_id=at(lax.rem(me + k, 64)), device_id_type=MESH
        )
        return carry

    lax.fori_loop(1, 64, one, 0)
    return barrier


def await_bytes(ref, sem):
    pltpu.make_async_copy(ref, ref, sem).wait()


def send_slot(me, p, src, dst, send_sem, recv_sem):
    @pl.when(p == me)
    def _():
        pltpu.make_async_copy(src, dst, recv_sem).start()

    @pl.when(p != me)
    def _():
        pltpu.make_async_remote_copy(
            src_ref=src, dst_ref=dst, send_sem=send_sem, recv_sem=recv_sem,
            device_id=at(p), device_id_type=MESH,
        ).start()


def turn(me, i):
    return lax.rem(me // 8 + i, 8)


def load_ext(g, ext, xbc_ref, halo):
    ext[8:136, :] = xbc_ref[:, pl.ds(off(g, GW), GW)].astype(f32)
    rows = pl.multiple_of(g * 32, 32)
    for k in range(3):
        for c in range(10):
            ext[5 + k : 6 + k, 128 * c : 128 * c + 128] = halo[pl.ds(rows + 10 * k + c, 1), :]


def windows(ext, prep_ref, lanes):
    return [
        ext[5:133, lanes] * prep_ref[6],
        ext[6:134, lanes] * prep_ref[7],
        ext[7:135, lanes] * prep_ref[8],
        ext[8:136, lanes],
    ]


def taps_of(w_refs, g, c):
    lanes = pl.ds(pl.multiple_of(lax.rem(g, 2) * GW + 128 * c, 128), 128)
    return [w_refs[0][g // 2, k : k + 1, lanes] for k in range(5)]


def conv(wins, taps):
    pre = taps[4] + taps[3] * wins[3]
    for k in range(3):
        pre = pre + taps[k] * wins[k]
    return pre


def params(w_refs, row):
    return jnp.concatenate([w_refs[2][q, row : row + 1, :32] for q in range(4)], axis=1)


def make_prep(halo, w_refs, dt_ref, seg_ref, prep_ref, pb_ref, segs):
    rate = jnp.exp(params(w_refs, 0))
    dtb = dt_ref[...].astype(f32) + params(w_refs, 1)
    step = jnp.maximum(dtb, 0.0) + jnp.log1p(jnp.exp(-jnp.abs(dtb)))
    decay = -step * rate
    rows, cols = iota((T, T), 0), iota((T, T), 1)
    low = (rows >= cols).astype(f32)
    run = mm(low, decay, NN, lax.Precision.HIGHEST) * LOG2E
    less = run - jnp.log(step) * LOG2E
    seg_row = jnp.broadcast_to(seg_ref[...].astype(f32) + 1.0, (T, T))
    seg_col = seg_row.T
    segs[8:136, :] = seg_col
    segs[5:8, :] = halo[256:259, :]
    prep_ref[0] = run
    prep_ref[1] = less
    prep_ref[2] = run.T
    prep_ref[3] = less.T
    same = seg_col == seg_row
    prep_ref[4] = jnp.where(same & (rows >= cols), 0.0, NEG)
    prep_ref[5] = jnp.where(same & (rows <= cols), 0.0, NEG)
    for k in range(3):
        prep_ref[6 + k] = (segs[5 + k : 133 + k, :] == seg_col).astype(f32)
    prep_ref[9] = step
    prep_ref[10] = decay
    linked = (seg_col == segs[7:8, :]).astype(f32)
    alpha = jnp.exp2(run) * linked
    omega = jnp.exp2(run[T - 1 :] - run) * (seg_col == seg_col[T - 1 :]).astype(f32) * step
    keep = alpha[T - 1 :]
    prep_ref[11] = sigmoid(dtb)
    for i, v in enumerate((alpha, omega)):
        hi, lo = split(v)
        pb_ref[i, :, :T] = hi
        pb_ref[i, :, T:] = lo
    both = jnp.where(rows == 0, params(w_refs, 2), keep)
    hi, lo = split(both)
    pb_ref[2, :, :T] = hi
    pb_ref[2, :, T:] = lo


def conv_group(g, xbc_ref, halo, w_refs, prep_ref, pb_ref, act_ref, slope, pay_ref, keep_own, ext):
    load_ext(g, ext, xbc_ref, halo)
    base = off(g, GW)
    for c in range(GW // 128):
        pre = conv(windows(ext, prep_ref, slice(128 * c, 128 * c + 128)), taps_of(w_refs, g, c))
        sg = sigmoid(pre)
        value = pre * sg
        act_ref[:, pl.ds(base + 128 * c, 128)] = value.astype(bf16)
        slope[:, pl.ds(base + 128 * c, 128)] = sg + value * (1.0 - sg)
    sel = selector(g)
    omega = mm(pb_ref[1], twice(sel))
    x_ref, b_ref, _ = parts_of(act_ref, g)
    weighted = (omega * x_ref[...].astype(f32)).astype(bf16)
    state = mm(b_ref[...], weighted, TN).astype(bf16)
    khi = mm(pb_ref[2, :16, :T], sel)
    klo = mm(pb_ref[2, :16, T:], sel)
    keep = khi[1:2] + klo[1:2]
    for i in range(8):
        lanes = slice(128 * i, 128 * i + 128)
        pay_ref[8 * g + i] = state[:, lanes]
        keep_own[8 * g + i] = keep[:, lanes]


def parts_of(act_ref, g):
    base = off(g, GW)
    return (
        act_ref.at[:, pl.ds(base, XW)],
        act_ref.at[:, pl.ds(base + XW, 128)],
        act_ref.at[:, pl.ds(base + XW + 128, 128)],
    )


def halves(v):
    left = iota(v.shape, 1) < 64
    zero = jnp.zeros_like(v)
    return jnp.concatenate([jnp.where(left, v, zero), jnp.where(left, zero, v)], axis=0)


def scan_up(keep_in, got_ref, start_ref, scale_ref):
    def one(j, state):
        top = jnp.maximum(jnp.max(jnp.abs(state), axis=0, keepdims=True) * 1.01, TINY)
        start_ref[j] = jnp.exp2(state * (SPAN / top)).astype(bf16)
        scale_ref[j] = top
        return keep_in[j] * state + got_ref[j].astype(f32)

    lax.fori_loop(0, 64, one, jnp.zeros((128, 128), f32))


def scan_down(keep_in, got_ref, end_ref):
    def one(i, grad):
        j = 63 - i
        end_ref[j] = grad.astype(bf16)
        return keep_in[j] * grad + got_ref[j].astype(f32)

    lax.fori_loop(0, 64, one, jnp.zeros((128, 128), f32))


def wide(slots_ref, g):
    return jnp.concatenate([slots_ref[8 * g + i] for i in range(8)], axis=1)


def inner_forward(g, act_ref, prep_ref, y_ref):
    x_ref, b_ref, c_ref = parts_of(act_ref, g)
    scores = mm(c_ref[...], b_ref[...], NT)
    run = pltpu.roll(prep_ref[0], lax.rem(128 - 16 * g, 128), 1)
    less = prep_ref[3, pl.ds(off(g, 16), 16), :]
    bias = prep_ref[4]
    for pair in range(8):
        mats = []
        for j in (2 * pair, 2 * pair + 1):
            el = jnp.exp2(run[:, j : j + 1] - less[j : j + 1, :] + bias)
            mats.append((el * scores).astype(bf16))
        lanes = slice(128 * pair, 128 * pair + 128)
        y_ref[:, pl.ds(off(g, XW) + 128 * pair, 128)] = mm(
            jnp.concatenate(mats, axis=1), halves(x_ref[:, lanes])
        )


def decode(code_ref, scale_ref, g):
    codes = wide(code_ref, g).astype(f32)
    scale = jnp.concatenate([scale_ref[8 * g + i] for i in range(8)], axis=1)
    return jnp.log2(codes) * (scale * (1.0 / SPAN))


def gate_group(
    g, act_ref, yi_ref, code_ref, scale_ref, start_ref, gate_ref, cot_ref, w_refs, pb_ref,
    dy_ref, dgate_ref, pay_ref, dcc_ref, rsum_ref, dgain_ref, dskip_ref,
    alpha_s, cs_s, ady_s, ady_lo, qhi_s, qlo_s,
):
    x_ref, _, c_ref = parts_of(act_ref, g)
    base = pl.ds(off(g, XW), XW)
    yi_ref, gate_ref, cot_ref = yi_ref.at[:, base], gate_ref.at[:, base], cot_ref.at[:, base]
    dy_ref, dgate_ref = dy_ref.at[:, base], dgate_ref.at[:, base]
    sel = selector(g)
    both = twice(sel)
    start, start_lo = split(decode(code_ref, scale_ref, g))
    for i in range(8):
        start_ref[8 * g + i] = start[:, 128 * i : 128 * i + 128]
    cs_s[...] = mm(c_ref[...], start) + mm(c_ref[...], start_lo)
    alpha_s[...] = mm(pb_ref[0], both)
    skip = mm(pb_ref[2, :16, :], both)[0:1]
    gain = w_refs[1][g // 2, :, pl.ds(off(lax.rem(g, 2), XW), XW)]
    dgain = jnp.zeros((16, XW), f32)
    dskip = jnp.zeros((16, XW), f32)
    for r in range(8):
        rows = slice(16 * r, 16 * r + 16)
        alpha = alpha_s[rows, :]
        yssm = yi_ref[rows, :] + alpha * cs_s[rows, :]
        x = x_ref[rows, :].astype(f32)
        ssm = (yssm + skip * x).astype(bf16).astype(f32)
        gate = gate_ref[rows, :].astype(f32)
        sg = sigmoid(gate)
        sl = gate * sg
        gated = ssm * sl
        rr = lax.rsqrt(jnp.sum(gated * gated, axis=1, keepdims=True) * (1.0 / XW) + EPS)
        norm = gated * rr
        cot = cot_ref[rows, :].astype(f32)
        dgain = dgain + cot * norm
        dn = cot * gain
        m2 = jnp.sum(dn * norm, axis=1, keepdims=True) * (1.0 / XW)
        dgated = rr * (dn - norm * m2)
        dy = (dgated * sl).astype(bf16)
        dy_ref[rows, :] = dy
        dgate_ref[rows, :] = (dgated * ssm * (sg + sl * (1.0 - sg))).astype(bf16)
        dyf = dy.astype(f32)
        hi, lo = split(alpha * dyf)
        ady_s[rows, :] = hi
        ady_lo[rows, :] = lo
        hi, lo = split(dyf * yssm)
        qhi_s[rows, :] = hi
        qlo_s[rows, :] = lo
        dskip = dskip + dyf * x
    ady = ady_s[...]
    dstart = (mm(c_ref[...], ady, TN) + mm(c_ref[...], ady_lo[...], TN)).astype(bf16)
    for i in range(8):
        pay_ref[8 * g + i] = dstart[:, 128 * i : 128 * i + 128]
    dcc_ref[g] = mm(ady, start, NT) + mm(ady, start_lo, NT) + mm(ady_lo[...], start, NT)
    rsum_ref[...] += mm(qhi_s[...], sel, NT) + mm(qlo_s[...], sel, NT)
    dskip_ref[...] += head_sums(dskip, sel)
    dgain_ref[g] = jnp.sum(dgain, axis=0, keepdims=True)


def send_turn(me, i, pairs):
    mine = me // 8
    group = lax.rem(mine + 8 - i, 8)
    for s in range(8):
        p = 8 * group + s
        for values, landing, send_sem, recv_sems in pairs:
            send_slot(me, p, values.at[p], landing.at[me], send_sem, recv_sems.at[mine])


def send_all(me, pairs):
    def one(i, carry):
        send_turn(me, i, pairs)
        return carry

    lax.fori_loop(0, 8, one, 0)


def inner_backward(g, act_ref, dy_ref, prep_ref, dcc_ref, dx_ref, db_ref, dc_ref):
    x_ref, b_ref, c_ref = parts_of(act_ref, g)
    scores = mm(b_ref[...], c_ref[...], NT)
    less = pltpu.roll(prep_ref[1], lax.rem(128 - 16 * g, 128), 1)
    run = prep_ref[2, pl.ds(off(g, 16), 16), :]
    bias = prep_ref[5]
    dscores = jnp.zeros((T, T), f32)
    for pair in range(8):
        out_lanes = pl.ds(off(g, XW) + 128 * pair, 128)
        dy2 = halves(dy_ref[:, out_lanes])
        dmat = mm(x_ref[:, 128 * pair : 128 * pair + 128], dy2, NT)
        mats = []
        for i in range(2):
            j = 2 * pair + i
            el = jnp.exp2(run[j : j + 1, :] - less[:, j : j + 1] + bias)
            mats.append((el * scores).astype(bf16))
            dscores = dscores + el * dmat[:, 128 * i : 128 * i + 128]
        dx_ref[:, out_lanes] = mm(jnp.concatenate(mats, axis=1), dy2)
    ds = dscores.astype(bf16)
    db_ref[g] = mm(ds, c_ref[...])
    dc_ref[g] = dcc_ref[g] + mm(ds, b_ref[...], TN)


def back_group(
    g, xbc_ref, halo, w_refs, act_ref, dy_ref, dxi, dbi, dci, start_ref, pay_ref, end,
    slope, prep_ref, pb_ref, dgain_ref, dxbc_ref, tail, rim, part, ext, dact, csum, ksum,
):
    x_ref, b_ref, _ = parts_of(act_ref, g)
    base = pl.ds(off(g, XW), XW)
    sel = selector(g)
    both = twice(sel)
    end_g = wide(end, g)
    rows16 = mm(pb_ref[2, :16, :], both)
    skip, keep = rows16[0:1], rows16[1:2]
    omega = mm(pb_ref[1], both)
    x = x_ref[...].astype(f32)
    dxs = dxi[:, base] + omega * mm(b_ref[...], end_g)
    csum[...] += head_sums(x * dxs, sel)
    dact[:, :XW] = (dxs + skip * dy_ref[:, base].astype(f32)).astype(bf16)
    dact[:, XW : XW + 128] = (dbi[g] + mm((omega * x).astype(bf16), end_g, NT)).astype(bf16)
    dact[:, XW + 128 :] = dci[g].astype(bf16)
    final = keep * wide(start_ref, g).astype(f32) + wide(pay_ref, g).astype(f32)
    ksum[...] += head_sums(jnp.sum((final * end_g.astype(f32)).reshape(16, 8, XW), axis=0), sel)

    load_ext(g, ext, xbc_ref, halo)
    rows = iota((T, 128), 0)
    for c in range(GW // 128):
        lanes = slice(128 * c, 128 * c + 128)
        wide_lanes = pl.ds(off(g, GW) + 128 * c, 128)
        taps = taps_of(w_refs, g, c)
        dpre = dact[:, lanes].astype(f32) * slope[:, wide_lanes]
        part[g, c, 3:4, :] = jnp.sum(dpre * ext[8:136, lanes], axis=0, keepdims=True)
        part[g, c, 4:5, :] = jnp.sum(dpre, axis=0, keepdims=True)
        if c < 8:
            part[g, c, 5:6, :] = dgain_ref[g, :, lanes]
        else:
            part[g, c, 5:6, :] = jnp.zeros((1, 128), f32)
        part[g, c, 6:8, :] = jnp.zeros((2, 128), f32)
        total = taps[3] * dpre
        over = jnp.zeros((8, 128), f32)
        for k in range(3):
            far = 3 - k
            used = dpre * prep_ref[6 + k]
            part[g, c, k : k + 1, :] = jnp.sum(
                used * ext[5 + k : 133 + k, lanes], axis=0, keepdims=True
            )
            moved = taps[k] * pltpu.roll(used, T - far, 0)
            inside = rows < T - far
            total = total + jnp.where(inside, moved, 0.0)
            over = over + jnp.where(inside, 0.0, moved)[T - 8 :]
        dxbc_ref[:, wide_lanes] = total.astype(bf16)
        tail[:, wide_lanes] = total[T - 16 :]
        for k in range(3):
            rim[pl.ds(pl.multiple_of(g * 32, 32) + 10 * k + c, 1), :] = over[5 + k : 6 + k]


def mixer(
    xbc_ref, own_conv, own_gain, own_head, dt_ref, seg_ref, gate_hbm, cot_hbm,
    dxbc_ref, dgate_hbm, ddt_ref, gconv_ref, ggain_ref, gheads_ref,
    gate_v, cot_v, dgate_v, act_ref, pay_ref, prep_ref, pb_ref, w_conv, w_gain, w_head, near, halo, got,
    start_own, codes, start_ref, yi_s, dy_ref, pay2, got2, dcc_ref, dbi, rsum_ref,
    dgain_ref, dskip_ref, end_own, end, tail, rim, rim_in, part, ext, segs, dact, csum,
    ksum, zbuf, hbuf, own, dhead, rbuf, total, fbuf, alpha_s, cs_s, ady_s, qhi_s, qlo_s,
    slope, ady_lo, keep_own, keep_in, scale_own, scales,
    keep_send, keep_recv, scale_send, gate_sem, cot_sem, near_sem, halo_sem, send_sem, recv_sem, start_send,
    grad_send, grad_recv, back_send, rim_send, rim_sem, z_send, z_sem, h_send, h_sem,
    r_send, r_sem, f_send, f_sem, near_send, w_sem, start_recv, back_recv, scale_recv,
):
    me = place()
    c, h, d = lax.axis_index("ctx"), lax.axis_index("head"), lax.axis_index("dp")
    barrier = greet(me)

    def greet_twin(k, carry):
        pl.semaphore_signal(
            barrier, inc=1, device_id={"dp": 1 - d, "ctx": k, "head": h}, device_id_type=MESH
        )
        return carry

    lax.fori_loop(0, 16, greet_twin, 0)
    gate_in = pltpu.make_async_copy(gate_hbm, gate_v, gate_sem)
    cot_in = pltpu.make_async_copy(cot_hbm, cot_v, cot_sem)
    gate_in.start()
    cot_in.start()

    for t in range(80):
        last = xbc_ref[112:128, 128 * t : 128 * t + 128].astype(f32)
        row = (t // 10) * 32 + t % 10
        for k in range(3):
            near[row + 10 * k : row + 10 * k + 1, :] = last[13 + k : 14 + k]
    for i in range(8):
        near[32 * i + 30 : 32 * i + 32, :] = jnp.zeros((2, 128), f32)
    ids = jnp.broadcast_to(seg_ref[...].astype(f32) + 1.0, (T, T)).T
    near[256:264, :] = jnp.zeros((8, 128), f32)
    near[256:259, :] = ids[T - 3 :]
    pl.semaphore_wait(barrier, 63 + 16)

    @pl.when(me < 63)
    def _():
        pltpu.make_async_remote_copy(
            src_ref=near, dst_ref=halo, send_sem=near_sem, recv_sem=halo_sem,
            device_id=at(lax.rem(me + 1, 64)), device_id_type=MESH,
        ).start()

    w_refs = (w_conv, w_gain, w_head)
    for n, own_w in enumerate((own_conv, own_gain, own_head)):
        pltpu.make_async_copy(own_w, w_refs[n].at[h], w_sem.at[n]).start()
        for k in range(1, 4):
            pltpu.make_async_remote_copy(
                src_ref=own_w, dst_ref=w_refs[n].at[h], send_sem=near_send.at[n],
                recv_sem=w_sem.at[n], device_id=at(me - h + lax.rem(h + k, 4)),
                device_id_type=MESH,
            ).start()

    @pl.when(me == 0)
    def _():
        halo[...] = jnp.zeros_like(halo)

    for n in range(3):
        await_bytes(w_refs[n], w_sem.at[n])
        await_bytes(w_refs[n].at[pl.ds(0, 3)], near_send.at[n])

    @pl.when(me > 0)
    def _():
        await_bytes(halo, halo_sem)

    @pl.when(me < 63)
    def _():
        await_bytes(near, near_sem)

    make_prep(halo, w_refs, dt_ref, seg_ref, prep_ref, pb_ref, segs)

    def conv_turn(i, carry):
        g = turn(me, i)
        conv_group(g, xbc_ref, halo, w_refs, prep_ref, pb_ref, act_ref, slope, pay_ref, keep_own, ext)
        for s in range(8):
            p = 8 * g + s
            send_slot(me, p, keep_own.at[p], keep_in.at[me], keep_send, keep_recv)
            send_slot(me, p, pay_ref.at[p], got.at[me], send_sem, recv_sem)
        return carry

    lax.fori_loop(0, 8, conv_turn, 0)

    def forward(i, carry):
        inner_forward(i, act_ref, prep_ref, yi_s)
        return carry

    lax.fori_loop(0, 8, forward, 0)
    await_bytes(keep_in, keep_recv)
    await_bytes(got, recv_sem)
    scan_up(keep_in, got, start_own, scale_own)


    rsum_ref[...] = jnp.zeros_like(rsum_ref)
    dskip_ref[...] = jnp.zeros_like(dskip_ref)
    starts = (
        (scale_own, scales, scale_send, scale_recv),
        (start_own, codes, start_send, start_recv),
    )
    send_all(me, starts)
    gate_in.wait()
    cot_in.wait()

    def gate_turn(i, carry):
        g = turn(me, i)
        await_bytes(scales.at[pl.ds(8 * g, 8)], scale_recv.at[g])
        await_bytes(codes.at[pl.ds(8 * g, 8)], start_recv.at[g])
        gate_group(
            g, act_ref, yi_s, codes, scales, start_ref, gate_v, cot_v, w_refs, pb_ref,
            dy_ref, dgate_v, pay2, dcc_ref, rsum_ref, dgain_ref, dskip_ref,
            alpha_s, cs_s, ady_s, ady_lo, qhi_s, qlo_s,
        )
        for s in range(8):
            p = 8 * g + s
            send_slot(me, p, pay2.at[p], got2.at[me], grad_send, grad_recv)
        return carry

    lax.fori_loop(0, 8, gate_turn, 0)
    dgate_out = pltpu.make_async_copy(dgate_v, dgate_hbm, gate_sem)
    dgate_out.start()
    csum[...] = jnp.zeros_like(csum)
    ksum[...] = jnp.zeros_like(ksum)
    rim[...] = jnp.zeros_like(rim)

    def backward(i, carry):
        inner_backward(i, act_ref, dy_ref, prep_ref, dcc_ref, yi_s, dbi, dcc_ref)
        return carry

    lax.fori_loop(0, 8, backward, 0)
    await_bytes(got2, grad_recv)
    scan_down(keep_in, got2, end_own)
    ends = ((end_own, end, back_send, back_recv),)
    send_all(me, ends)

    def back_turn(i, carry):
        g = turn(me, i)
        await_bytes(end.at[pl.ds(8 * g, 8)], back_recv.at[g])
        back_group(
            g, xbc_ref, halo, w_refs, act_ref, dy_ref, yi_s, dbi, dcc_ref, start_ref, pay_ref, end,
            slope, prep_ref, pb_ref, dgain_ref, dxbc_ref, tail, rim, part, ext, dact, csum, ksum,
        )
        send_slot(
            me, me - h + g // 2, part.at[g], zbuf.at[h, lax.rem(g, 2)], z_send, z_sem
        )

        @pl.when(me > 0)
        def _():
            rows = pl.ds(pl.multiple_of(g * 32, 32), 32)
            pltpu.make_async_remote_copy(
                src_ref=rim.at[rows], dst_ref=rim_in.at[rows], send_sem=rim_send,
                recv_sem=rim_sem, device_id=at(lax.rem(me + 63, 64)), device_id_type=MESH,
            ).start()

        return carry

    lax.fori_loop(0, 8, back_turn, 0)

    high = (iota((T, T), 0) <= iota((T, T), 1)).astype(f32)
    step, decay = prep_ref[9], prep_ref[10]
    col = csum[...]
    dlog = mm(high, rsum_ref[...] - col, NN, lax.Precision.HIGHEST)
    dlog = dlog + jnp.sum(ksum[...], axis=0, keepdims=True)
    dstep = col / step - dlog * jnp.exp(params(w_refs, 0))
    ddt = dstep * prep_ref[11]
    ddt_ref[...] = ddt.astype(bf16)
    dhead[0:1, :] = jnp.sum(dlog * decay, axis=0, keepdims=True)
    dhead[1:2, :] = jnp.sum(ddt, axis=0, keepdims=True)
    dhead[2:3, :] = jnp.sum(dskip_ref[...], axis=0, keepdims=True)
    dhead[3:8, :] = jnp.zeros((5, HEADS), f32)
    pltpu.make_async_copy(dhead, hbuf.at[h], h_sem).start()
    for k in range(1, 4):
        pltpu.make_async_remote_copy(
            src_ref=dhead, dst_ref=hbuf.at[h], send_sem=h_send, recv_sem=h_sem,
            device_id=at(me - h + lax.rem(h + k, 4)), device_id_type=MESH,
        ).start()

    await_bytes(zbuf, z_sem)
    for q in range(2):
        own[10 * q : 10 * q + 10] = zbuf[0, q] + zbuf[1, q] + zbuf[2, q] + zbuf[3, q]
    await_bytes(hbuf, h_sem)
    own[20] = hbuf[0] + hbuf[1] + hbuf[2] + hbuf[3]
    rank = d * 16 + c

    def to_rank(r, src, dst, send_sem, recv_sem):
        @pl.when(r == rank)
        def _():
            pltpu.make_async_copy(src, dst, recv_sem).start()

        @pl.when(r != rank)
        def _():
            pltpu.make_async_remote_copy(
                src_ref=src, dst_ref=dst, send_sem=send_sem, recv_sem=recv_sem,
                device_id={"dp": r // 16, "ctx": lax.rem(r, 16), "head": h},
                device_id_type=MESH,
            ).start()

    def spread(r, carry):
        to_rank(r, own.at[r], rbuf.at[rank], r_send, r_sem)
        return carry

    lax.fori_loop(0, 21, spread, 0)

    @pl.when(me < 63)
    def _():
        await_bytes(rim_in, rim_sem)
        for t in range(80):
            lanes = slice(128 * t, 128 * t + 128)
            row = (t // 10) * 32 + t % 10
            for k in range(3):
                tail[13 + k : 14 + k, lanes] += rim_in[row + 10 * k : row + 10 * k + 1, :]
            dxbc_ref[112:128, lanes] = tail[:, lanes].astype(bf16)

    @pl.when(rank < 21)
    def _():
        await_bytes(rbuf, r_sem)
        total[...] = jnp.sum(rbuf[...], axis=0)

        def share(k, carry):
            to_rank(lax.rem(rank + k, 32), total, fbuf.at[rank], f_send, f_sem)
            return carry

        lax.fori_loop(0, 32, share, 0)

    await_bytes(fbuf, f_sem)
    for q in range(2):
        for t in range(10):
            lanes = slice(GW * q + 128 * t, GW * q + 128 * t + 128)
            gconv_ref[:, lanes] = fbuf[10 * q + t, :5, :]
            if t < 8:
                lanes = slice(XW * q + 128 * t, XW * q + 128 * t + 128)
                ggain_ref[:, lanes] = fbuf[10 * q + t, 5:6, :]
    gheads_ref[...] = pltpu.roll(fbuf[20], lax.rem(128 - 32 * h, 128), 1)[:3, :32]

    await_bytes(end.at[pl.ds(0, 63)], back_send)
    await_bytes(hbuf.at[pl.ds(0, 3)], h_send)
    await_bytes(part.at[pl.ds(0, 6)], z_send)

    @pl.when(me > 0)
    def _():
        await_bytes(rim, rim_send)

    @pl.when(rank < 21)
    def _():
        await_bytes(rbuf.at[pl.ds(0, 20)], r_send)
        await_bytes(rbuf.at[pl.ds(0, 31)], f_send)

    @pl.when(rank >= 21)
    def _():
        await_bytes(rbuf.at[pl.ds(0, 21)], r_send)

    await_bytes(keep_in.at[pl.ds(0, 63)], keep_send)
    await_bytes(scales.at[pl.ds(0, 63)], scale_send)
    await_bytes(got.at[pl.ds(0, 63)], send_sem)
    await_bytes(codes.at[pl.ds(0, 63)], start_send)
    await_bytes(got2.at[pl.ds(0, 63)], grad_send)
    dgate_out.wait()


def hand_over(*refs):
    half = len(refs) // 2
    for src, dst in zip(refs[:half], refs[half:]):
        dst[...] = src[...]


def S(shape, dtype):
    return jax.ShapeDtypeStruct(shape, dtype)


def body(
    xbc_raw, gate_raw, dt_raw, segment_ids, conv_weight, norm_gain, head_params, out_cotangent
):
    xbc, gate, dt, cot = xbc_raw[0], gate_raw[0], dt_raw[0], out_cotangent[0]
    own_head = jnp.pad(head_params, ((0, 5), (0, 96)))
    dma = pltpu.SemaphoreType.DMA
    near = pl.BlockSpec(memory_space=VMEM)
    far = pl.BlockSpec(memory_space=pl.ANY)
    outs = (
        S((T, CH), bf16),
        S((T, HP), bf16),
        S((T, HEADS), bf16),
        S((5, 2560), f32),
        S((1, 2048), f32),
        S((3, 32), f32),
    )
    results = pl.pallas_call(
        mixer,
        in_specs=[near, near, near, near, near, near, far, far],
        out_specs=[near, far, near, near, near, near],
        out_shape=outs,
        scratch_shapes=(
            VMEM((T, HP), bf16),
            VMEM((T, HP), bf16),
            VMEM((T, HP), bf16),
            VMEM((T, CH), bf16),
            VMEM((64, 128, 128), bf16),
            VMEM((12, T, T), f32),
            VMEM((3, T, 2 * T), bf16),
            VMEM((4, 5, 2560), f32),
            VMEM((4, 1, 2048), f32),
            VMEM((4, 8, 128), f32),
            VMEM((264, 128), f32),
            VMEM((264, 128), f32),
            VMEM((64, 128, 128), bf16),
            VMEM((64, 128, 128), bf16),
            VMEM((64, 128, 128), bf16),
            VMEM((64, 128, 128), bf16),
            VMEM((T, HP), f32),
            VMEM((T, HP), bf16),
            VMEM((64, 128, 128), bf16),
            VMEM((64, 128, 128), bf16),
            VMEM((8, T, 128), f32),
            VMEM((8, T, 128), f32),
            VMEM((T, HEADS), f32),
            VMEM((8, 1, XW), f32),
            VMEM((16, HEADS), f32),
            VMEM((64, 128, 128), bf16),
            VMEM((64, 128, 128), bf16),
            VMEM((16, CH), f32),
            VMEM((256, 128), f32),
            VMEM((256, 128), f32),
            VMEM((8, 10, 8, 128), f32),
            VMEM((136, GW), f32),
            VMEM((136, 128), f32),
            VMEM((T, GW), bf16),
            VMEM((T, HEADS), f32),
            VMEM((8, HEADS), f32),
            VMEM((4, 2, 10, 8, 128), f32),
            VMEM((4, 8, 128), f32),
            VMEM((21, 8, 128), f32),
            VMEM((8, 128), f32),
            VMEM((32, 8, 128), f32),
            VMEM((8, 128), f32),
            VMEM((21, 8, 128), f32),
            VMEM((T, XW), f32),
            VMEM((T, XW), f32),
            VMEM((T, XW), bf16),
            VMEM((T, XW), bf16),
            VMEM((T, XW), bf16),
            VMEM((T, CH), f32),
            VMEM((T, XW), bf16),
            *([VMEM((64, 1, 128), f32)] * 4),
            *([dma] * 23),
            dma((3,)),
            dma((3,)),
            dma((8,)),
            dma((8,)),
            dma((8,)),
        ),
        compiler_params=pltpu.CompilerParams(
            vmem_limit_bytes=58 << 20, collective_id=1, has_side_effects=True
        ),
        cost_estimate=pl.CostEstimate(flops=4 << 30, bytes_accessed=16 << 20, transcendentals=0),
        name="mixer",
    )(xbc, conv_weight, norm_gain[None], own_head, dt, segment_ids, gate, cot)

    def cut(shape, dtype):
        lead = (0,) * (len(shape) - 1)
        if shape[-1] > 4096:
            return pl.BlockSpec((shape[0], shape[1] // 4), lambda g: (0, g))
        return pl.BlockSpec(shape, lambda g: lead + (0,))

    specs = [cut(o.shape, o.dtype) for o in outs]
    dxbc, dgate, ddt, gconv, ggain, gheads = pl.pallas_call(
        hand_over,
        grid=(4,),
        in_specs=specs,
        out_specs=specs,
        out_shape=outs,
        name="hand_over",
    )(*results)
    return (dxbc[None], dgate[None], ddt[None], gconv, ggain[0], gheads)


def solution(mesh):
    token = P("dp", ("ctx", "head"), None)
    return jax.shard_map(
        body,
        mesh=mesh,
        in_specs=(
            token, token, token, P("dp", ("ctx", "head")),
            P(None, "head"), P("head"), P(None, "head"), token,
        ),
        out_specs=(token, token, token, P(None, "head"), P("head"), P(None, "head")),
        check_vma=False,
    )
```

```python
import jax
import jax.numpy as jnp
from jax import lax
from jax.experimental import pallas as pl
from jax.experimental.pallas import tpu as pltpu
from jax.sharding import PartitionSpec as P

HEADS = 128
GROUPS = 8
T = 128
GW = 1280
XW = 1024
CH = 10240
HP = 8192
LOG2E = 1.4426950408889634
EPS = 1e-05
NEG = -1e30
SPAN = 120.0
TINY = 1e-30
MESH = pl.DeviceIdType.MESH
VMEM = pltpu.VMEM

f32 = jnp.float32
bf16 = jnp.bfloat16
NN = ((1,), (0,))
NT = ((1,), (1,))
TN = ((0,), (0,))


def mm(a, b, dims=NN, precision=None):
    return lax.dot_general(a, b, (dims, ((), ())), preferred_element_type=f32, precision=precision)


def iota(shape, dim):
    return lax.broadcasted_iota(jnp.int32, shape, dim)


def sigmoid(v):
    return 0.5 * jnp.tanh(0.5 * v) + 0.5


def split(v):
    hi = v.astype(bf16)
    return hi, (v - hi.astype(f32)).astype(bf16)


def selector(g):
    return (iota((HEADS, XW), 0) == 16 * g + iota((HEADS, XW), 1) // 64).astype(f32).astype(bf16)


def twice(sel):
    return jnp.concatenate([sel, sel], axis=0)


def head_sums(v, sel):
    hi, lo = split(v)
    return mm(hi, sel, NT) + mm(lo, sel, NT)


def place():
    return lax.axis_index("ctx") * 4 + lax.axis_index("head")


def at(p):
    return {"ctx": p // 4, "head": lax.rem(p, 4)}


def off(index, width):
    return pl.multiple_of(index * width, width)


def greet(me):
    barrier = pltpu.get_barrier_semaphore()

    def one(k, carry):
        pl.semaphore_signal(
            barrier, inc=1, device_id=at(lax.rem(me + k, 64)), device_id_type=MESH
        )
        return carry

    lax.fori_loop(1, 64, one, 0)
    return barrier


def await_bytes(ref, sem):
    pltpu.make_async_copy(ref, ref, sem).wait()


def send_slot(me, p, src, dst, send_sem, recv_sem):
    @pl.when(p == me)
    def _():
        pltpu.make_async_copy(src, dst, recv_sem).start()

    @pl.when(p != me)
    def _():
        pltpu.make_async_remote_copy(
            src_ref=src, dst_ref=dst, send_sem=send_sem, recv_sem=recv_sem,
            device_id=at(p), device_id_type=MESH,
        ).start()


def turn(me, i):
    return lax.rem(me // 8 + i, 8)


def load_ext(g, ext, xbc_ref, halo):
    ext[8:136, :] = xbc_ref[:, pl.ds(off(g, GW), GW)].astype(f32)
    rows = pl.multiple_of(g * 32, 32)
    for k in range(3):
        for c in range(10):
            ext[5 + k : 6 + k, 128 * c : 128 * c + 128] = halo[pl.ds(rows + 10 * k + c, 1), :]


def windows(ext, prep_ref, lanes):
    return [
        ext[5:133, lanes] * prep_ref[6],
        ext[6:134, lanes] * prep_ref[7],
        ext[7:135, lanes] * prep_ref[8],
        ext[8:136, lanes],
    ]


def taps_of(w_refs, g, c):
    lanes = pl.ds(pl.multiple_of(lax.rem(g, 2) * GW + 128 * c, 128), 128)
    return [w_refs[0][g // 2, k : k + 1, lanes] for k in range(5)]


def conv(wins, taps):
    pre = taps[4] + taps[3] * wins[3]
    for k in range(3):
        pre = pre + taps[k] * wins[k]
    return pre


def params(w_refs, row):
    return jnp.concatenate([w_refs[2][q, row : row + 1, :32] for q in range(4)], axis=1)


def make_prep(halo, w_refs, dt_ref, seg_ref, prep_ref, pb_ref, segs):
    rate = jnp.exp(params(w_refs, 0))
    dtb = dt_ref[...].astype(f32) + params(w_refs, 1)
    step = jnp.maximum(dtb, 0.0) + jnp.log1p(jnp.exp(-jnp.abs(dtb)))
    decay = -step * rate
    rows, cols = iota((T, T), 0), iota((T, T), 1)
    low = (rows >= cols).astype(f32)
    run = mm(low, decay, NN, lax.Precision.HIGHEST) * LOG2E
    less = run - jnp.log(step) * LOG2E
    seg_row = jnp.broadcast_to(seg_ref[...].astype(f32) + 1.0, (T, T))
    seg_col = seg_row.T
    segs[8:136, :] = seg_col
    segs[5:8, :] = halo[256:259, :]
    prep_ref[0] = run
    prep_ref[1] = less
    prep_ref[2] = run.T
    prep_ref[3] = less.T
    same = seg_col == seg_row
    prep_ref[4] = jnp.where(same & (rows >= cols), 0.0, NEG)
    prep_ref[5] = jnp.where(same & (rows <= cols), 0.0, NEG)
    for k in range(3):
        prep_ref[6 + k] = (segs[5 + k : 133 + k, :] == seg_col).astype(f32)
    prep_ref[9] = step
    prep_ref[10] = decay
    linked = (seg_col == segs[7:8, :]).astype(f32)
    alpha = jnp.exp2(run) * linked
    omega = jnp.exp2(run[T - 1 :] - run) * (seg_col == seg_col[T - 1 :]).astype(f32) * step
    keep = alpha[T - 1 :]
    prep_ref[11] = sigmoid(dtb)
    for i, v in enumerate((alpha, omega)):
        hi, lo = split(v)
        pb_ref[i, :, :T] = hi
        pb_ref[i, :, T:] = lo
    both = jnp.where(rows == 0, params(w_refs, 2), keep)
    hi, lo = split(both)
    pb_ref[2, :, :T] = hi
    pb_ref[2, :, T:] = lo


def conv_group(g, xbc_ref, halo, w_refs, prep_ref, pb_ref, act_ref, slope, pay_ref, keep_own, ext):
    load_ext(g, ext, xbc_ref, halo)
    base = off(g, GW)
    for c in range(GW // 128):
        pre = conv(windows(ext, prep_ref, slice(128 * c, 128 * c + 128)), taps_of(w_refs, g, c))
        sg = sigmoid(pre)
        value = pre * sg
        act_ref[:, pl.ds(base + 128 * c, 128)] = value.astype(bf16)
        slope[:, pl.ds(base + 128 * c, 128)] = sg + value * (1.0 - sg)
    sel = selector(g)
    omega = mm(pb_ref[1], twice(sel))
    x_ref, b_ref, _ = parts_of(act_ref, g)
    weighted = (omega * x_ref[...].astype(f32)).astype(bf16)
    state = mm(b_ref[...], weighted, TN).astype(bf16)
    khi = mm(pb_ref[2, :16, :T], sel)
    klo = mm(pb_ref[2, :16, T:], sel)
    keep = khi[1:2] + klo[1:2]
    for i in range(8):
        lanes = slice(128 * i, 128 * i + 128)
        pay_ref[8 * g + i] = state[:, lanes]
        keep_own[8 * g + i] = keep[:, lanes]


def parts_of(act_ref, g):
    base = off(g, GW)
    return (
        act_ref.at[:, pl.ds(base, XW)],
        act_ref.at[:, pl.ds(base + XW, 128)],
        act_ref.at[:, pl.ds(base + XW + 128, 128)],
    )


def halves(v):
    left = iota(v.shape, 1) < 64
    zero = jnp.zeros_like(v)
    return jnp.concatenate([jnp.where(left, v, zero), jnp.where(left, zero, v)], axis=0)


def scan_up(keep_in, got_ref, start_ref, scale_ref):
    def one(j, state):
        top = jnp.maximum(jnp.max(jnp.abs(state), axis=0, keepdims=True) * 1.01, TINY)
        start_ref[j] = jnp.exp2(state * (SPAN / top)).astype(bf16)
        scale_ref[j] = top
        return keep_in[j] * state + got_ref[j].astype(f32)

    lax.fori_loop(0, 64, one, jnp.zeros((128, 128), f32))


def scan_down(keep_in, got_ref, end_ref):
    def one(i, grad):
        j = 63 - i
        end_ref[j] = grad.astype(bf16)
        return keep_in[j] * grad + got_ref[j].astype(f32)

    lax.fori_loop(0, 64, one, jnp.zeros((128, 128), f32))


def wide(slots_ref, g):
    return jnp.concatenate([slots_ref[8 * g + i] for i in range(8)], axis=1)


def inner_forward(g, act_ref, prep_ref, y_ref):
    x_ref, b_ref, c_ref = parts_of(act_ref, g)
    scores = mm(c_ref[...], b_ref[...], NT)
    run = pltpu.roll(prep_ref[0], lax.rem(128 - 16 * g, 128), 1)
    less = prep_ref[3, pl.ds(off(g, 16), 16), :]
    bias = prep_ref[4]
    for pair in range(8):
        mats = []
        for j in (2 * pair, 2 * pair + 1):
            el = jnp.exp2(run[:, j : j + 1] - less[j : j + 1, :] + bias)
            mats.append((el * scores).astype(bf16))
        lanes = slice(128 * pair, 128 * pair + 128)
        y_ref[:, pl.ds(off(g, XW) + 128 * pair, 128)] = mm(
            jnp.concatenate(mats, axis=1), halves(x_ref[:, lanes])
        )


def decode(code_ref, scale_ref, g):
    codes = wide(code_ref, g).astype(f32)
    scale = jnp.concatenate([scale_ref[8 * g + i] for i in range(8)], axis=1)
    return jnp.log2(codes) * (scale * (1.0 / SPAN))


def gate_group(
    g, act_ref, yi_ref, code_ref, scale_ref, start_ref, gate_ref, cot_ref, w_refs, pb_ref,
    dy_ref, dgate_ref, pay_ref, dcc_ref, rsum_ref, dgain_ref, dskip_ref,
    alpha_s, cs_s, ady_s, ady_lo, qhi_s, qlo_s,
):
    x_ref, _, c_ref = parts_of(act_ref, g)
    base = pl.ds(off(g, XW), XW)
    yi_ref, gate_ref, cot_ref = yi_ref.at[:, base], gate_ref.at[:, base], cot_ref.at[:, base]
    dy_ref, dgate_ref = dy_ref.at[:, base], dgate_ref.at[:, base]
    sel = selector(g)
    both = twice(sel)
    start, start_lo = split(decode(code_ref, scale_ref, g))
    for i in range(8):
        start_ref[8 * g + i] = start[:, 128 * i : 128 * i + 128]
    cs_s[...] = mm(c_ref[...], start) + mm(c_ref[...], start_lo)
    alpha_s[...] = mm(pb_ref[0], both)
    skip = mm(pb_ref[2, :16, :], both)[0:1]
    gain = w_refs[1][g // 2, :, pl.ds(off(lax.rem(g, 2), XW), XW)]
    dgain = jnp.zeros((16, XW), f32)
    dskip = jnp.zeros((16, XW), f32)
    for r in range(8):
        rows = slice(16 * r, 16 * r + 16)
        alpha = alpha_s[rows, :]
        yssm = yi_ref[rows, :] + alpha * cs_s[rows, :]
        x = x_ref[rows, :].astype(f32)
        ssm = (yssm + skip * x).astype(bf16).astype(f32)
        gate = gate_ref[rows, :].astype(f32)
        sg = sigmoid(gate)
        sl = gate * sg
        gated = ssm * sl
        rr = lax.rsqrt(jnp.sum(gated * gated, axis=1, keepdims=True) * (1.0 / XW) + EPS)
        norm = gated * rr
        cot = cot_ref[rows, :].astype(f32)
        dgain = dgain + cot * norm
        dn = cot * gain
        m2 = jnp.sum(dn * norm, axis=1, keepdims=True) * (1.0 / XW)
        dgated = rr * (dn - norm * m2)
        dy = (dgated * sl).astype(bf16)
        dy_ref[rows, :] = dy
        dgate_ref[rows, :] = (dgated * ssm * (sg + sl * (1.0 - sg))).astype(bf16)
        dyf = dy.astype(f32)
        hi, lo = split(alpha * dyf)
        ady_s[rows, :] = hi
        ady_lo[rows, :] = lo
        hi, lo = split(dyf * yssm)
        qhi_s[rows, :] = hi
        qlo_s[rows, :] = lo
        dskip = dskip + dyf * x
    ady = ady_s[...]
    dstart = (mm(c_ref[...], ady, TN) + mm(c_ref[...], ady_lo[...], TN)).astype(bf16)
    for i in range(8):
        pay_ref[8 * g + i] = dstart[:, 128 * i : 128 * i + 128]
    dcc_ref[g] = mm(ady, start, NT) + mm(ady, start_lo, NT) + mm(ady_lo[...], start, NT)
    rsum_ref[...] += mm(qhi_s[...], sel, NT) + mm(qlo_s[...], sel, NT)
    dskip_ref[...] += head_sums(dskip, sel)
    dgain_ref[g] = jnp.sum(dgain, axis=0, keepdims=True)


def send_turn(me, i, pairs):
    mine = me // 8
    group = lax.rem(mine + 8 - i, 8)
    for s in range(8):
        p = 8 * group + s
        for values, landing, send_sem, recv_sems in pairs:
            send_slot(me, p, values.at[p], landing.at[me], send_sem, recv_sems.at[mine])


def send_all(me, pairs):
    def one(i, carry):
        send_turn(me, i, pairs)
        return carry

    lax.fori_loop(0, 8, one, 0)


def inner_backward(g, act_ref, dy_ref, prep_ref, dcc_ref, dx_ref, db_ref, dc_ref):
    x_ref, b_ref, c_ref = parts_of(act_ref, g)
    scores = mm(b_ref[...], c_ref[...], NT)
    less = pltpu.roll(prep_ref[1], lax.rem(128 - 16 * g, 128), 1)
    run = prep_ref[2, pl.ds(off(g, 16), 16), :]
    bias = prep_ref[5]
    dscores = jnp.zeros((T, T), f32)
    for pair in range(8):
        out_lanes = pl.ds(off(g, XW) + 128 * pair, 128)
        dy2 = halves(dy_ref[:, out_lanes])
        dmat = mm(x_ref[:, 128 * pair : 128 * pair + 128], dy2, NT)
        mats = []
        for i in range(2):
            j = 2 * pair + i
            el = jnp.exp2(run[j : j + 1, :] - less[:, j : j + 1] + bias)
            mats.append((el * scores).astype(bf16))
            dscores = dscores + el * dmat[:, 128 * i : 128 * i + 128]
        dx_ref[:, out_lanes] = mm(jnp.concatenate(mats, axis=1), dy2)
    ds = dscores.astype(bf16)
    db_ref[g] = mm(ds, c_ref[...])
    dc_ref[g] = dcc_ref[g] + mm(ds, b_ref[...], TN)


def back_group(
    g, xbc_ref, halo, w_refs, act_ref, dy_ref, dxi, dbi, dci, start_ref, pay_ref, end,
    slope, prep_ref, pb_ref, dgain_ref, dxbc_ref, tail, rim, part, ext, dact, csum, ksum,
):
    x_ref, b_ref, _ = parts_of(act_ref, g)
    base = pl.ds(off(g, XW), XW)
    sel = selector(g)
    both = twice(sel)
    end_g = wide(end, g)
    rows16 = mm(pb_ref[2, :16, :], both)
    skip, keep = rows16[0:1], rows16[1:2]
    omega = mm(pb_ref[1], both)
    x = x_ref[...].astype(f32)
    dxs = dxi[:, base] + omega * mm(b_ref[...], end_g)
    csum[...] += head_sums(x * dxs, sel)
    dact[:, :XW] = (dxs + skip * dy_ref[:, base].astype(f32)).astype(bf16)
    dact[:, XW : XW + 128] = (dbi[g] + mm((omega * x).astype(bf16), end_g, NT)).astype(bf16)
    dact[:, XW + 128 :] = dci[g].astype(bf16)
    final = keep * wide(start_ref, g).astype(f32) + wide(pay_ref, g).astype(f32)
    ksum[...] += head_sums(jnp.sum((final * end_g.astype(f32)).reshape(16, 8, XW), axis=0), sel)

    load_ext(g, ext, xbc_ref, halo)
    rows = iota((T, 128), 0)
    for c in range(GW // 128):
        lanes = slice(128 * c, 128 * c + 128)
        wide_lanes = pl.ds(off(g, GW) + 128 * c, 128)
        taps = taps_of(w_refs, g, c)
        dpre = dact[:, lanes].astype(f32) * slope[:, wide_lanes]
        part[g, c, 3:4, :] = jnp.sum(dpre * ext[8:136, lanes], axis=0, keepdims=True)
        part[g, c, 4:5, :] = jnp.sum(dpre, axis=0, keepdims=True)
        if c < 8:
            part[g, c, 5:6, :] = dgain_ref[g, :, lanes]
        else:
            part[g, c, 5:6, :] = jnp.zeros((1, 128), f32)
        part[g, c, 6:8, :] = jnp.zeros((2, 128), f32)
        total = taps[3] * dpre
        over = jnp.zeros((8, 128), f32)
        for k in range(3):
            far = 3 - k
            used = dpre * prep_ref[6 + k]
            part[g, c, k : k + 1, :] = jnp.sum(
                used * ext[5 + k : 133 + k, lanes], axis=0, keepdims=True
            )
            moved = taps[k] * pltpu.roll(used, T - far, 0)
            inside = rows < T - far
            total = total + jnp.where(inside, moved, 0.0)
            over = over + jnp.where(inside, 0.0, moved)[T - 8 :]
        dxbc_ref[:, wide_lanes] = total.astype(bf16)
        tail[:, wide_lanes] = total[T - 16 :]
        for k in range(3):
            rim[pl.ds(pl.multiple_of(g * 32, 32) + 10 * k + c, 1), :] = over[5 + k : 6 + k]


def mixer(
    xbc_ref, own_conv, own_gain, own_head, dt_ref, seg_ref, gate_hbm, cot_hbm,
    dxbc_ref, dgate_hbm, ddt_ref, gconv_ref, ggain_ref, gheads_ref,
    gate_v, cot_v, dgate_v, act_ref, pay_ref, prep_ref, pb_ref, w_conv, w_gain, w_head, near, halo, got,
    start_own, codes, start_ref, yi_s, dy_ref, pay2, got2, dcc_ref, dbi, rsum_ref,
    dgain_ref, dskip_ref, end_own, end, tail, rim, rim_in, part, ext, segs, dact, csum,
    ksum, zbuf, hbuf, own, dhead, rbuf, total, fbuf, alpha_s, cs_s, ady_s, qhi_s, qlo_s,
    slope, ady_lo, keep_own, keep_in, scale_own, scales,
    keep_send, keep_recv, scale_send, gate_sem, cot_sem, near_sem, halo_sem, send_sem, recv_sem, start_send,
    grad_send, grad_recv, back_send, rim_send, rim_sem, z_send, z_sem, h_send, h_sem,
    r_send, r_sem, f_send, f_sem, near_send, w_sem, start_recv, back_recv, scale_recv,
):
    me = place()
    c, h, d = lax.axis_index("ctx"), lax.axis_index("head"), lax.axis_index("dp")
    barrier = greet(me)

    def greet_twin(k, carry):
        pl.semaphore_signal(
            barrier, inc=1, device_id={"dp": 1 - d, "ctx": k, "head": h}, device_id_type=MESH
        )
        return carry

    lax.fori_loop(0, 16, greet_twin, 0)
    gate_in = pltpu.make_async_copy(gate_hbm, gate_v, gate_sem)
    cot_in = pltpu.make_async_copy(cot_hbm, cot_v, cot_sem)
    gate_in.start()
    cot_in.start()

    for t in range(80):
        last = xbc_ref[112:128, 128 * t : 128 * t + 128].astype(f32)
        row = (t // 10) * 32 + t % 10
        for k in range(3):
            near[row + 10 * k : row + 10 * k + 1, :] = last[13 + k : 14 + k]
    for i in range(8):
        near[32 * i + 30 : 32 * i + 32, :] = jnp.zeros((2, 128), f32)
    ids = jnp.broadcast_to(seg_ref[...].astype(f32) + 1.0, (T, T)).T
    near[256:264, :] = jnp.zeros((8, 128), f32)
    near[256:259, :] = ids[T - 3 :]
    pl.semaphore_wait(barrier, 63 + 16)

    @pl.when(me < 63)
    def _():
        pltpu.make_async_remote_copy(
            src_ref=near, dst_ref=halo, send_sem=near_sem, recv_sem=halo_sem,
            device_id=at(lax.rem(me + 1, 64)), device_id_type=MESH,
        ).start()

    w_refs = (w_conv, w_gain, w_head)
    for n, own_w in ((2, own_head), (0, own_conv), (1, own_gain)):
        pltpu.make_async_copy(own_w, w_refs[n].at[h], w_sem.at[n]).start()
        for k in range(1, 4):
            pltpu.make_async_remote_copy(
                src_ref=own_w, dst_ref=w_refs[n].at[h], send_sem=near_send.at[n],
                recv_sem=w_sem.at[n], device_id=at(me - h + lax.rem(h + k, 4)),
                device_id_type=MESH,
            ).start()

    @pl.when(me == 0)
    def _():
        halo[...] = jnp.zeros_like(halo)

    for n in (0, 2):
        await_bytes(w_refs[n], w_sem.at[n])

    @pl.when(me > 0)
    def _():
        await_bytes(halo, halo_sem)

    make_prep(halo, w_refs, dt_ref, seg_ref, prep_ref, pb_ref, segs)

    def conv_turn(i, carry):
        g = turn(me, i)
        conv_group(g, xbc_ref, halo, w_refs, prep_ref, pb_ref, act_ref, slope, pay_ref, keep_own, ext)
        for s in range(8):
            p = 8 * g + s
            send_slot(me, p, keep_own.at[p], keep_in.at[me], keep_send, keep_recv)
            send_slot(me, p, pay_ref.at[p], got.at[me], send_sem, recv_sem)
        return carry

    lax.fori_loop(0, 8, conv_turn, 0)

    def forward(i, carry):
        inner_forward(i, act_ref, prep_ref, yi_s)
        return carry

    lax.fori_loop(0, 8, forward, 0)
    await_bytes(keep_in, keep_recv)
    await_bytes(got, recv_sem)
    scan_up(keep_in, got, start_own, scale_own)


    rsum_ref[...] = jnp.zeros_like(rsum_ref)
    dskip_ref[...] = jnp.zeros_like(dskip_ref)
    starts = (
        (scale_own, scales, scale_send, scale_recv),
        (start_own, codes, start_send, start_recv),
    )
    send_all(me, starts)
    gate_in.wait()
    cot_in.wait()
    await_bytes(w_gain, w_sem.at[1])

    def gate_turn(i, carry):
        g = turn(me, i)
        await_bytes(scales.at[pl.ds(8 * g, 8)], scale_recv.at[g])
        await_bytes(codes.at[pl.ds(8 * g, 8)], start_recv.at[g])
        gate_group(
            g, act_ref, yi_s, codes, scales, start_ref, gate_v, cot_v, w_refs, pb_ref,
            dy_ref, dgate_v, pay2, dcc_ref, rsum_ref, dgain_ref, dskip_ref,
            alpha_s, cs_s, ady_s, ady_lo, qhi_s, qlo_s,
        )
        for s in range(8):
            p = 8 * g + s
            send_slot(me, p, pay2.at[p], got2.at[me], grad_send, grad_recv)
        return carry

    lax.fori_loop(0, 8, gate_turn, 0)
    dgate_out = pltpu.make_async_copy(dgate_v, dgate_hbm, gate_sem)
    dgate_out.start()
    csum[...] = jnp.zeros_like(csum)
    ksum[...] = jnp.zeros_like(ksum)
    rim[...] = jnp.zeros_like(rim)

    def backward(i, carry):
        inner_backward(i, act_ref, dy_ref, prep_ref, dcc_ref, yi_s, dbi, dcc_ref)
        return carry

    lax.fori_loop(0, 8, backward, 0)
    await_bytes(got2, grad_recv)
    scan_down(keep_in, got2, end_own)
    ends = ((end_own, end, back_send, back_recv),)
    send_all(me, ends)

    def back_turn(i, carry):
        g = turn(me, i)
        await_bytes(end.at[pl.ds(8 * g, 8)], back_recv.at[g])
        back_group(
            g, xbc_ref, halo, w_refs, act_ref, dy_ref, yi_s, dbi, dcc_ref, start_ref, pay_ref, end,
            slope, prep_ref, pb_ref, dgain_ref, dxbc_ref, tail, rim, part, ext, dact, csum, ksum,
        )
        send_slot(
            me, me - h + g // 2, part.at[g], zbuf.at[h, lax.rem(g, 2)], z_send, z_sem
        )

        @pl.when(me > 0)
        def _():
            rows = pl.ds(pl.multiple_of(g * 32, 32), 32)
            pltpu.make_async_remote_copy(
                src_ref=rim.at[rows], dst_ref=rim_in.at[rows], send_sem=rim_send,
                recv_sem=rim_sem, device_id=at(lax.rem(me + 63, 64)), device_id_type=MESH,
            ).start()

        return carry

    lax.fori_loop(0, 8, back_turn, 0)

    high = (iota((T, T), 0) <= iota((T, T), 1)).astype(f32)
    step, decay = prep_ref[9], prep_ref[10]
    col = csum[...]
    dlog = mm(high, rsum_ref[...] - col, NN, lax.Precision.HIGHEST)
    dlog = dlog + jnp.sum(ksum[...], axis=0, keepdims=True)
    dstep = col / step - dlog * jnp.exp(params(w_refs, 0))
    ddt = dstep * prep_ref[11]
    ddt_ref[...] = ddt.astype(bf16)
    dhead[0:1, :] = jnp.sum(dlog * decay, axis=0, keepdims=True)
    dhead[1:2, :] = jnp.sum(ddt, axis=0, keepdims=True)
    dhead[2:3, :] = jnp.sum(dskip_ref[...], axis=0, keepdims=True)
    dhead[3:8, :] = jnp.zeros((5, HEADS), f32)
    pltpu.make_async_copy(dhead, hbuf.at[h], h_sem).start()
    for k in range(1, 4):
        pltpu.make_async_remote_copy(
            src_ref=dhead, dst_ref=hbuf.at[h], send_sem=h_send, recv_sem=h_sem,
            device_id=at(me - h + lax.rem(h + k, 4)), device_id_type=MESH,
        ).start()

    await_bytes(zbuf, z_sem)
    for q in range(2):
        own[10 * q : 10 * q + 10] = zbuf[0, q] + zbuf[1, q] + zbuf[2, q] + zbuf[3, q]
    await_bytes(hbuf, h_sem)
    own[20] = hbuf[0] + hbuf[1] + hbuf[2] + hbuf[3]
    rank = d * 16 + c

    def to_rank(r, src, dst, send_sem, recv_sem):
        @pl.when(r == rank)
        def _():
            pltpu.make_async_copy(src, dst, recv_sem).start()

        @pl.when(r != rank)
        def _():
            pltpu.make_async_remote_copy(
                src_ref=src, dst_ref=dst, send_sem=send_sem, recv_sem=recv_sem,
                device_id={"dp": r // 16, "ctx": lax.rem(r, 16), "head": h},
                device_id_type=MESH,
            ).start()

    def spread(r, carry):
        to_rank(r, own.at[r], rbuf.at[rank], r_send, r_sem)
        return carry

    lax.fori_loop(0, 21, spread, 0)

    @pl.when(rank < 21)
    def _():
        await_bytes(rbuf, r_sem)
        total[...] = jnp.sum(rbuf[...], axis=0)

        def share(k, carry):
            to_rank(lax.rem(rank + k, 32), total, fbuf.at[rank], f_send, f_sem)
            return carry

        lax.fori_loop(0, 32, share, 0)

    @pl.when(me < 63)
    def _():
        await_bytes(rim_in, rim_sem)
        for t in range(80):
            lanes = slice(128 * t, 128 * t + 128)
            row = (t // 10) * 32 + t % 10
            for k in range(3):
                tail[13 + k : 14 + k, lanes] += rim_in[row + 10 * k : row + 10 * k + 1, :]
            dxbc_ref[112:128, lanes] = tail[:, lanes].astype(bf16)

    await_bytes(fbuf, f_sem)
    for q in range(2):
        for t in range(10):
            lanes = slice(GW * q + 128 * t, GW * q + 128 * t + 128)
            gconv_ref[:, lanes] = fbuf[10 * q + t, :5, :]
            if t < 8:
                lanes = slice(XW * q + 128 * t, XW * q + 128 * t + 128)
                ggain_ref[:, lanes] = fbuf[10 * q + t, 5:6, :]
    gheads_ref[...] = pltpu.roll(fbuf[20], lax.rem(128 - 32 * h, 128), 1)[:3, :32]

    await_bytes(end.at[pl.ds(0, 63)], back_send)
    await_bytes(hbuf.at[pl.ds(0, 3)], h_send)
    await_bytes(part.at[pl.ds(0, 6)], z_send)

    @pl.when(me > 0)
    def _():
        await_bytes(rim, rim_send)

    @pl.when(rank < 21)
    def _():
        await_bytes(rbuf.at[pl.ds(0, 20)], r_send)
        await_bytes(rbuf.at[pl.ds(0, 31)], f_send)

    @pl.when(rank >= 21)
    def _():
        await_bytes(rbuf.at[pl.ds(0, 21)], r_send)

    for n in range(3):
        await_bytes(w_refs[n].at[pl.ds(0, 3)], near_send.at[n])

    @pl.when(me < 63)
    def _():
        await_bytes(near, near_sem)

    await_bytes(keep_in.at[pl.ds(0, 63)], keep_send)
    await_bytes(scales.at[pl.ds(0, 63)], scale_send)
    await_bytes(got.at[pl.ds(0, 63)], send_sem)
    await_bytes(codes.at[pl.ds(0, 63)], start_send)
    await_bytes(got2.at[pl.ds(0, 63)], grad_send)
    dgate_out.wait()


def hand_over(*refs):
    half = len(refs) // 2
    for src, dst in zip(refs[:half], refs[half:]):
        dst[...] = src[...]


def S(shape, dtype):
    return jax.ShapeDtypeStruct(shape, dtype)


def body(
    xbc_raw, gate_raw, dt_raw, segment_ids, conv_weight, norm_gain, head_params, out_cotangent
):
    xbc, gate, dt, cot = xbc_raw[0], gate_raw[0], dt_raw[0], out_cotangent[0]
    own_head = jnp.pad(head_params, ((0, 5), (0, 96)))
    dma = pltpu.SemaphoreType.DMA
    near = pl.BlockSpec(memory_space=VMEM)
    far = pl.BlockSpec(memory_space=pl.ANY)
    outs = (
        S((T, CH), bf16),
        S((T, HP), bf16),
        S((T, HEADS), bf16),
        S((5, 2560), f32),
        S((1, 2048), f32),
        S((3, 32), f32),
    )
    results = pl.pallas_call(
        mixer,
        in_specs=[near, near, near, near, near, near, far, far],
        out_specs=[near, far, near, near, near, near],
        out_shape=outs,
        scratch_shapes=(
            VMEM((T, HP), bf16),
            VMEM((T, HP), bf16),
            VMEM((T, HP), bf16),
            VMEM((T, CH), bf16),
            VMEM((64, 128, 128), bf16),
            VMEM((12, T, T), f32),
            VMEM((3, T, 2 * T), bf16),
            VMEM((4, 5, 2560), f32),
            VMEM((4, 1, 2048), f32),
            VMEM((4, 8, 128), f32),
            VMEM((264, 128), f32),
            VMEM((264, 128), f32),
            VMEM((64, 128, 128), bf16),
            VMEM((64, 128, 128), bf16),
            VMEM((64, 128, 128), bf16),
            VMEM((64, 128, 128), bf16),
            VMEM((T, HP), f32),
            VMEM((T, HP), bf16),
            VMEM((64, 128, 128), bf16),
            VMEM((64, 128, 128), bf16),
            VMEM((8, T, 128), f32),
            VMEM((8, T, 128), f32),
            VMEM((T, HEADS), f32),
            VMEM((8, 1, XW), f32),
            VMEM((16, HEADS), f32),
            VMEM((64, 128, 128), bf16),
            VMEM((64, 128, 128), bf16),
            VMEM((16, CH), f32),
            VMEM((256, 128), f32),
            VMEM((256, 128), f32),
            VMEM((8, 10, 8, 128), f32),
            VMEM((136, GW), f32),
            VMEM((136, 128), f32),
            VMEM((T, GW), bf16),
            VMEM((T, HEADS), f32),
            VMEM((8, HEADS), f32),
            VMEM((4, 2, 10, 8, 128), f32),
            VMEM((4, 8, 128), f32),
            VMEM((21, 8, 128), f32),
            VMEM((8, 128), f32),
            VMEM((32, 8, 128), f32),
            VMEM((8, 128), f32),
            VMEM((21, 8, 128), f32),
            VMEM((T, XW), f32),
            VMEM((T, XW), f32),
            VMEM((T, XW), bf16),
            VMEM((T, XW), bf16),
            VMEM((T, XW), bf16),
            VMEM((T, CH), f32),
            VMEM((T, XW), bf16),
            *([VMEM((64, 1, 128), f32)] * 4),
            *([dma] * 23),
            dma((3,)),
            dma((3,)),
            dma((8,)),
            dma((8,)),
            dma((8,)),
        ),
        compiler_params=pltpu.CompilerParams(
            vmem_limit_bytes=58 << 20, collective_id=1, has_side_effects=True
        ),
        cost_estimate=pl.CostEstimate(flops=4 << 30, bytes_accessed=16 << 20, transcendentals=0),
        name="mixer",
    )(xbc, conv_weight, norm_gain[None], own_head, dt, segment_ids, gate, cot)

    def cut(shape, dtype):
        lead = (0,) * (len(shape) - 1)
        if shape[-1] > 4096:
            return pl.BlockSpec((shape[0], shape[1] // 4), lambda g: (0, g))
        return pl.BlockSpec(shape, lambda g: lead + (0,))

    specs = [cut(o.shape, o.dtype) for o in outs]
    dxbc, dgate, ddt, gconv, ggain, gheads = pl.pallas_call(
        hand_over,
        grid=(4,),
        in_specs=specs,
        out_specs=specs,
        out_shape=outs,
        name="hand_over",
    )(*results)
    return (dxbc[None], dgate[None], ddt[None], gconv, ggain[0], gheads)


def solution(mesh):
    token = P("dp", ("ctx", "head"), None)
    return jax.shard_map(
        body,
        mesh=mesh,
        in_specs=(
            token, token, token, P("dp", ("ctx", "head")),
            P(None, "head"), P("head"), P(None, "head"), token,
        ),
        out_specs=(token, token, token, P(None, "head"), P("head"), P(None, "head")),
        check_vma=False,
    )
```
